256 devices in a mesh: vocab: 8 (over x, core), tok: 32 (over y, z).
Axes of the slice: x: 4, y: 4, z: 8, core: 2. Of those that a mesh axis runs over, the one named last changes fastest.
Arguments:
- student_hidden: bfloat16 [512, 4096], P('tok'), may hold values from -40 to 40
- teacher_hidden: bfloat16 [512, 4096], P('tok'), may hold values from -40 to 40
- student_weight: bfloat16 [4096, 131072], P(None, ('vocab', 'tok')), may hold values from -0.1 to 0.1
- teacher_weight: bfloat16 [4096, 131072], P(None, ('vocab', 'tok')), may hold values from -0.1 to 0.1
- source_rows: int32 [512], P('tok'), may hold values from 0 to 511, each once
Outputs:
- loss: float32 [], replicated
- hidden_grad: bfloat16 [512, 4096], P('tok', 'vocab')
The draws below stay inside these ranges and needn't reach their ends.
Inputs may be any that keep to these rules, and one draw needn't show every extreme that they name: source_rows is a permutation of the 512 teacher rows.
All inputs are finite; a program needn't handle non-finite values.
Results may differ from the reference program's by a relative error of at most 0.025.
Values may be sent and summed in bfloat16 or wider, within the bound.
No kernel may reach another device: no remote copies, remote signals or barrier semaphores. Data moves between devices by JAX's collectives and lax.ppermute only.
A program may use at most 64 MiB of HBM per device.

```python
import math
import jax
import jax.numpy as jnp

D = 4096
VOCAB = 131072
TOKENS = 512


def row_scales(subkey_rows, subkey_cols):
    row_index = jnp.arange(TOKENS, dtype=jnp.float32)
    row_ramp = 1.0 + 2.0 * row_index / max(TOKENS - 1, 1)
    row_factor = jnp.exp(jax.random.uniform(subkey_rows, (TOKENS,), minval=math.log(0.5), maxval=math.log(2.0)))
    col_scale = jnp.exp(jax.random.uniform(subkey_cols, (D,), minval=math.log(0.5), maxval=math.log(2.0)))
    return (0.7 * row_ramp * row_factor, col_scale)


def hidden_rows(key):
    subkeys = jax.random.split(key, 3)
    rows_scale, col_scale = row_scales(subkeys[1], subkeys[2])
    values = jax.random.normal(subkeys[0], (TOKENS, D))
    result = values * rows_scale[:, None] * col_scale[None, :]
    return jnp.clip(result, -40.0, 40.0).astype(jnp.bfloat16)


def weight_columns(key):
    subkeys = jax.random.split(key, 1)
    values = jnp.clip(jax.random.normal(subkeys[0], (D, VOCAB)), -6.0, 6.0) / math.sqrt(D)
    return values.astype(jnp.bfloat16)


def draw_student_hidden(key, part):
    key = jax.random.fold_in(key, 11)
    return hidden_rows(key)


def draw_teacher_hidden(key, part):
    key = jax.random.fold_in(key, 12)
    return hidden_rows(key)


def draw_student_weight(key, part):
    key = jax.random.fold_in(key, 21)
    return weight_columns(key)


def draw_teacher_weight(key, part):
    key = jax.random.fold_in(key, 22)
    return weight_columns(key)


def setup_inputs(seed: int = 0) -> dict:
    arg_keys = jax.random.split(jax.random.key(seed), 6)
    student_hidden = draw_student_hidden(jax.random.fold_in(arg_keys[5], 71), 0)
    teacher_hidden = draw_teacher_hidden(jax.random.fold_in(arg_keys[5], 71), 0)
    student_weight = draw_student_weight(jax.random.fold_in(arg_keys[5], 71), 0)
    teacher_weight = draw_teacher_weight(jax.random.fold_in(arg_keys[5], 71), 0)
    source_rows = jax.random.permutation(arg_keys[4], TOKENS).astype(jnp.int32)
    return {"student_hidden": student_hidden, "teacher_hidden": teacher_hidden, "student_weight": student_weight, "teacher_weight": teacher_weight, "source_rows": source_rows}


def reference(student_hidden, teacher_hidden, student_weight, teacher_weight, source_rows):
    teacher_rows = jnp.take(teacher_hidden, source_rows.astype(jnp.int32), axis=0)
    student_logits = jnp.dot(student_hidden, student_weight, preferred_element_type=jnp.float32)
    teacher_logits = jnp.dot(teacher_rows, teacher_weight, preferred_element_type=jnp.float32)
    student_top = jnp.max(student_logits, axis=1, keepdims=True)
    teacher_top = jnp.max(teacher_logits, axis=1, keepdims=True)
    student_norm = student_top + jnp.log(jnp.sum(jnp.exp(student_logits - student_top), axis=1, keepdims=True))
    teacher_norm = teacher_top + jnp.log(jnp.sum(jnp.exp(teacher_logits - teacher_top), axis=1, keepdims=True))
    log_student = student_logits - student_norm
    log_teacher = teacher_logits - teacher_norm
    student_prob = jnp.exp(log_student)
    divergence = jnp.sum(student_prob * (log_student - log_teacher), axis=1)
    logit_grad = (student_prob * (log_student - log_teacher - divergence[:, None])).astype(jnp.bfloat16)
    hidden_grad = jnp.dot(logit_grad, student_weight.T, preferred_element_type=jnp.float32).astype(jnp.bfloat16)
    loss = jnp.sum(divergence) / TOKENS
    return loss, hidden_grad
```

```python
import functools

import jax
import jax.numpy as jnp
from jax import lax
from jax.experimental import pallas as pl
from jax.experimental.pallas import tpu as pltpu
from jax.sharding import PartitionSpec as P

BF = jnp.bfloat16
F32 = jnp.float32
TOK, VOC = 32, 8
NY, NZ = 4, 8
N = 512
D = 4096
C = 512
SA = 512
TA = 256
TB = 1024
MIB = 1 << 20

Y_GROUPS = [[y * NZ + z for y in range(NY)] for z in range(NZ)]
Z_GROUPS = [[y * NZ + z for z in range(NZ)] for y in range(NY)]


def dot(a, b, dims=((1,), (0,))):
    return lax.dot_general(a, b, (dims, ((), ())), preferred_element_type=F32)


def params(limit):
    return pltpu.CompilerParams(vmem_limit_bytes=limit * MIB)


def pack_kernel(where_ref, a_ref, b_ref, out_ref):
    x = jnp.concatenate([a_ref[...], b_ref[...]], axis=1)
    out_ref[...] = jnp.broadcast_to(x[None], out_ref.shape)


def pack(where, a, a_width, b, b_width):
    rows = a.shape[0]
    width = a_width + b_width
    return pl.pallas_call(
        pack_kernel,
        grid_spec=pltpu.PrefetchScalarGridSpec(
            num_scalar_prefetch=1,
            grid=(1,),
            in_specs=[
                pl.BlockSpec((rows, a_width), lambda i, w: (0, w[0])),
                pl.BlockSpec((rows, b_width), lambda i, w: (0, w[1])),
            ],
            out_specs=pl.BlockSpec((TOK, rows, width), lambda i, w: (0, 0, 0)),
        ),
        out_shape=jax.ShapeDtypeStruct((TOK, rows, width), BF),
        compiler_params=params(16),
    )(where, a, b)


def first_kernel(core_ref, own_ref, other_ref, w_own_ref, w_other_ref, out_ref):
    out_ref[...] = dot(own_ref[...], w_own_ref[...]) + dot(other_ref[...], w_other_ref[...])


def first(core, own, other, teacher_weight):
    base = VOC * TA // TB
    return pl.pallas_call(
        first_kernel,
        grid_spec=pltpu.PrefetchScalarGridSpec(
            num_scalar_prefetch=1,
            grid=(1,),
            in_specs=[
                pl.BlockSpec((N, TB), lambda i, c: (0, 0)),
                pl.BlockSpec((N, TB), lambda i, c: (0, 0)),
                pl.BlockSpec((TB, C), lambda i, c: (base + c[0], 0)),
                pl.BlockSpec((TB, C), lambda i, c: (base + 1 - c[0], 0)),
            ],
            out_specs=pl.BlockSpec((N, C), lambda i, c: (0, 0)),
        ),
        out_shape=jax.ShapeDtypeStruct((N, C), F32),
        compiler_params=params(24),
        cost_estimate=pl.CostEstimate(
            flops=4 * N * TB * C, bytes_accessed=5 * MIB, transcendentals=0
        ),
    )(core, own, other, teacher_weight, teacher_weight)


def logits_kernel(rows_ref, sw_ref, tw_ref, part_ref, index_ref, s_ref, d_ref, stat_ref, t_ref):
    step = pl.program_id(0)
    rows = rows_ref[0]
    s_part = dot(rows[:, :SA], sw_ref[...])
    t_part = dot(rows[:, SA:], tw_ref[...])

    @pl.when(step == 0)
    def _():
        s_ref[...] = s_part
        t_ref[...] = part_ref[...] + t_part

    @pl.when(step > 0)
    def _():
        s_ref[...] += s_part
        t_ref[...] += t_part

    @pl.when(step == VOC - 1)
    def _():
        digits = index_ref[...].astype(F32)
        index = (digits[:, 0:1] * 32.0 + digits[:, 1:2]).astype(jnp.int32)
        column = lax.broadcasted_iota(jnp.int32, (N, N), 1)
        select = (index == column).astype(F32).astype(BF)
        t = t_ref[...]
        high = t.astype(BF)
        rest = t - high.astype(F32)
        middle = rest.astype(BF)
        low = (rest - middle.astype(F32)).astype(BF)
        t = dot(select, high) + dot(select, middle) + dot(select, low)
        s = s_ref[...]
        d = s - t
        d_ref[...] = d
        s_top = jnp.max(s, axis=1, keepdims=True)
        t_top = jnp.max(t, axis=1, keepdims=True)
        e = jnp.exp(s - s_top)
        s_sum = jnp.sum(e, axis=1, keepdims=True)
        mix = jnp.sum(e * d, axis=1, keepdims=True)
        t_sum = jnp.sum(jnp.exp(t - t_top), axis=1, keepdims=True)
        lane = lax.broadcasted_iota(jnp.int32, (N, 128), 1)
        table = jnp.zeros((N, 128), F32)
        for k, value in enumerate((s_top, s_sum, mix, t_top, t_sum)):
            table = jnp.where(lane == k, value, table)
        stat = jnp.transpose(table)[:8]
        stat_ref[...] = jnp.broadcast_to(stat[None], stat_ref.shape)


def logits(rows, student_weight, teacher_weight, part, packed):
    return pl.pallas_call(
        logits_kernel,
        grid=(VOC,),
        in_specs=[
            pl.BlockSpec((1, N, SA + TA), lambda i: (i, 0, 0)),
            pl.BlockSpec((SA, C), lambda i: (i, 0)),
            pl.BlockSpec((TA, C), lambda i: (i, 0)),
            pl.BlockSpec((N, C), lambda i: (0, 0)),
            pl.BlockSpec((N, 128), lambda i: (0, TB // 128)),
        ],
        out_specs=[
            pl.BlockSpec((N, C), lambda i: (0, 0)),
            pl.BlockSpec((N, C), lambda i: (0, 0)),
            pl.BlockSpec((VOC, 8, N), lambda i: (0, 0, 0)),
        ],
        out_shape=[
            jax.ShapeDtypeStruct((N, C), F32),
            jax.ShapeDtypeStruct((N, C), F32),
            jax.ShapeDtypeStruct((VOC, 8, N), F32),
        ],
        scratch_shapes=[pltpu.VMEM((N, C), F32)],
        compiler_params=params(32),
        cost_estimate=pl.CostEstimate(
            flops=2 * N * C * (D + VOC * TA), bytes_accessed=16 * MIB, transcendentals=2 * N * C
        ),
    )(rows, student_weight, teacher_weight, part, packed)


def merge(stats):
    s_top = jnp.max(stats[:, 0:1], axis=0)
    t_top = jnp.max(stats[:, 3:4], axis=0)
    s_scale = jnp.exp(stats[:, 0:1] - s_top[None])
    t_scale = jnp.exp(stats[:, 3:4] - t_top[None])
    s_sum = jnp.sum(stats[:, 1:2] * s_scale, axis=0)
    mix = jnp.sum(stats[:, 2:3] * s_scale, axis=0)
    t_sum = jnp.sum(stats[:, 4:5] * t_scale, axis=0)
    return s_top, s_sum, mix, t_top, t_sum


def merge_kernel(in_ref, out_ref):
    values = merge(in_ref[...])
    row = lax.broadcasted_iota(jnp.int32, (8, N), 0)
    stat = jnp.zeros((8, N), F32)
    for k, value in enumerate(values):
        stat = jnp.where(row == k, value, stat)
    out_ref[...] = jnp.broadcast_to(stat[None], out_ref.shape)


def merged(stats, copies):
    return pl.pallas_call(
        merge_kernel,
        out_shape=jax.ShapeDtypeStruct((copies, 8, N), F32),
        compiler_params=params(16),
    )(stats)


def exchange(x, axis, groups=None):
    n = x.shape[0]
    flat = x.reshape((n * x.shape[1],) + x.shape[2:])
    out = lax.all_to_all(flat, axis, 0, 0, axis_index_groups=groups, tiled=True)
    return out.reshape(x.shape)


def grad_kernel(stat_ref, s_ref, d_ref, sw_ref, out_ref, loss_ref, g_ref):
    @pl.when(pl.program_id(0) == 0)
    def _():
        s_top, s_sum, mix, t_top, t_sum = merge(stat_ref[...])
        mean = mix / s_sum
        divergence = mean - (s_top + jnp.log(s_sum)) + (t_top + jnp.log(t_sum))
        loss_ref[...] = jnp.sum(divergence, axis=1, keepdims=True) / N
        row = lax.broadcasted_iota(jnp.int32, (128, N), 0)
        table = jnp.zeros((128, N), F32)
        for k, value in enumerate((s_top, 1.0 / s_sum, mean)):
            table = jnp.where(row == k, value, table)
        table = jnp.transpose(table)
        prob = jnp.exp(s_ref[...] - table[:, 0:1]) * table[:, 1:2]
        g_ref[...] = (prob * (d_ref[...] - table[:, 2:3])).astype(BF)

    out_ref[0] = dot(g_ref[...], sw_ref[...], ((1,), (1,))).astype(BF)


def gradient(stats, s, d, student_weight):
    width = D // VOC
    return pl.pallas_call(
        grad_kernel,
        grid=(VOC,),
        in_specs=[
            pl.BlockSpec((NZ, 8, N), lambda i: (0, 0, 0)),
            pl.BlockSpec((N, C), lambda i: (0, 0)),
            pl.BlockSpec((N, C), lambda i: (0, 0)),
            pl.BlockSpec((width, C), lambda i: (i, 0)),
        ],
        out_specs=[
            pl.BlockSpec((1, N, width), lambda i: (i, 0, 0)),
            pl.BlockSpec((1, 1), lambda i: (0, 0)),
        ],
        out_shape=[
            jax.ShapeDtypeStruct((VOC, N, width), BF),
            jax.ShapeDtypeStruct((1, 1), F32),
        ],
        scratch_shapes=[pltpu.VMEM((N, C), BF)],
        compiler_params=params(32),
        cost_estimate=pl.CostEstimate(
            flops=2 * N * C * D, bytes_accessed=10 * MIB, transcendentals=N * C
        ),
    )(stats, s, d, student_weight)


def per_device(student_hidden, teacher_hidden, student_weight, teacher_weight, source_rows):
    v = lax.axis_index("vocab").astype(jnp.int32)
    core = v % 2
    slices = exchange(
        pack(jnp.stack([v, v]), student_hidden, SA, teacher_hidden, TA), "tok"
    ).reshape(N, SA + TA)
    rows = lax.all_gather(slices, "vocab", axis=0)
    digits = jnp.stack([source_rows // 32, source_rows % 32], axis=1).astype(BF)
    digits = jnp.pad(digits, ((0, 0), (0, 126)))
    packed = pack(
        jnp.stack([VOC * TA // TB + core, 0 * core]), teacher_hidden, TB, digits, 128
    )
    packed, _ = lax.optimization_barrier((packed, slices))
    packed = exchange(packed, "tok").reshape(N, TB + 128)
    other = lax.ppermute(packed, "vocab", [(k, k ^ 1) for k in range(VOC)])
    part = first(core[None], packed, other, teacher_weight)
    s, d, stats = logits(rows, student_weight, teacher_weight, part, packed)
    stats = merged(exchange(stats, "vocab"), NY)
    stats = merged(exchange(stats, "tok", Y_GROUPS), NZ)
    stats = exchange(stats, "tok", Z_GROUPS)
    partial, loss = gradient(stats, s, d, student_weight)
    partial = lax.psum_scatter(partial, "vocab", scatter_dimension=0)
    parts = exchange(partial.reshape(TOK, N // TOK, D // VOC), "tok")
    hidden_grad = jnp.sum(parts.astype(F32), axis=0).astype(BF)
    return loss[0, 0], hidden_grad


def solution(mesh):
    in_specs = (
        P("tok", None),
        P("tok", None),
        P(None, ("vocab", "tok")),
        P(None, ("vocab", "tok")),
        P("tok"),
    )
    out_specs = (P(), P("tok", "vocab"))
    return jax.shard_map(
        per_device, mesh=mesh, in_specs=in_specs, out_specs=out_specs, check_vma=False
    )
```

```python
import functools

import jax
import jax.numpy as jnp
from jax import lax
from jax.experimental import pallas as pl
from jax.experimental.pallas import tpu as pltpu
from jax.sharding import PartitionSpec as P

BF = jnp.bfloat16
F32 = jnp.float32
TOK, VOC = 32, 8
NX = 4
N = 512
D = 4096
C = 512
SA = 512
TA = 256
TB = 1024
MIB = 1 << 20

X_GROUPS = [[2 * x + core for x in range(NX)] for core in range(2)]


def dot(a, b, dims=((1,), (0,))):
    return lax.dot_general(a, b, (dims, ((), ())), preferred_element_type=F32)


PARAMS = pltpu.CompilerParams(vmem_limit_bytes=56 * MIB)


def pack_kernel(where_ref, a_ref, b_ref, out_ref):
    x = jnp.concatenate([a_ref[...], b_ref[...]], axis=1)
    out_ref[...] = jnp.broadcast_to(x[None], out_ref.shape)


def pack(where, a, a_width, b, b_width):
    rows = a.shape[0]
    width = a_width + b_width
    return pl.pallas_call(
        pack_kernel,
        grid_spec=pltpu.PrefetchScalarGridSpec(
            num_scalar_prefetch=1,
            grid=(1,),
            in_specs=[
                pl.BlockSpec((rows, a_width), lambda i, w: (0, w[0])),
                pl.BlockSpec((rows, b_width), lambda i, w: (0, w[1])),
            ],
            out_specs=pl.BlockSpec((TOK, rows, width), lambda i, w: (0, 0, 0)),
        ),
        out_shape=jax.ShapeDtypeStruct((TOK, rows, width), BF),
        compiler_params=PARAMS,
    )(where, a, b)


def pieces_kernel(where_ref, *refs):
    count = (len(refs) - 2) // 3
    s_ref, t_ref = refs[-2:]
    s = t = None
    for k in range(count):
        rows, sw, tw = refs[3 * k : 3 * k + 3]
        s_part = dot(rows[:, :SA], sw[...])
        t_part = dot(rows[:, SA:], tw[...])
        s = s_part if s is None else s + s_part
        t = t_part if t is None else t + t_part
    s_ref[...] = s
    t_ref[...] = t


def piece_specs(k):
    return [
        pl.BlockSpec((N, SA + TA), lambda i, w: (0, 0)),
        pl.BlockSpec((SA, C), lambda i, w: (w[k], 0)),
        pl.BlockSpec((TA, C), lambda i, w: (w[k], 0)),
    ]


def pieces(where, rows, student_weight, teacher_weight):
    count = len(rows)
    whole = pl.BlockSpec((N, C), lambda i, w: (0, 0))
    return pl.pallas_call(
        pieces_kernel,
        grid_spec=pltpu.PrefetchScalarGridSpec(
            num_scalar_prefetch=1,
            grid=(1,),
            in_specs=[spec for k in range(count) for spec in piece_specs(k)],
            out_specs=[whole, whole],
        ),
        out_shape=[jax.ShapeDtypeStruct((N, C), F32)] * 2,
        compiler_params=PARAMS,
        cost_estimate=pl.CostEstimate(
            flops=2 * N * C * (SA + TA) * count, bytes_accessed=2 * MIB * count, transcendentals=0
        ),
    )(where, *(x for r in rows for x in (r, student_weight, teacher_weight)))


def pack_stats(lse_s, mean, lse_t):
    half = N // 2
    row = lax.broadcasted_iota(jnp.int32, (8, half), 0)
    out = jnp.zeros((8, half), F32)
    for k, value in enumerate((lse_s, mean, lse_t)):
        out = jnp.where(row == k, value[:, :half], out)
        out = jnp.where(row == k + 4, value[:, half:], out)
    return out


def merge(stats):
    def rows(k):
        return jnp.concatenate([stats[:, k : k + 1], stats[:, k + 4 : k + 5]], axis=2)

    def lse(x):
        top = jnp.max(x, axis=0)
        return top + jnp.log(jnp.sum(jnp.exp(x - top[None]), axis=0))

    each_s, each_mean, each_t = rows(0), rows(1), rows(2)
    lse_s = lse(each_s)
    mean = jnp.sum(jnp.exp(each_s - lse_s[None]) * each_mean, axis=0)
    return lse_s, mean, lse(each_t)


def logits_kernel(
    where_ref, c_ref, d_ref, c2_ref, d2_ref, sw1_ref, tw1_ref, sw2_ref, tw2_ref,
    own_ref, other_ref, w_own_ref, w_other_ref, s0_ref, t0_ref, s_ref, diff_ref, stat_ref,
):
    half = N // 2

    def far(x_ref, y_ref, a, b):
        return jnp.concatenate([x_ref[:, a:b], y_ref[:, a:b]], axis=0)

    s = s0_ref[...] + (
        dot(far(c_ref, d_ref, 0, SA), sw1_ref[...]) + dot(far(c2_ref, d2_ref, 0, SA), sw2_ref[...])
    )
    t = t0_ref[...] + (
        dot(far(c_ref, d_ref, SA, SA + TA), tw1_ref[...])
        + dot(far(c2_ref, d2_ref, SA, SA + TA), tw2_ref[...])
        + dot(own_ref[:, :TB], w_own_ref[...])
        + dot(other_ref[:, :TB], w_other_ref[...])
    )
    digits = own_ref[:, TB:].astype(F32)
    index = (digits[:, 0:1] * 32.0 + digits[:, 1:2]).astype(jnp.int32)
    column = lax.broadcasted_iota(jnp.int32, (N, N), 1)
    select = (index == column).astype(F32).astype(BF)
    high = t.astype(BF)
    rest = t - high.astype(F32)
    middle = rest.astype(BF)
    low = (rest - middle.astype(F32)).astype(BF)
    t = dot(select, high) + dot(select, middle) + dot(select, low)
    diff = s - t
    s_ref[...] = s
    diff_ref[...] = diff
    s_top = jnp.max(s, axis=1, keepdims=True)
    t_top = jnp.max(t, axis=1, keepdims=True)
    e = jnp.exp(s - s_top)
    s_sum = jnp.sum(e, axis=1, keepdims=True)
    mix = jnp.sum(e * diff, axis=1, keepdims=True)
    t_sum = jnp.sum(jnp.exp(t - t_top), axis=1, keepdims=True)
    lane = lax.broadcasted_iota(jnp.int32, (N, 128), 1)
    table = jnp.zeros((N, 128), F32)
    for k, value in enumerate((s_top, s_sum, mix, t_top, t_sum)):
        table = jnp.where(lane == k, value, table)
    table = jnp.transpose(table)
    s_top, s_sum, mix, t_top, t_sum = (table[k : k + 1] for k in range(5))
    stat = pack_stats(s_top + jnp.log(s_sum), mix / s_sum, t_top + jnp.log(t_sum))
    stat_ref[...] = jnp.broadcast_to(stat[None], stat_ref.shape)


def logits(where, far, student_weight, teacher_weight, own, other, s0, t0):
    base = VOC * TA // TB
    half = N // 2
    whole = pl.BlockSpec((N, C), lambda i, w: (0, 0))
    piece = pl.BlockSpec((half, SA + TA), lambda i, w: (0, 0))
    packed = pl.BlockSpec((N, TB + 128), lambda i, w: (0, 0))
    return pl.pallas_call(
        logits_kernel,
        grid_spec=pltpu.PrefetchScalarGridSpec(
            num_scalar_prefetch=1,
            grid=(1,),
            in_specs=[piece] * 4
            + [
                pl.BlockSpec((SA, C), lambda i, w: (w[0], 0)),
                pl.BlockSpec((TA, C), lambda i, w: (w[0], 0)),
                pl.BlockSpec((SA, C), lambda i, w: (w[1], 0)),
                pl.BlockSpec((TA, C), lambda i, w: (w[1], 0)),
                packed,
                packed,
                pl.BlockSpec((TB, C), lambda i, w: (base + w[2], 0)),
                pl.BlockSpec((TB, C), lambda i, w: (base + 1 - w[2], 0)),
                whole,
                whole,
            ],
            out_specs=[
                whole,
                whole,
                pl.BlockSpec((VOC, 8, half), lambda i, w: (0, 0, 0)),
            ],
        ),
        out_shape=[
            jax.ShapeDtypeStruct((N, C), F32),
            jax.ShapeDtypeStruct((N, C), F32),
            jax.ShapeDtypeStruct((VOC, 8, half), F32),
        ],
        compiler_params=PARAMS,
        cost_estimate=pl.CostEstimate(
            flops=2 * N * C * (2 * (SA + TA) + 2 * TB + 3 * N),
            bytes_accessed=14 * MIB,
            transcendentals=2 * N * C,
        ),
    )(
        where, *far, student_weight, teacher_weight, student_weight, teacher_weight,
        own, other, teacher_weight, teacher_weight, s0, t0,
    )


def merge_kernel(in_ref, out_ref):
    out_ref[...] = jnp.broadcast_to(pack_stats(*merge(in_ref[...]))[None], out_ref.shape)


def merged(stats, copies):
    return pl.pallas_call(
        merge_kernel,
        out_shape=jax.ShapeDtypeStruct((copies,) + stats.shape[1:], F32),
        compiler_params=PARAMS,
    )(stats)


def exchange(x, axis, groups=None):
    n = x.shape[0]
    flat = x.reshape((n * x.shape[1],) + x.shape[2:])
    out = lax.all_to_all(flat, axis, 0, 0, axis_index_groups=groups, tiled=True)
    return out.reshape(x.shape)


def grad_first_kernel(core_ref, stat_ref, s_ref, d_ref, sw_ref, out_ref, g_ref, loss_ref):
    @pl.when(pl.program_id(0) == 0)
    def _():
        lse_s, mean, lse_t = merge(stat_ref[...])
        loss_ref[...] = jnp.sum(mean - lse_s + lse_t, axis=1, keepdims=True) / N
        row = lax.broadcasted_iota(jnp.int32, (128, N), 0)
        table = jnp.where(row == 0, lse_s, jnp.where(row == 1, mean, 0.0))
        table = jnp.transpose(table)
        prob = jnp.exp(s_ref[...] - table[:, 0:1])
        g_ref[...] = (prob * (d_ref[...] - table[:, 1:2])).astype(BF)

    out_ref[0] = dot(g_ref[...], sw_ref[...], ((1,), (1,))).astype(BF)


def grad_second_kernel(core_ref, g_ref, in_ref, sw_ref, out_ref):
    out_ref[0] = (dot(g_ref[...], sw_ref[...], ((1,), (1,))) + in_ref[0].astype(F32)).astype(BF)


WIDTH = D // VOC
GRAD_COST = pl.CostEstimate(flops=N * C * D, bytes_accessed=8 * MIB, transcendentals=N * C)


def grad_first(core, stats, s, d, student_weight):
    whole = pl.BlockSpec((N, C), lambda i, c: (0, 0))
    return pl.pallas_call(
        grad_first_kernel,
        grid_spec=pltpu.PrefetchScalarGridSpec(
            num_scalar_prefetch=1,
            grid=(NX,),
            in_specs=[
                pl.BlockSpec(stats.shape, lambda i, c: (0, 0, 0)),
                whole,
                whole,
                pl.BlockSpec((WIDTH, C), lambda i, c: (2 * i + 1 - c[0], 0)),
            ],
            out_specs=[
                pl.BlockSpec((1, N, WIDTH), lambda i, c: (i, 0, 0)),
                whole,
                pl.BlockSpec((1, 1), lambda i, c: (0, 0)),
            ],
        ),
        out_shape=[
            jax.ShapeDtypeStruct((NX, N, WIDTH), BF),
            jax.ShapeDtypeStruct((N, C), BF),
            jax.ShapeDtypeStruct((1, 1), F32),
        ],
        compiler_params=PARAMS,
        cost_estimate=GRAD_COST,
    )(core, stats, s, d, student_weight)


def grad_second(core, g, received, student_weight):
    return pl.pallas_call(
        grad_second_kernel,
        grid_spec=pltpu.PrefetchScalarGridSpec(
            num_scalar_prefetch=1,
            grid=(NX,),
            in_specs=[
                pl.BlockSpec((N, C), lambda i, c: (0, 0)),
                pl.BlockSpec((1, N, WIDTH), lambda i, c: (i, 0, 0)),
                pl.BlockSpec((WIDTH, C), lambda i, c: (2 * i + c[0], 0)),
            ],
            out_specs=pl.BlockSpec((1, N, WIDTH), lambda i, c: (i, 0, 0)),
        ),
        out_shape=jax.ShapeDtypeStruct((NX, N, WIDTH), BF),
        compiler_params=PARAMS,
        cost_estimate=GRAD_COST,
    )(core, g, received, student_weight)


def sum_kernel(in_ref, out_ref):
    out_ref[...] = jnp.sum(in_ref[...].astype(F32), axis=0).astype(BF)


def summed(x, blocks):
    n, rows, width = x.shape
    rows //= blocks
    return pl.pallas_call(
        sum_kernel,
        grid=(blocks,),
        in_specs=[pl.BlockSpec((n, rows, width), lambda i: (0, i, 0))],
        out_specs=pl.BlockSpec((rows, width), lambda i: (i, 0)),
        out_shape=jax.ShapeDtypeStruct((rows * blocks, width), BF),
        compiler_params=PARAMS,
    )(x)


def along_x(a, step):
    pairs = [(k, (k // 2 + step) % NX * 2 + k % 2) for k in range(VOC)]
    return lax.ppermute(a, "vocab", pairs)


def to_other_core(a):
    return lax.ppermute(a, "vocab", [(k, k ^ 1) for k in range(VOC)])


def per_device(student_hidden, teacher_hidden, student_weight, teacher_weight, source_rows):
    v = lax.axis_index("vocab").astype(jnp.int32)
    x, core = v // 2, v % 2

    def slice_of(step, other):
        return (x + step) % NX * 2 + (core + other) % 2

    own = exchange(pack(jnp.stack([v, v]), student_hidden, SA, teacher_hidden, TA), "tok")
    own = own.reshape(N, SA + TA)
    left, right = along_x(own, 1), along_x(own, -1)
    own2 = to_other_core(own)
    digits = jnp.stack([source_rows // 32, source_rows % 32], axis=1).astype(BF)
    digits = jnp.pad(digits, ((0, 0), (0, 126)))
    packed = pack(
        jnp.stack([VOC * TA // TB + core, 0 * core]), teacher_hidden, TB, digits, 128
    )
    packed, _ = lax.optimization_barrier((packed, own))
    packed = exchange(packed, "tok").reshape(N, TB + 128)
    packed2 = to_other_core(packed)
    half = N // 2
    far1, far2 = along_x(left[:half], 1), along_x(right[half:], -1)
    left2, right2 = to_other_core(left), to_other_core(right)
    far = (far1, far2, to_other_core(far1), to_other_core(far2))
    where = jnp.stack([slice_of(k, o) for k in (0, -1, 1) for o in (0, 1)])
    s0, t0 = pieces(
        where, (own, own2, left, left2, right, right2), student_weight, teacher_weight
    )
    where = jnp.stack([slice_of(2, 0), slice_of(2, 1), core])
    s, d, stats = logits(
        where, far, student_weight, teacher_weight, packed, packed2, s0, t0
    )
    stats = merged(exchange(stats, "vocab"), TOK)
    stats = exchange(stats, "tok")
    partial, g, loss = grad_first(core[None], stats, s, d, student_weight)
    partial = grad_second(core[None], g, to_other_core(partial), student_weight)
    partial = summed(exchange(partial, "vocab", X_GROUPS), 4)
    hidden_grad = summed(exchange(partial.reshape(TOK, N // TOK, WIDTH), "tok"), 1)
    return loss[0, 0], hidden_grad


def solution(mesh):
    in_specs = (
        P("tok", None),
        P("tok", None),
        P(None, ("vocab", "tok")),
        P(None, ("vocab", "tok")),
        P("tok"),
    )
    out_specs = (P(), P("tok", "vocab"))
    return jax.shard_map(
        per_device, mesh=mesh, in_specs=in_specs, out_specs=out_specs, check_vma=False
    )
```

```python
import functools

import jax
import jax.numpy as jnp
from jax import lax
from jax.experimental import pallas as pl
from jax.experimental.pallas import tpu as pltpu
from jax.sharding import PartitionSpec as P

BF = jnp.bfloat16
F32 = jnp.float32
TOK, VOC = 32, 8
NX, NY, NZ = 4, 4, 8
N = 512
D = 4096
C = 512
W = 512
ROWS = N // TOK
NEAR = N // NY
HALF = NX * W
MIB = 1 << 20
STEPS = (0, -1, 1, 2)

X_GROUPS = [[2 * x + core for x in range(NX)] for core in range(2)]
Z_GROUPS = [[y * NZ + z for z in range(NZ)] for y in range(NY)]


def dot(a, b, dims=((1,), (0,))):
    return lax.dot_general(a, b, (dims, ((), ())), preferred_element_type=F32)


PARAMS = pltpu.CompilerParams(vmem_limit_bytes=20 * MIB)
VM = pl.BlockSpec(memory_space=pltpu.VMEM)
SM = pl.BlockSpec(memory_space=pltpu.SMEM)
HBM = pl.BlockSpec(memory_space=pltpu.HBM)


def out(shape, dtype):
    return pltpu.VMEM(shape, dtype)


def in_hbm(x):
    return pltpu.with_memory_space_constraint(x, pltpu.HBM)


def cost(flops, mib=0):
    return pl.CostEstimate(flops=flops, bytes_accessed=mib * MIB, transcendentals=0)


def call(kernel, in_specs, outs, *args, scratch=(), flops=0):
    return pl.pallas_call(
        kernel,
        in_specs=in_specs,
        out_specs=[VM] * len(outs),
        out_shape=[out(*o) for o in outs],
        scratch_shapes=list(scratch),
        compiler_params=PARAMS,
        cost_estimate=cost(flops),
    )(*args)


def at_block(index, size):
    return pl.ds(pl.multiple_of(index * size, size), size)


def started(src, dst, sem):
    copy = pltpu.make_async_copy(src, dst, sem)
    copy.start()
    return copy


def pack_kernel(place_ref, source_ref, s_ref, t_ref, out_ref, s_buf, t_buf, sem):
    columns = at_block(place_ref[1] * NX + place_ref[0], W)
    copies = [
        started(s_ref.at[:, columns], s_buf, sem.at[0]),
        started(t_ref.at[:, columns], t_buf, sem.at[1]),
    ]
    row = lax.broadcasted_iota(jnp.int32, (ROWS, 128), 0)
    lane = lax.broadcasted_iota(jnp.int32, (ROWS, 128), 1)
    digits = jnp.zeros((ROWS, 128), jnp.int32)
    for r in range(ROWS):
        source = source_ref[r]
        value = jnp.where(lane == 0, source >> 5, jnp.where(lane == 1, source & 31, 0))
        digits = jnp.where(row == r, value, digits)
    digits = digits.astype(F32).astype(BF)
    out_ref[:, :, 2 * W :] = jnp.broadcast_to(digits[None], (NZ, ROWS, 128))
    for k, (copy, buf) in enumerate(zip(copies, (s_buf, t_buf))):
        copy.wait()
        out_ref[:, :, k * W : (k + 1) * W] = jnp.broadcast_to(buf[...][None], (NZ, ROWS, W))


def split_kernel(in_ref, s_ref, t_ref, digits_ref):
    s_ref[...] = in_ref[:, :W]
    t_ref[...] = in_ref[:, W : 2 * W]
    digits_ref[...] = in_ref[:, 2 * W :]


def join_kernel(place_ref, s0, s1, s2, s3, t0, t1, t2, t3, digits_ref, s_out, t_out):
    for step, ref in zip(STEPS, (s0, s1, s2, s3)):
        s_out[at_block((place_ref[2] + step) % NY, NEAR)] = ref[...]
    for k, ref in enumerate((t0, t1, t2, t3)):
        t_out[:, k * W : (k + 1) * W] = ref[...]
    t_out[:, HALF:] = digits_ref[...]


def hold_kernel(place_ref, sw_ref, tw_ref, sw2_ref, tw2_ref, sw_out, tw_out, sw2_out, tw2_out, sem):
    half = at_block(place_ref[1], HALF)
    copies = [
        started(sw_ref, sw_out, sem.at[0]),
        started(tw_ref.at[half], tw_out, sem.at[1]),
        started(sw2_ref.at[half], sw2_out, sem.at[2]),
        started(tw2_ref.at[half], tw2_out, sem.at[3]),
    ]
    for copy in copies:
        copy.wait()


def partial_logits(place_ref, sw_ref, tw_ref, s_refs, t_ref, out_ref, first):
    s0, s1, s2, s3, s4 = s_refs
    blocks = [s0[...], s1[...], s2[...], jnp.concatenate([s3[...], s4[...]], axis=0)]
    s_total = t_total = None
    for k, (step, block) in enumerate(zip(STEPS, blocks)):
        at = (place_ref[0] + step) % NX
        s_part = dot(block, sw_ref[at_block(first + at, W)])
        t_part = dot(t_ref[:, k * W : (k + 1) * W], tw_ref[at_block(at, W)])
        s_total = s_part if s_total is None else s_total + s_part
        t_total = t_part if t_total is None else t_total + t_part
    out_ref[0] = s_total
    out_ref[1] = t_total


def other_kernel(
    place_ref, sw_ref, tw_ref, s0, s1, s2, s3, s4, t0, t1, t2, t3, t4, out_ref, t_all
):
    for step, ref in zip(STEPS, (t0, t1, t2)):
        t_all[at_block((place_ref[2] + step) % NY, NEAR)] = ref[...]
    far = (place_ref[2] + STEPS[3]) % NY * 2
    for k, ref in enumerate((t3, t4)):
        t_all[at_block(far + k, NEAR // 2)] = ref[...]
    partial_logits(place_ref, sw_ref, tw_ref, (s0, s1, s2, s3, s4), t_all, out_ref, 0)


def own_kernel(place_ref, sw_ref, tw_ref, s0, s1, s2, s3, s4, t_all, out_ref):
    first = place_ref[1] * NX
    partial_logits(place_ref, sw_ref, tw_ref, (s0, s1, s2, s3, s4), t_all, out_ref, first)


def pack_stats(lse_s, mean, lse_t):
    half = N // 2
    row = lax.broadcasted_iota(jnp.int32, (8, half), 0)
    out = jnp.zeros((8, half), F32)
    for k, value in enumerate((lse_s, mean, lse_t)):
        out = jnp.where(row == k, value[:, :half], out)
        out = jnp.where(row == k + 4, value[:, half:], out)
    return out


def merge(stats):
    def rows(k):
        return jnp.concatenate([stats[:, k : k + 1], stats[:, k + 4 : k + 5]], axis=2)

    def lse(x):
        top = jnp.max(x, axis=0)
        return top + jnp.log(jnp.sum(jnp.exp(x - top[None]), axis=0))

    each_s, each_mean, each_t = rows(0), rows(1), rows(2)
    lse_s = lse(each_s)
    mean = jnp.sum(jnp.exp(each_s - lse_s[None]) * each_mean, axis=0)
    return lse_s, mean, lse(each_t)


def logits_kernel(own_ref, other_ref, digits_ref, s_ref, diff_ref, stat_ref):
    digits = digits_ref[:, HALF:].astype(F32)
    index = (digits[:, 0:1] * 32.0 + digits[:, 1:2]).astype(jnp.int32)
    column = lax.broadcasted_iota(jnp.int32, (N, N), 1)
    select = (index == column).astype(F32).astype(BF)
    t = own_ref[1] + other_ref[1]
    high = t.astype(BF)
    rest = t - high.astype(F32)
    middle = rest.astype(BF)
    low = (rest - middle.astype(F32)).astype(BF)
    t = dot(select, high) + dot(select, middle) + dot(select, low)
    s = own_ref[0] + other_ref[0]
    s_ref[...] = s
    diff = s - t
    diff_ref[...] = diff
    s_top = jnp.max(s, axis=1, keepdims=True)
    t_top = jnp.max(t, axis=1, keepdims=True)
    e = jnp.exp(s - s_top)
    s_sum = jnp.sum(e, axis=1, keepdims=True)
    mix = jnp.sum(e * diff, axis=1, keepdims=True)
    t_sum = jnp.sum(jnp.exp(t - t_top), axis=1, keepdims=True)
    lane = lax.broadcasted_iota(jnp.int32, (N, 128), 1)
    table = jnp.zeros((N, 128), F32)
    for k, value in enumerate((s_top, s_sum, mix, t_top, t_sum)):
        table = jnp.where(lane == k, value, table)
    table = jnp.transpose(table)
    s_top, s_sum, mix, t_top, t_sum = (table[k : k + 1] for k in range(5))
    stat = pack_stats(s_top + jnp.log(s_sum), mix / s_sum, t_top + jnp.log(t_sum))
    stat_ref[...] = jnp.broadcast_to(stat[None], stat_ref.shape)


def merge_kernel(in_ref, out_ref):
    out_ref[...] = jnp.broadcast_to(pack_stats(*merge(in_ref[...]))[None], out_ref.shape)


def exchange(x, axis, groups=None):
    n = x.shape[0]
    flat = x.reshape((n * x.shape[1],) + x.shape[2:])
    out = lax.all_to_all(flat, axis, 0, 0, axis_index_groups=groups, tiled=True)
    return out.reshape(x.shape)


def grad_first_kernel(place_ref, stat_ref, s_ref, d_ref, sw_ref, out_ref, g_ref, loss_ref):
    lse_s, mean, lse_t = merge(stat_ref[...])
    loss_ref[...] = jnp.sum(mean - lse_s + lse_t, axis=1, keepdims=True) / N
    row = lax.broadcasted_iota(jnp.int32, (128, N), 0)
    table = jnp.where(row == 0, lse_s, jnp.where(row == 1, mean, 0.0))
    table = jnp.transpose(table)
    prob = jnp.exp(s_ref[...] - table[:, 0:1])
    g = (prob * (d_ref[...] - table[:, 1:2])).astype(BF)
    g_ref[...] = g
    for x in range(NX):
        columns = sw_ref[at_block(2 * x + 1 - place_ref[1], W)]
        out_ref[x] = dot(g, columns, ((1,), (1,))).astype(BF)


def grad_second_kernel(place_ref, g_ref, in_ref, sw_ref, out_ref):
    for x in range(NX):
        columns = sw_ref[at_block(2 * x + place_ref[1], W)]
        part = dot(g_ref[...], columns, ((1,), (1,)))
        out_ref[x] = (part + in_ref[x].astype(F32)).astype(BF)


def sum_kernel(in_ref, out_ref):
    out_ref[...] = jnp.sum(in_ref[...].astype(F32), axis=0).astype(BF)


def summed(x):
    return call(sum_kernel, [VM], [(x.shape[1:], BF)], x)[0]


def along_x(a, step):
    pairs = [(k, (k // 2 + step) % NX * 2 + k % 2) for k in range(VOC)]
    return lax.ppermute(a, "vocab", pairs)


def along_y(a, step):
    pairs = [(k, (k // NZ + step) % NY * NZ + k % NZ) for k in range(TOK)]
    return lax.ppermute(a, "tok", pairs)


def to_other_core(a):
    return lax.ppermute(a, "vocab", [(k, k ^ 1) for k in range(VOC)])


def ring(a, along):
    return [a] + [along(a, -step) for step in STEPS[1:3]] + [along(a, 2)]


def per_device(student_hidden, teacher_hidden, student_weight, teacher_weight, source_rows):
    v = lax.axis_index("vocab").astype(jnp.int32)
    y = lax.axis_index("tok").astype(jnp.int32) // NZ
    place = jnp.stack([v // 2, v % 2, y])
    packed = call(
        pack_kernel,
        [SM, SM, HBM, HBM],
        [((NZ, ROWS, 2 * W + 128), BF)],
        place, source_rows, in_hbm(student_hidden), in_hbm(teacher_hidden),
        scratch=[pltpu.VMEM((ROWS, W), BF)] * 2 + [pltpu.SemaphoreType.DMA((2,))],
    )[0]
    sw2, tw2 = to_other_core(student_weight), to_other_core(teacher_weight)
    near = exchange(packed, "tok", Z_GROUPS).reshape(NEAR, 2 * W + 128)
    near, sw2, tw2 = lax.optimization_barrier((near, sw2, tw2))
    s_near, t_near, digits = call(
        split_kernel, [VM], [((NEAR, W), BF), ((NEAR, W), BF), ((NEAR, 128), BF)], near
    )
    s_near, t_near = ring(s_near, along_y), ring(t_near, along_x)
    s_near, t_near = lax.optimization_barrier((s_near, t_near))
    s_mine, t_mine = call(
        join_kernel,
        [SM] + [VM] * 9,
        [((N, W), BF), ((NEAR, HALF + 128), BF)],
        place, *s_near, *t_near, digits,
    )
    s_left, s_right = along_x(s_mine, 1), along_x(s_mine, -1)
    t_left, t_right = along_y(t_mine, 1), along_y(t_mine, -1)
    held = call(
        hold_kernel,
        [SM] + [HBM] * 4,
        [((D, C), BF)] + [((HALF, C), BF)] * 3,
        place, *(in_hbm(x) for x in (student_weight, teacher_weight, sw2, tw2)),
        scratch=[pltpu.SemaphoreType.DMA((4,))],
    )
    s_left, s_right, t_left, t_right, held = lax.optimization_barrier(
        (s_left, s_right, t_left, t_right, held)
    )
    sw, tw, sw2, tw2 = held
    s_rows = (
        s_mine, s_left, s_right,
        along_x(s_left[: N // 2], 1), along_x(s_right[N // 2 :], -1),
    )
    t_rows = (
        t_mine, t_left, t_right,
        along_y(t_left[: NEAR // 2], 1), along_y(t_right[NEAR // 2 :], -1),
    )
    s_rows, t_rows = lax.optimization_barrier((s_rows, t_rows))
    flops = 4 * N * HALF * C
    for_other, t_all = call(
        other_kernel,
        [SM] + [VM] * 12,
        [((2, N, C), F32), ((N, HALF + 128), BF)],
        place, sw2, tw2, *s_rows, *t_rows,
        flops=flops,
    )
    own = call(
        own_kernel,
        [SM] + [VM] * 8,
        [((2, N, C), F32)],
        place, sw, tw, *s_rows, t_all,
        flops=flops,
    )[0]
    other, own = lax.optimization_barrier((to_other_core(for_other), own))
    s, d, stats = call(
        logits_kernel,
        [VM] * 3,
        [((N, C), F32), ((N, C), F32), ((VOC, 8, N // 2), F32)],
        own, other, t_all,
        flops=6 * N * N * C,
    )
    stats = exchange(stats, "vocab")
    stats = call(merge_kernel, [VM], [((TOK, 8, N // 2), F32)], stats)[0]
    stats = exchange(stats, "tok")
    for_other, g, loss = call(
        grad_first_kernel,
        [SM] + [VM] * 4,
        [((NX, N, W), BF), ((N, C), BF), ((1, 1), F32)],
        place, stats, s, d, sw,
        flops=N * C * D,
    )
    partial = call(
        grad_second_kernel,
        [SM] + [VM] * 3,
        [((NX, N, W), BF)],
        place, g, to_other_core(for_other), sw,
        flops=N * C * D,
    )[0]
    partial = summed(exchange(partial, "vocab", X_GROUPS))
    hidden_grad = summed(exchange(partial.reshape(TOK, ROWS, W), "tok"))
    return loss[0, 0], hidden_grad


def solution(mesh):
    in_specs = (
        P("tok", None),
        P("tok", None),
        P(None, ("vocab", "tok")),
        P(None, ("vocab", "tok")),
        P("tok"),
    )
    out_specs = (P(), P("tok", "vocab"))
    return jax.shard_map(
        per_device, mesh=mesh, in_specs=in_specs, out_specs=out_specs, check_vma=False
    )
```

```python
import functools

import jax
import jax.numpy as jnp
from jax import lax
from jax.experimental import pallas as pl
from jax.experimental.pallas import tpu as pltpu
from jax.sharding import PartitionSpec as P

BF = jnp.bfloat16
F32 = jnp.float32
TOK, VOC = 32, 8
NX, NY, NZ = 4, 4, 8
N = 512
D = 4096
C = 512
W = 512
ROWS = N // TOK
NEAR = N // NY
HALF = NX * W
MIB = 1 << 20
STEPS = (0, -1, 1, 2)

X_GROUPS = [[2 * x + core for x in range(NX)] for core in range(2)]
Z_GROUPS = [[y * NZ + z for z in range(NZ)] for y in range(NY)]


def dot(a, b, dims=((1,), (0,))):
    return lax.dot_general(a, b, (dims, ((), ())), preferred_element_type=F32)


PARAMS = pltpu.CompilerParams(vmem_limit_bytes=20 * MIB)
VM = pl.BlockSpec(memory_space=pltpu.VMEM)
SM = pl.BlockSpec(memory_space=pltpu.SMEM)
HBM = pl.BlockSpec(memory_space=pltpu.HBM)


def out(shape, dtype):
    return pltpu.VMEM(shape, dtype)


def in_hbm(x):
    return pltpu.with_memory_space_constraint(x, pltpu.HBM)


def cost(flops, mib=0):
    return pl.CostEstimate(flops=flops, bytes_accessed=mib * MIB, transcendentals=0)


def call(kernel, in_specs, outs, *args, scratch=(), flops=0):
    return pl.pallas_call(
        kernel,
        in_specs=in_specs,
        out_specs=[VM] * len(outs),
        out_shape=[out(*o) for o in outs],
        scratch_shapes=list(scratch),
        compiler_params=PARAMS,
        cost_estimate=cost(flops),
    )(*args)


def at_block(index, size):
    return pl.ds(pl.multiple_of(index * size, size), size)


def started(src, dst, sem):
    copy = pltpu.make_async_copy(src, dst, sem)
    copy.start()
    return copy


def pack_kernel(place_ref, source_ref, s_ref, t_ref, out_ref, s_buf, t_buf, sem):
    columns = at_block(place_ref[1] * NX + place_ref[0], W)
    copies = [
        started(s_ref.at[:, columns], s_buf, sem.at[0]),
        started(t_ref.at[:, columns], t_buf, sem.at[1]),
    ]
    row = lax.broadcasted_iota(jnp.int32, (ROWS, 128), 0)
    lane = lax.broadcasted_iota(jnp.int32, (ROWS, 128), 1)
    digits = jnp.zeros((ROWS, 128), jnp.int32)
    for r in range(ROWS):
        source = source_ref[r]
        value = jnp.where(lane == 0, source >> 5, jnp.where(lane == 1, source & 31, 0))
        digits = jnp.where(row == r, value, digits)
    digits = digits.astype(F32).astype(BF)
    out_ref[:, :, 2 * W :] = jnp.broadcast_to(digits[None], (NZ, ROWS, 128))
    for k, (copy, buf) in enumerate(zip(copies, (s_buf, t_buf))):
        copy.wait()
        out_ref[:, :, k * W : (k + 1) * W] = jnp.broadcast_to(buf[...][None], (NZ, ROWS, W))


def split_kernel(in_ref, s_ref, t_ref, digits_ref):
    s_ref[...] = in_ref[:, :W]
    t_ref[...] = in_ref[:, W : 2 * W]
    digits_ref[...] = in_ref[:, 2 * W :]


def join_kernel(place_ref, s0, s1, s2, s3, t0, t1, t2, t3, digits_ref, s_out, t_out):
    for step, ref in zip(STEPS, (s0, s1, s2, s3)):
        s_out[at_block((place_ref[2] + step) % NY, NEAR)] = ref[...]
    for k, ref in enumerate((t0, t1, t2, t3)):
        t_out[:, k * W : (k + 1) * W] = ref[...]
    t_out[:, HALF:] = digits_ref[...]


def hold_kernel(place_ref, sw_ref, tw_ref, sw2_ref, tw2_ref, sw_out, tw_out, sw2_out, tw2_out, sem):
    half = at_block(place_ref[1], HALF)
    copies = [
        started(sw_ref, sw_out, sem.at[0]),
        started(tw_ref.at[half], tw_out, sem.at[1]),
        started(sw2_ref.at[half], sw2_out, sem.at[2]),
        started(tw2_ref.at[half], tw2_out, sem.at[3]),
    ]
    for copy in copies:
        copy.wait()


def partial_logits(place_ref, sw_ref, tw_ref, s_refs, t_ref, out_ref, first):
    s0, s1, s2, s3, s4 = s_refs
    blocks = [s0[...], s1[...], s2[...], jnp.concatenate([s3[...], s4[...]], axis=0)]
    s_total = t_total = None
    for k, (step, block) in enumerate(zip(STEPS, blocks)):
        at = (place_ref[0] + step) % NX
        s_part = dot(block, sw_ref[at_block(first + at, W)])
        t_part = dot(t_ref[:, k * W : (k + 1) * W], tw_ref[at_block(at, W)])
        s_total = s_part if s_total is None else s_total + s_part
        t_total = t_part if t_total is None else t_total + t_part
    out_ref[0] = s_total
    out_ref[1] = t_total


def other_kernel(
    place_ref, sw_ref, tw_ref, s0, s1, s2, s3, s4, t0, t1, t2, t3, t4, out_ref, t_all
):
    for step, ref in zip(STEPS, (t0, t1, t2)):
        t_all[at_block((place_ref[2] + step) % NY, NEAR)] = ref[...]
    far = (place_ref[2] + STEPS[3]) % NY * 2
    for k, ref in enumerate((t3, t4)):
        t_all[at_block(far + k, NEAR // 2)] = ref[...]
    partial_logits(place_ref, sw_ref, tw_ref, (s0, s1, s2, s3, s4), t_all, out_ref, 0)


def own_kernel(place_ref, sw_ref, tw_ref, s0, s1, s2, s3, s4, t_all, out_ref):
    first = place_ref[1] * NX
    partial_logits(place_ref, sw_ref, tw_ref, (s0, s1, s2, s3, s4), t_all, out_ref, first)


def pack_stats(lse_s, mean, lse_t):
    half = N // 2
    row = lax.broadcasted_iota(jnp.int32, (8, half), 0)
    out = jnp.zeros((8, half), F32)
    for k, value in enumerate((lse_s, mean, lse_t)):
        out = jnp.where(row == k, value[:, :half], out)
        out = jnp.where(row == k + 4, value[:, half:], out)
    return out


def merge(stats):
    def rows(k):
        return jnp.concatenate([stats[:, k : k + 1], stats[:, k + 4 : k + 5]], axis=2)

    def lse(x):
        top = jnp.max(x, axis=0)
        return top + jnp.log(jnp.sum(jnp.exp(x - top[None]), axis=0))

    each_s, each_mean, each_t = rows(0), rows(1), rows(2)
    lse_s = lse(each_s)
    mean = jnp.sum(jnp.exp(each_s - lse_s[None]) * each_mean, axis=0)
    return lse_s, mean, lse(each_t)


def logits_kernel(own_ref, other_ref, digits_ref, s_ref, diff_ref, stat_ref):
    digits = digits_ref[:, HALF:].astype(F32)
    index = (digits[:, 0:1] * 32.0 + digits[:, 1:2]).astype(jnp.int32)
    column = lax.broadcasted_iota(jnp.int32, (N, N), 1)
    select = (index == column).astype(F32).astype(BF)
    t = own_ref[1] + other_ref[1]
    high = t.astype(BF)
    rest = t - high.astype(F32)
    middle = rest.astype(BF)
    low = (rest - middle.astype(F32)).astype(BF)
    t = dot(select, high) + dot(select, middle) + dot(select, low)
    s = own_ref[0] + other_ref[0]
    s_ref[...] = s
    diff = s - t
    diff_ref[...] = diff
    s_top = jnp.max(s, axis=1, keepdims=True)
    t_top = jnp.max(t, axis=1, keepdims=True)
    e = jnp.exp(s - s_top)
    s_sum = jnp.sum(e, axis=1, keepdims=True)
    mix = jnp.sum(e * diff, axis=1, keepdims=True)
    t_sum = jnp.sum(jnp.exp(t - t_top), axis=1, keepdims=True)
    lane = lax.broadcasted_iota(jnp.int32, (N, 128), 1)
    table = jnp.zeros((N, 128), F32)
    for k, value in enumerate((s_top, s_sum, mix, t_top, t_sum)):
        table = jnp.where(lane == k, value, table)
    table = jnp.transpose(table)
    s_top, s_sum, mix, t_top, t_sum = (table[k : k + 1] for k in range(5))
    stat = pack_stats(s_top + jnp.log(s_sum), mix / s_sum, t_top + jnp.log(t_sum))
    stat_ref[...] = jnp.broadcast_to(stat[None], stat_ref.shape)


def merge_kernel(in_ref, out_ref):
    out_ref[...] = jnp.broadcast_to(pack_stats(*merge(in_ref[...]))[None], out_ref.shape)


def exchange(x, axis, groups=None):
    n = x.shape[0]
    flat = x.reshape((n * x.shape[1],) + x.shape[2:])
    out = lax.all_to_all(flat, axis, 0, 0, axis_index_groups=groups, tiled=True)
    return out.reshape(x.shape)


H = W // 2


def terms(place_ref, g, sw_ref, core, second):
    for step in STEPS:
        block = ((place_ref[0] + step) % NX * 2 + core) * 2 + second
        yield dot(g, sw_ref[at_block(block, H)], ((1,), (1,)))


def first_for_other_kernel(
    place_ref, stat_ref, s_ref, d_ref, sw_ref, out_ref, g_ref, turned_ref, loss_ref
):
    lse_s, mean, lse_t = merge(stat_ref[...])
    loss_ref[...] = jnp.sum(mean - lse_s + lse_t, axis=1, keepdims=True) / N
    row = lax.broadcasted_iota(jnp.int32, (128, N), 0)
    table = jnp.where(row == 0, lse_s, jnp.where(row == 1, mean, 0.0))
    table = jnp.transpose(table)
    prob = jnp.exp(s_ref[...] - table[:, 0:1])
    g = (prob * (d_ref[...] - table[:, 1:2])).astype(BF)
    g_ref[...] = g
    for k, part in enumerate(terms(place_ref, g, sw_ref, 1 - place_ref[1], 0)):
        out_ref[:, k * H : (k + 1) * H] = part.astype(BF)
    for k, step in enumerate(STEPS):
        turned_ref[k * NEAR : (k + 1) * NEAR] = g_ref[at_block((place_ref[2] + step) % NY, NEAR)]


def second_for_other_kernel(place_ref, g_ref, sw_ref, out_ref):
    for k, part in enumerate(terms(place_ref, g_ref[...], sw_ref, 1 - place_ref[1], 1)):
        out_ref[:, k * H : (k + 1) * H] = part.astype(BF)


def first_own_kernel(place_ref, g_ref, in_ref, sw_ref, *out_refs):
    for k, part in enumerate(terms(place_ref, g_ref[...], sw_ref, place_ref[1], 0)):
        received = in_ref[:, k * H : (k + 1) * H].astype(F32)
        out_refs[k][...] = (part + received).astype(BF)


def second_own_kernel(place_ref, g_ref, in_ref, sw_ref, *out_refs):
    for k, part in enumerate(terms(place_ref, g_ref[...], sw_ref, place_ref[1], 1)):
        columns = slice(k * H, (k + 1) * H)
        total = (part + in_ref[:, columns].astype(F32)).astype(BF)
        for j, ref in enumerate(out_refs):
            ref[:, columns] = total[j * NEAR : (j + 1) * NEAR]


def total_of(refs):
    total = refs[0][...].astype(F32)
    for ref in refs[1:]:
        total = total + ref[...].astype(F32)
    return total


def sum_first_kernel(place_ref, *refs):
    buf = refs[-1]
    buf[...] = total_of(refs[:4])
    for step, ref in zip(STEPS, refs[4:8]):
        ref[...] = buf[at_block((place_ref[2] + step) % NY, NEAR)].astype(BF)


def sum_second_kernel(*refs):
    total = total_of(refs[:4]).astype(BF)
    for k, ref in enumerate(refs[4:]):
        ref[...] = total[:, k * H : (k + 1) * H]


def sum_both_kernel(*refs):
    out_ref = refs[-1]
    out_ref[:, :H] = total_of(refs[:4]).astype(BF)
    out_ref[:, H:] = total_of(refs[4:8]).astype(BF)


def sum_kernel(in_ref, out_ref):
    out_ref[...] = jnp.sum(in_ref[...].astype(F32), axis=0).astype(BF)


def summed(x):
    return call(sum_kernel, [VM], [(x.shape[1:], BF)], x)[0]


def along_x(a, step):
    pairs = [(k, (k // 2 + step) % NX * 2 + k % 2) for k in range(VOC)]
    return lax.ppermute(a, "vocab", pairs)


def along_y(a, step):
    pairs = [(k, (k // NZ + step) % NY * NZ + k % NZ) for k in range(TOK)]
    return lax.ppermute(a, "tok", pairs)


def to_other_core(a):
    return lax.ppermute(a, "vocab", [(k, k ^ 1) for k in range(VOC)])


def ring(a, along):
    return [a] + [along(a, -step) for step in STEPS[1:3]] + [along(a, 2)]


def to_ring(blocks, along):
    return [along(a, step) if step else a for step, a in zip(STEPS, blocks)]


def per_device(student_hidden, teacher_hidden, student_weight, teacher_weight, source_rows):
    v = lax.axis_index("vocab").astype(jnp.int32)
    y = lax.axis_index("tok").astype(jnp.int32) // NZ
    place = jnp.stack([v // 2, v % 2, y])
    packed = call(
        pack_kernel,
        [SM, SM, HBM, HBM],
        [((NZ, ROWS, 2 * W + 128), BF)],
        place, source_rows, in_hbm(student_hidden), in_hbm(teacher_hidden),
        scratch=[pltpu.VMEM((ROWS, W), BF)] * 2 + [pltpu.SemaphoreType.DMA((2,))],
    )[0]
    sw2, tw2 = to_other_core(student_weight), to_other_core(teacher_weight)
    near = exchange(packed, "tok", Z_GROUPS).reshape(NEAR, 2 * W + 128)
    near, sw2, tw2 = lax.optimization_barrier((near, sw2, tw2))
    s_near, t_near, digits = call(
        split_kernel, [VM], [((NEAR, W), BF), ((NEAR, W), BF), ((NEAR, 128), BF)], near
    )
    s_near, t_near = ring(s_near, along_y), ring(t_near, along_x)
    s_near, t_near = lax.optimization_barrier((s_near, t_near))
    s_mine, t_mine = call(
        join_kernel,
        [SM] + [VM] * 9,
        [((N, W), BF), ((NEAR, HALF + 128), BF)],
        place, *s_near, *t_near, digits,
    )
    s_left, s_right = along_x(s_mine, 1), along_x(s_mine, -1)
    t_left, t_right = along_y(t_mine, 1), along_y(t_mine, -1)
    held = call(
        hold_kernel,
        [SM] + [HBM] * 4,
        [((D, C), BF)] + [((HALF, C), BF)] * 3,
        place, *(in_hbm(x) for x in (student_weight, teacher_weight, sw2, tw2)),
        scratch=[pltpu.SemaphoreType.DMA((4,))],
    )
    s_left, s_right, t_left, t_right, held = lax.optimization_barrier(
        (s_left, s_right, t_left, t_right, held)
    )
    sw, tw, sw2, tw2 = held
    s_rows = (
        s_mine, s_left, s_right,
        along_x(s_left[: N // 2], 1), along_x(s_right[N // 2 :], -1),
    )
    t_rows = (
        t_mine, t_left, t_right,
        along_y(t_left[: NEAR // 2], 1), along_y(t_right[NEAR // 2 :], -1),
    )
    s_rows, t_rows = lax.optimization_barrier((s_rows, t_rows))
    flops = 4 * N * HALF * C
    for_other, t_all = call(
        other_kernel,
        [SM] + [VM] * 12,
        [((2, N, C), F32), ((N, HALF + 128), BF)],
        place, sw2, tw2, *s_rows, *t_rows,
        flops=flops,
    )
    own = call(
        own_kernel,
        [SM] + [VM] * 8,
        [((2, N, C), F32)],
        place, sw, tw, *s_rows, t_all,
        flops=flops,
    )[0]
    other, own = lax.optimization_barrier((to_other_core(for_other), own))
    s, d, stats = call(
        logits_kernel,
        [VM] * 3,
        [((N, C), F32), ((N, C), F32), ((VOC, 8, N // 2), F32)],
        own, other, t_all,
        flops=6 * N * N * C,
    )
    stats = exchange(stats, "vocab")
    stats = call(merge_kernel, [VM], [((TOK, 8, N // 2), F32)], stats)[0]
    stats = exchange(stats, "tok")
    flops = N * C * D // 2
    half = ((N, NX * H), BF)
    first, g, turned, loss = call(
        first_for_other_kernel,
        [SM] + [VM] * 4,
        [half, ((N, C), BF), ((N, C), BF), ((1, 1), F32)],
        place, stats, s, d, sw,
        flops=flops,
    )
    second = call(
        second_for_other_kernel, [SM, VM, VM], [half], place, turned, sw, flops=flops
    )[0]
    first = call(
        first_own_kernel,
        [SM] + [VM] * 3,
        [((N, H), BF)] * 4,
        place, g, to_other_core(first), sw,
        flops=flops,
    )
    first = to_ring(first, along_x)
    second = call(
        second_own_kernel,
        [SM] + [VM] * 3,
        [((NEAR, NX * H), BF)] * 4,
        place, turned, to_other_core(second), sw,
        flops=flops,
    )
    second = to_ring(second, along_y)
    blocks = [((NEAR, H), BF)] * 4
    first = call(
        sum_first_kernel, [SM] + [VM] * 4, blocks, place, *first,
        scratch=[pltpu.VMEM((N, H), F32)],
    )
    first = to_ring(first, along_y)
    second = call(sum_second_kernel, [VM] * 4, blocks, *second)
    second = to_ring(second, along_x)
    partial = call(sum_both_kernel, [VM] * 8, [((NEAR, W), BF)], *first, *second)[0]
    hidden_grad = summed(exchange(partial.reshape(NZ, ROWS, W), "tok", Z_GROUPS))
    return loss[0, 0], hidden_grad


def solution(mesh):
    in_specs = (
        P("tok", None),
        P("tok", None),
        P(None, ("vocab", "tok")),
        P(None, ("vocab", "tok")),
        P("tok"),
    )
    out_specs = (P(), P("tok", "vocab"))
    return jax.shard_map(
        per_device, mesh=mesh, in_specs=in_specs, out_specs=out_specs, check_vma=False
    )
```

```python
import functools

import jax
import jax.numpy as jnp
from jax import lax
from jax.experimental import pallas as pl
from jax.experimental.pallas import tpu as pltpu
from jax.sharding import PartitionSpec as P

BF = jnp.bfloat16
F32 = jnp.float32
TOK, VOC = 32, 8
NX, NY, NZ = 4, 4, 8
N = 512
D = 4096
C = 512
W = 512
ROWS = N // TOK
NEAR = N // NY
HALF = NX * W
MIB = 1 << 20
STEPS = (0, -1, 1, 2)
Z_GROUPS = [[y * NZ + z for z in range(NZ)] for y in range(NY)]


def dot(a, b, dims=((1,), (0,))):
    return lax.dot_general(a, b, (dims, ((), ())), preferred_element_type=F32)


PARAMS = pltpu.CompilerParams(vmem_limit_bytes=20 * MIB)
VM = pl.BlockSpec(memory_space=pltpu.VMEM)
SM = pl.BlockSpec(memory_space=pltpu.SMEM)
HBM = pl.BlockSpec(memory_space=pltpu.HBM)


def out(shape, dtype):
    return pltpu.VMEM(shape, dtype)


def in_hbm(x):
    return pltpu.with_memory_space_constraint(x, pltpu.HBM)


def cost(flops, mib=0):
    return pl.CostEstimate(flops=flops, bytes_accessed=mib * MIB, transcendentals=0)


def call(kernel, in_specs, outs, *args, scratch=(), flops=0):
    return pl.pallas_call(
        kernel,
        in_specs=in_specs,
        out_specs=[VM] * len(outs),
        out_shape=[out(*o) for o in outs],
        scratch_shapes=list(scratch),
        compiler_params=PARAMS,
        cost_estimate=cost(flops),
    )(*args)


def at_block(index, size):
    return pl.ds(pl.multiple_of(index * size, size), size)


def started(src, dst, sem):
    copy = pltpu.make_async_copy(src, dst, sem)
    copy.start()
    return copy


def pack_kernel(source_ref, s_ref, t_ref, out_ref, s_buf, t_buf, sem):
    v = lax.axis_index("vocab")
    columns = at_block(v % 2 * NX + v // 2, W)
    copies = [
        started(s_ref.at[:, columns], s_buf, sem.at[0]),
        started(t_ref.at[:, columns], t_buf, sem.at[1]),
    ]
    row = lax.broadcasted_iota(jnp.int32, (ROWS, 128), 0)
    lane = lax.broadcasted_iota(jnp.int32, (ROWS, 128), 1)
    digits = jnp.zeros((ROWS, 128), jnp.int32)
    for r in range(ROWS):
        source = source_ref[r]
        value = jnp.where(lane == 0, source >> 5, jnp.where(lane == 1, source & 31, 0))
        digits = jnp.where(row == r, value, digits)
    digits = digits.astype(F32).astype(BF)
    out_ref[:, :, 2 * W :] = jnp.broadcast_to(digits[None], (NZ, ROWS, 128))
    for k, (copy, buf) in enumerate(zip(copies, (s_buf, t_buf))):
        copy.wait()
        out_ref[:, :, k * W : (k + 1) * W] = jnp.broadcast_to(buf[...][None], (NZ, ROWS, W))


def split_kernel(in_ref, s_ref, t_ref, digits_ref):
    s_ref[...] = in_ref[:, :W]
    t_ref[...] = in_ref[:, W : 2 * W]
    digits_ref[...] = in_ref[:, 2 * W :]


def join_student_kernel(place_ref, far_ref, own_ref, left_ref, right_ref, out_ref):
    for step, ref in zip(STEPS, (own_ref, left_ref, right_ref, far_ref)):
        out_ref[at_block((place_ref[2] + step) % NY, NEAR)] = ref[...]


def join_teacher_kernel(far_ref, own_ref, left_ref, right_ref, digits_ref, out_ref):
    for k, ref in enumerate((own_ref, left_ref, right_ref, far_ref)):
        out_ref[:, k * W : (k + 1) * W] = ref[...]
    out_ref[:, HALF:] = digits_ref[...]


def hold_kernel(place_ref, sw_ref, tw_ref, sw2_ref, tw2_ref, sw_out, tw_out, sw2_out, tw2_out, sem):
    half = at_block(place_ref[1], HALF)
    copies = [
        started(sw_ref, sw_out, sem.at[0]),
        started(tw_ref.at[half], tw_out, sem.at[1]),
        started(sw2_ref.at[half], sw2_out, sem.at[2]),
        started(tw2_ref.at[half], tw2_out, sem.at[3]),
    ]
    for copy in copies:
        copy.wait()


def near_kernel(own, place_ref, sw_ref, tw_ref, s0, s1, s2, t0, t1, t2, out_ref):
    x, y = place_ref[0], place_ref[2]
    first = place_ref[1] * NX if own else 0
    s_total = t_total = None
    for step, ref in zip(STEPS, (s0, s1, s2)):
        s_part = dot(ref[...], sw_ref[at_block(first + (x + step) % NX, W)])
        s_total = s_part if s_total is None else s_total + s_part
    for k, step in enumerate(STEPS):
        columns = slice(k * W, (k + 1) * W)
        rows = jnp.concatenate([ref[:, columns] for ref in (t0, t1, t2)], axis=0)
        t_part = dot(rows, tw_ref[at_block((x + step) % NX, W)])
        t_total = t_part if t_total is None else t_total + t_part
    out_ref[0] = s_total
    for k, step in enumerate(STEPS[:3]):
        out_ref[1, at_block((y + step) % NY, NEAR)] = t_total[k * NEAR : (k + 1) * NEAR]
    out_ref[1, at_block((y + 2) % NY, NEAR)] = jnp.zeros((NEAR, C), F32)


def far_terms(place_ref, sw_ref, tw_ref, s3, s4, t3, t4, first):
    x = place_ref[0]
    s_rows = jnp.concatenate([s3[...], s4[...]], axis=0)
    s_part = dot(s_rows, sw_ref[at_block(first + (x + 2) % NX, W)])
    t_total = None
    for k, step in enumerate(STEPS):
        columns = slice(k * W, (k + 1) * W)
        rows = jnp.concatenate([t3[:, columns], t4[:, columns]], axis=0)
        t_part = dot(rows, tw_ref[at_block((x + step) % NX, W)])
        t_total = t_part if t_total is None else t_total + t_part
    return s_part, t_total


def far_other_kernel(place_ref, sw_ref, tw_ref, s3, s4, t3, t4, near_ref, out_ref):
    s_part, t_part = far_terms(place_ref, sw_ref, tw_ref, s3, s4, t3, t4, 0)
    out_ref[0] = near_ref[0] + s_part
    out_ref[1] = near_ref[1]
    out_ref[1, at_block((place_ref[2] + 2) % NY, NEAR)] = t_part


def far_own_kernel(
    place_ref, sw_ref, tw_ref, s3, s4, t3, t4, t0, t1, t2, near_ref, out_ref, digits_ref
):
    y = place_ref[2]
    s_part, t_part = far_terms(
        place_ref, sw_ref, tw_ref, s3, s4, t3, t4, place_ref[1] * NX
    )
    far = at_block((y + 2) % NY, NEAR)
    out_ref[0] = near_ref[0] + s_part
    out_ref[1] = near_ref[1]
    out_ref[1, far] = t_part
    for step, ref in zip(STEPS, (t0, t1, t2)):
        digits_ref[at_block((y + step) % NY, NEAR)] = ref[:, HALF:]
    for k, ref in enumerate((t3, t4)):
        digits_ref[at_block((y + 2) % NY * 2 + k, NEAR // 2)] = ref[:, HALF:]


def pack_stats(lse_s, mean, lse_t):
    half = N // 2
    row = lax.broadcasted_iota(jnp.int32, (8, half), 0)
    out = jnp.zeros((8, half), F32)
    for k, value in enumerate((lse_s, mean, lse_t)):
        out = jnp.where(row == k, value[:, :half], out)
        out = jnp.where(row == k + 4, value[:, half:], out)
    return out


def merge(stats):
    def rows(k):
        return jnp.concatenate([stats[:, k : k + 1], stats[:, k + 4 : k + 5]], axis=2)

    def lse(x):
        top = jnp.max(x, axis=0)
        return top + jnp.log(jnp.sum(jnp.exp(x - top[None]), axis=0))

    each_s, each_mean, each_t = rows(0), rows(1), rows(2)
    lse_s = lse(each_s)
    mean = jnp.sum(jnp.exp(each_s - lse_s[None]) * each_mean, axis=0)
    return lse_s, mean, lse(each_t)


def logits_kernel(
    own_ref, other_ref, digits_ref, s_ref, diff_ref, stat_ref
):
    digits = digits_ref[...].astype(F32)
    index = (digits[:, 0:1] * 32.0 + digits[:, 1:2]).astype(jnp.int32)
    column = lax.broadcasted_iota(jnp.int32, (N, N), 1)
    select = (index == column).astype(F32).astype(BF)
    t = own_ref[1] + other_ref[1]
    high = t.astype(BF)
    rest = t - high.astype(F32)
    middle = rest.astype(BF)
    low = (rest - middle.astype(F32)).astype(BF)
    t = dot(select, high) + dot(select, middle) + dot(select, low)
    s = own_ref[0] + other_ref[0]
    s_ref[...] = s
    diff = s - t
    diff_ref[...] = diff
    s_top = jnp.max(s, axis=1, keepdims=True)
    t_top = jnp.max(t, axis=1, keepdims=True)
    e = jnp.exp(s - s_top)
    s_sum = jnp.sum(e, axis=1, keepdims=True)
    mix = jnp.sum(e * diff, axis=1, keepdims=True)
    t_sum = jnp.sum(jnp.exp(t - t_top), axis=1, keepdims=True)
    lane = lax.broadcasted_iota(jnp.int32, (N, 128), 1)
    table = jnp.zeros((N, 128), F32)
    for k, value in enumerate((s_top, s_sum, mix, t_top, t_sum)):
        table = jnp.where(lane == k, value, table)
    table = jnp.transpose(table)
    s_top, s_sum, mix, t_top, t_sum = (table[k : k + 1] for k in range(5))
    stat = pack_stats(s_top + jnp.log(s_sum), mix / s_sum, t_top + jnp.log(t_sum))
    stat_ref[...] = jnp.broadcast_to(stat[None], stat_ref.shape)


def merge_kernel(in_ref, out_ref):
    out_ref[...] = jnp.broadcast_to(pack_stats(*merge(in_ref[...]))[None], out_ref.shape)


def exchange(x, axis, groups=None):
    n = x.shape[0]
    flat = x.reshape((n * x.shape[1],) + x.shape[2:])
    out = lax.all_to_all(flat, axis, 0, 0, axis_index_groups=groups, tiled=True)
    return out.reshape(x.shape)


H = W // 2


def terms(place_ref, g, sw_ref, core, second):
    for step in STEPS:
        block = ((place_ref[0] + step) % NX * 2 + core) * 2 + second
        yield dot(g, sw_ref[at_block(block, H)], ((1,), (1,)))


def first_for_other_kernel(
    place_ref, stat_ref, s_ref, d_ref, sw_ref, out_ref, g_ref, turned_ref, loss_ref
):
    lse_s, mean, lse_t = merge(stat_ref[...])
    loss_ref[...] = jnp.sum(mean - lse_s + lse_t, axis=1, keepdims=True) / N
    row = lax.broadcasted_iota(jnp.int32, (128, N), 0)
    table = jnp.where(row == 0, lse_s, jnp.where(row == 1, mean, 0.0))
    table = jnp.transpose(table)
    prob = jnp.exp(s_ref[...] - table[:, 0:1])
    g = (prob * (d_ref[...] - table[:, 1:2])).astype(BF)
    g_ref[...] = g
    for k, part in enumerate(terms(place_ref, g, sw_ref, 1 - place_ref[1], 0)):
        out_ref[:, k * H : (k + 1) * H] = part.astype(BF)
    for k, step in enumerate(STEPS):
        turned_ref[k * NEAR : (k + 1) * NEAR] = g_ref[at_block((place_ref[2] + step) % NY, NEAR)]


def second_for_other_kernel(place_ref, g_ref, sw_ref, out_ref):
    for k, part in enumerate(terms(place_ref, g_ref[...], sw_ref, 1 - place_ref[1], 1)):
        out_ref[:, k * H : (k + 1) * H] = part.astype(BF)


def own_terms_kernel(second, place_ref, g_ref, sw_ref, out_ref):
    for k, part in enumerate(terms(place_ref, g_ref[...], sw_ref, place_ref[1], second)):
        out_ref[:, k * H : (k + 1) * H] = part


def first_add_kernel(own_ref, in_ref, *out_refs):
    for k, ref in enumerate(out_refs):
        columns = slice(k * H, (k + 1) * H)
        ref[...] = (own_ref[:, columns] + in_ref[:, columns].astype(F32)).astype(BF)


def second_add_kernel(own_ref, in_ref, *out_refs):
    for k, ref in enumerate(out_refs):
        rows = slice(k * NEAR, (k + 1) * NEAR)
        ref[...] = (own_ref[rows] + in_ref[rows].astype(F32)).astype(BF)


def total_of(refs):
    total = refs[0][...].astype(F32)
    for ref in refs[1:]:
        total = total + ref[...].astype(F32)
    return total


def sum_first_kernel(place_ref, *refs):
    buf = refs[-1]
    buf[...] = total_of(refs[:4])
    for step, ref in zip(STEPS, refs[4:8]):
        ref[...] = buf[at_block((place_ref[2] + step) % NY, NEAR)].astype(BF)


def sum_second_kernel(*refs):
    total = total_of(refs[:4]).astype(BF)
    for k, ref in enumerate(refs[4:]):
        ref[...] = total[:, k * H : (k + 1) * H]


def sum_both_kernel(*refs):
    out_ref = refs[-1]
    out_ref[:, :H] = total_of(refs[:4]).astype(BF)
    out_ref[:, H:] = total_of(refs[4:8]).astype(BF)


def sum_kernel(in_ref, out_ref):
    out_ref[...] = jnp.sum(in_ref[...].astype(F32), axis=0).astype(BF)


def summed(x):
    return call(sum_kernel, [VM], [(x.shape[1:], BF)], x)[0]


def along_x(a, step):
    pairs = [(k, (k // 2 + step) % NX * 2 + k % 2) for k in range(VOC)]
    return lax.ppermute(a, "vocab", pairs)


def along_y(a, step):
    pairs = [(k, (k // NZ + step) % NY * NZ + k % NZ) for k in range(TOK)]
    return lax.ppermute(a, "tok", pairs)


def to_other_core(a):
    return lax.ppermute(a, "vocab", [(k, k ^ 1) for k in range(VOC)])


def ring(a, along):
    return along(a, 2), a, along(a, 1), along(a, -1)


def to_ring(blocks, along):
    own, left, right, far = blocks
    return along(far, 2), along(left, -1), along(right, 1), own


def per_device(student_hidden, teacher_hidden, student_weight, teacher_weight, source_rows):
    v = lax.axis_index("vocab").astype(jnp.int32)
    y = lax.axis_index("tok").astype(jnp.int32) // NZ
    place = jnp.stack([v // 2, v % 2, y])
    packed = call(
        pack_kernel,
        [SM, HBM, HBM],
        [((NZ, ROWS, 2 * W + 128), BF)],
        source_rows, in_hbm(student_hidden), in_hbm(teacher_hidden),
        scratch=[pltpu.VMEM((ROWS, W), BF)] * 2 + [pltpu.SemaphoreType.DMA((2,))],
    )[0]
    sw2, tw2 = to_other_core(student_weight), to_other_core(teacher_weight)
    near = exchange(packed, "tok", Z_GROUPS).reshape(NEAR, 2 * W + 128)
    near, sw2, tw2 = lax.optimization_barrier((near, sw2, tw2))
    s_near, t_near, digits = call(
        split_kernel, [VM], [((NEAR, W), BF), ((NEAR, W), BF), ((NEAR, 128), BF)], near
    )
    s_mine = call(
        join_student_kernel, [SM] + [VM] * 4, [((N, W), BF)], place, *ring(s_near, along_y)
    )[0]
    t_mine = call(
        join_teacher_kernel,
        [VM] * 5,
        [((NEAR, HALF + 128), BF)],
        *ring(t_near, along_x), digits,
    )[0]
    s_left, s_right = along_x(s_mine, 1), along_x(s_mine, -1)
    t_left, t_right = along_y(t_mine, 1), along_y(t_mine, -1)
    held = call(
        hold_kernel,
        [SM] + [HBM] * 4,
        [((D, C), BF)] + [((HALF, C), BF)] * 3,
        place, *(in_hbm(x) for x in (student_weight, teacher_weight, sw2, tw2)),
        scratch=[pltpu.SemaphoreType.DMA((4,))],
    )
    t_left, t_right, held = lax.optimization_barrier((t_left, t_right, held))
    sw, tw, sw2, tw2 = held
    s_near, t_near = (s_mine, s_left, s_right), (t_mine, t_left, t_right)
    far = (
        along_x(s_left[: N // 2], 1), along_x(s_right[N // 2 :], -1),
        along_y(t_left[: NEAR // 2], 1), along_y(t_right[NEAR // 2 :], -1),
    )
    flops = 3 * N * HALF * C
    part = [((2, N, C), F32)]

    def near(mine, *args):
        kernel = functools.partial(near_kernel, mine)
        return call(kernel, [SM] + [VM] * 8, part, place, *args, flops=flops)[0]

    for_other = near(False, sw2, tw2, *s_near, *t_near)
    own = near(True, sw, tw, *s_near, *t_near)
    far, for_other, own = lax.optimization_barrier((far, for_other, own))
    flops = N * HALF * C
    for_other = call(
        far_other_kernel, [SM] + [VM] * 7, part, place, sw2, tw2, *far, for_other, flops=flops
    )[0]
    own, digits = call(
        far_own_kernel,
        [SM] + [VM] * 10,
        part + [((N, 128), BF)],
        place, sw, tw, *far, *t_near, own,
        flops=flops,
    )
    other, own = lax.optimization_barrier((to_other_core(for_other), own))
    s, d, stats = call(
        logits_kernel,
        [VM] * 3,
        [((N, C), F32), ((N, C), F32), ((VOC, 8, N // 2), F32)],
        own, other, digits,
        flops=6 * N * N * C,
    )
    stats = exchange(stats, "vocab")
    stats = call(merge_kernel, [VM], [((TOK, 8, N // 2), F32)], stats)[0]
    stats = exchange(stats, "tok")
    flops = N * C * D // 2
    half = ((N, NX * H), BF)
    first, g, turned, loss = call(
        first_for_other_kernel,
        [SM] + [VM] * 4,
        [half, ((N, C), BF), ((N, C), BF), ((1, 1), F32)],
        place, stats, s, d, sw,
        flops=flops,
    )
    second = call(
        second_for_other_kernel, [SM, VM, VM], [half], place, turned, sw, flops=flops
    )[0]
    first, second = to_other_core(first), to_other_core(second)

    def own_terms(number, rows):
        kernel = functools.partial(own_terms_kernel, number)
        return call(
            kernel, [SM, VM, VM], [((N, NX * H), F32)], place, rows, sw, flops=flops
        )[0]

    first, mine = lax.optimization_barrier((first, own_terms(0, g)))
    first = call(first_add_kernel, [VM] * 2, [((N, H), BF)] * 4, mine, first)
    first = to_ring(first, along_x)
    second, mine = lax.optimization_barrier((second, own_terms(1, turned)))
    second = call(second_add_kernel, [VM] * 2, [((NEAR, NX * H), BF)] * 4, mine, second)
    second = to_ring(second, along_y)
    blocks = [((NEAR, H), BF)] * 4
    first = call(
        sum_first_kernel, [SM] + [VM] * 4, blocks, place, *first,
        scratch=[pltpu.VMEM((N, H), F32)],
    )
    first = to_ring(first, along_y)
    second = call(sum_second_kernel, [VM] * 4, blocks, *second)
    second = to_ring(second, along_x)
    partial = call(sum_both_kernel, [VM] * 8, [((NEAR, W), BF)], *first, *second)[0]
    hidden_grad = summed(exchange(partial.reshape(NZ, ROWS, W), "tok", Z_GROUPS))
    return loss[0, 0], hidden_grad


def solution(mesh):
    in_specs = (
        P("tok", None),
        P("tok", None),
        P(None, ("vocab", "tok")),
        P(None, ("vocab", "tok")),
        P("tok"),
    )
    out_specs = (P(), P("tok", "vocab"))
    return jax.shard_map(
        per_device, mesh=mesh, in_specs=in_specs, out_specs=out_specs, check_vma=False
    )
```

```python
import functools

import jax
import jax.numpy as jnp
from jax import lax
from jax.experimental import pallas as pl
from jax.experimental.pallas import tpu as pltpu
from jax.sharding import PartitionSpec as P

BF = jnp.bfloat16
F32 = jnp.float32
TOK, VOC = 32, 8
NX, NY, NZ = 4, 4, 8
N = 512
D = 4096
C = 512
W = 512
ROWS = N // TOK
NEAR = N // NY
HALF = NX * W
MIB = 1 << 20
STEPS = (0, -1, 1, 2)
Z_GROUPS = [[y * NZ + z for z in range(NZ)] for y in range(NY)]


def dot(a, b, dims=((1,), (0,))):
    return lax.dot_general(a, b, (dims, ((), ())), preferred_element_type=F32)


PARAMS = pltpu.CompilerParams(vmem_limit_bytes=20 * MIB)
VM = pl.BlockSpec(memory_space=pltpu.VMEM)
SM = pl.BlockSpec(memory_space=pltpu.SMEM)
HBM = pl.BlockSpec(memory_space=pltpu.HBM)


def out(shape, dtype):
    return pltpu.VMEM(shape, dtype)


def in_hbm(x):
    return pltpu.with_memory_space_constraint(x, pltpu.HBM)


def cost(flops, mib=0):
    return pl.CostEstimate(flops=flops, bytes_accessed=mib * MIB, transcendentals=0)


def call(kernel, in_specs, outs, *args, scratch=(), flops=0):
    return pl.pallas_call(
        kernel,
        in_specs=in_specs,
        out_specs=[VM] * len(outs),
        out_shape=[out(*o) for o in outs],
        scratch_shapes=list(scratch),
        compiler_params=PARAMS,
        cost_estimate=cost(flops),
    )(*args)


def at_block(index, size):
    return pl.ds(pl.multiple_of(index * size, size), size)


def started(src, dst, sem):
    copy = pltpu.make_async_copy(src, dst, sem)
    copy.start()
    return copy


def pack_kernel(source_ref, s_ref, t_ref, out_ref, s_buf, t_buf, sem):
    v = lax.axis_index("vocab")
    columns = at_block(v % 2 * NX + v // 2, W)
    copies = [
        started(s_ref.at[:, columns], s_buf, sem.at[0]),
        started(t_ref.at[:, columns], t_buf, sem.at[1]),
    ]
    row = lax.broadcasted_iota(jnp.int32, (ROWS, 128), 0)
    lane = lax.broadcasted_iota(jnp.int32, (ROWS, 128), 1)
    digits = jnp.zeros((ROWS, 128), jnp.int32)
    for r in range(ROWS):
        source = source_ref[r]
        value = jnp.where(lane == 0, source >> 5, jnp.where(lane == 1, source & 31, 0))
        digits = jnp.where(row == r, value, digits)
    digits = digits.astype(F32).astype(BF)
    out_ref[:, :, 2 * W :] = jnp.broadcast_to(digits[None], (NZ, ROWS, 128))
    for k, (copy, buf) in enumerate(zip(copies, (s_buf, t_buf))):
        copy.wait()
        out_ref[:, :, k * W : (k + 1) * W] = jnp.broadcast_to(buf[...][None], (NZ, ROWS, W))


def join_kernel(place_ref, far_ref, own_ref, left_ref, right_ref, out_ref, digits_ref):
    for k, (step, ref) in enumerate(zip(STEPS, (own_ref, left_ref, right_ref, far_ref))):
        out_ref[k * NEAR : (k + 1) * NEAR] = ref[:, : 2 * W]
        digits_ref[at_block((place_ref[2] + step) % NY, NEAR)] = ref[:, 2 * W :]


def hold_kernel(place_ref, sw_ref, tw_ref, sw2_ref, tw2_ref, sw_out, tw_out, sw2_out, tw2_out, sem):
    half = at_block(place_ref[1], HALF)
    copies = [
        started(sw_ref, sw_out, sem.at[0]),
        started(tw_ref.at[half], tw_out, sem.at[1]),
        started(sw2_ref.at[half], sw2_out, sem.at[2]),
        started(tw2_ref.at[half], tw2_out, sem.at[3]),
    ]
    for copy in copies:
        copy.wait()


def weights(place_ref, own, refs, step):
    at = (place_ref[0] + step) % NX
    first = place_ref[1] * NX if own else 0
    return refs[0][at_block(first + at, W)], refs[1][at_block(at, W)]


def near_kernel(own, place_ref, sw_ref, tw_ref, p0, p1, p2, out_ref):
    pieces = (p0, p1, p2)
    y = place_ref[2]

    @pl.when(place_ref[1] == 0)
    def _():
        for n in range(2):
            columns = slice(n * W, (n + 1) * W)
            total = None
            for step, ref in zip(STEPS, pieces):
                weight = weights(place_ref, own, (sw_ref, tw_ref), step)[n]
                part = dot(ref[:, columns], weight)
                total = part if total is None else total + part
            for k, step in enumerate(STEPS):
                out_ref[n, at_block((y + step) % NY, NEAR)] = total[k * NEAR : (k + 1) * NEAR]

    @pl.when(place_ref[1] == 1)
    def _():
        for n in range(2):
            columns = slice(n * W, (n + 1) * W)
            total = None
            for k, step in enumerate(STEPS):
                rows = slice(k * NEAR, (k + 1) * NEAR)
                block = jnp.concatenate([ref[rows, columns] for ref in pieces], axis=0)
                part = dot(block, weights(place_ref, own, (sw_ref, tw_ref), step)[n])
                total = part if total is None else total + part
            for k, step in enumerate(STEPS[:3]):
                out_ref[n, at_block((y + step) % NY, NEAR)] = total[k * NEAR : (k + 1) * NEAR]


def far_kernel(own, place_ref, sw_ref, tw_ref, p3, p4, near_ref, *refs):
    y = place_ref[2]
    outs = refs[:2]

    @pl.when(place_ref[1] == 0)
    def _():
        for n, out_ref in enumerate(outs):
            columns = slice(n * W, (n + 1) * W)
            block = jnp.concatenate([p3[:, columns], p4[:, columns]], axis=0)
            part = dot(block, weights(place_ref, own, (sw_ref, tw_ref), STEPS[3])[n])
            for k, step in enumerate(STEPS):
                rows = at_block((y + step) % NY, NEAR)
                out_ref[rows] = near_ref[n, rows] + part[k * NEAR : (k + 1) * NEAR]

    @pl.when(place_ref[1] == 1)
    def _():
        for n, out_ref in enumerate(outs):
            columns = slice(n * W, (n + 1) * W)
            for step in STEPS[:3]:
                rows = at_block((y + step) % NY, NEAR)
                out_ref[rows] = near_ref[n, rows]
            total = None
            for k, step in enumerate(STEPS):
                rows = slice(k % 2 * NEAR, (k % 2 + 1) * NEAR)
                block = (p3, p4)[k // 2][rows, columns]
                part = dot(block, weights(place_ref, own, (sw_ref, tw_ref), step)[n])
                total = part if total is None else total + part
            out_ref[at_block((y + STEPS[3]) % NY, NEAR)] = total


def choose_kernel(place_ref, own_ref, other_ref, out_ref):
    digits = jnp.where(
        place_ref[1] == 0, own_ref[...].astype(F32), other_ref[...].astype(F32)
    )
    index = (digits[:, 0:1] * 32.0 + digits[:, 1:2]).astype(jnp.int32)
    column = lax.broadcasted_iota(jnp.int32, (N, N), 1)
    out_ref[...] = (index == column).astype(F32).astype(BF)


def pack_stats(lse_s, mean, lse_t):
    half = N // 2
    row = lax.broadcasted_iota(jnp.int32, (8, half), 0)
    out = jnp.zeros((8, half), F32)
    for k, value in enumerate((lse_s, mean, lse_t)):
        out = jnp.where(row == k, value[:, :half], out)
        out = jnp.where(row == k + 4, value[:, half:], out)
    return out


def merge(stats):
    def rows(k):
        return jnp.concatenate([stats[:, k : k + 1], stats[:, k + 4 : k + 5]], axis=2)

    def lse(x):
        top = jnp.max(x, axis=0)
        return top + jnp.log(jnp.sum(jnp.exp(x - top[None]), axis=0))

    each_s, each_mean, each_t = rows(0), rows(1), rows(2)
    lse_s = lse(each_s)
    mean = jnp.sum(jnp.exp(each_s - lse_s[None]) * each_mean, axis=0)
    return lse_s, mean, lse(each_t)


def table_of(pairs, table):
    lane = lax.broadcasted_iota(jnp.int32, (N, 128), 1)
    for k, value in pairs:
        table = jnp.where(lane == k, value, table)
    return table


def teacher_logits_kernel(own_ref, other_ref, select_ref, t_ref, table_ref):
    t = own_ref[...] + other_ref[...]
    select = select_ref[...]
    high = t.astype(BF)
    rest = t - high.astype(F32)
    middle = rest.astype(BF)
    low = (rest - middle.astype(F32)).astype(BF)
    t = dot(select, high) + dot(select, middle) + dot(select, low)
    t_ref[...] = t
    top = jnp.max(t, axis=1, keepdims=True)
    total = jnp.sum(jnp.exp(t - top), axis=1, keepdims=True)
    table_ref[...] = table_of(((3, top), (4, total)), jnp.zeros((N, 128), F32))


def student_logits_kernel(own_ref, other_ref, t_ref, table_ref, s_ref, diff_ref, stat_ref):
    s = own_ref[...] + other_ref[...]
    s_ref[...] = s
    diff = s - t_ref[...]
    diff_ref[...] = diff
    top = jnp.max(s, axis=1, keepdims=True)
    e = jnp.exp(s - top)
    total = jnp.sum(e, axis=1, keepdims=True)
    mix = jnp.sum(e * diff, axis=1, keepdims=True)
    table = table_of(((0, top), (1, total), (2, mix)), table_ref[...])
    table = jnp.transpose(table)
    s_top, s_sum, mix, t_top, t_sum = (table[k : k + 1] for k in range(5))
    stat = pack_stats(s_top + jnp.log(s_sum), mix / s_sum, t_top + jnp.log(t_sum))
    stat_ref[...] = jnp.broadcast_to(stat[None], stat_ref.shape)


def merge_kernel(in_ref, out_ref):
    out_ref[...] = jnp.broadcast_to(pack_stats(*merge(in_ref[...]))[None], out_ref.shape)


def exchange(x, axis, groups=None):
    n = x.shape[0]
    flat = x.reshape((n * x.shape[1],) + x.shape[2:])
    out = lax.all_to_all(flat, axis, 0, 0, axis_index_groups=groups, tiled=True)
    return out.reshape(x.shape)


def terms(place_ref, g, sw_ref, core, numbers):
    for k in numbers:
        block = (place_ref[0] + STEPS[k]) % NX * 2 + core
        yield dot(g, sw_ref[at_block(block, W)], ((1,), (1,)))


def first_for_other_kernel(
    place_ref, stat_ref, s_ref, d_ref, sw_ref, out_ref, turned_ref, loss_ref, g_ref
):
    lse_s, mean, lse_t = merge(stat_ref[...])
    loss_ref[...] = jnp.sum(mean - lse_s + lse_t, axis=1, keepdims=True) / N
    row = lax.broadcasted_iota(jnp.int32, (128, N), 0)
    table = jnp.where(row == 0, lse_s, jnp.where(row == 1, mean, 0.0))
    table = jnp.transpose(table)
    prob = jnp.exp(s_ref[...] - table[:, 0:1])
    g_ref[...] = prob * (d_ref[...] - table[:, 1:2])
    for k, step in enumerate(STEPS):
        rows = g_ref[at_block((place_ref[2] + step) % NY, NEAR)]
        turned_ref[k * NEAR : (k + 1) * NEAR] = rows.astype(BF)
    for k, part in enumerate(terms(place_ref, turned_ref[...], sw_ref, 1 - place_ref[1], (0, 1))):
        out_ref[k] = part.astype(BF)


def second_for_other_kernel(place_ref, g_ref, sw_ref, out_ref):
    for k, part in enumerate(terms(place_ref, g_ref[...], sw_ref, 1 - place_ref[1], (2, 3))):
        out_ref[k] = part.astype(BF)


def own_terms_kernel(place_ref, g_ref, sw_ref, out_ref):
    for k, part in enumerate(terms(place_ref, g_ref[...], sw_ref, place_ref[1], range(NX))):
        out_ref[k] = part


def add_kernel(place_ref, own_ref, first_ref, second_ref, *out_refs):
    core = place_ref[1]
    for k in range(NX):
        received = (first_ref, second_ref)[k // 2][k % 2]
        total = (own_ref[k] + received.astype(F32)).astype(BF)

        @pl.when(core == 0)
        def _():
            out_refs[k][...] = total

        @pl.when(core == 1)
        def _():
            for j, ref in enumerate(out_refs):
                ref[k * NEAR : (k + 1) * NEAR] = total[j * NEAR : (j + 1) * NEAR]


def total_of(refs):
    total = refs[0][...].astype(F32)
    for ref in refs[1:]:
        total = total + ref[...].astype(F32)
    return total.astype(BF)


def sum_first_kernel(*refs):
    total = total_of(refs[:4])
    for k, ref in enumerate(refs[4:]):
        ref[...] = total[k * NEAR : (k + 1) * NEAR]


def sum_second_kernel(*refs):
    refs[-1][...] = total_of(refs[:4])


def sum_kernel(in_ref, out_ref):
    out_ref[...] = jnp.sum(in_ref[...].astype(F32), axis=0).astype(BF)


def summed(x):
    return call(sum_kernel, [VM], [(x.shape[1:], BF)], x)[0]


def to_other_core(a):
    return lax.ppermute(a, "vocab", [(k, k ^ 1) for k in range(VOC)])


def along_rings(a, step, x_core):
    pairs = []
    for v in range(VOC):
        for t in range(TOK):
            if v % 2 == x_core:
                to = (v // 2 + step) % NX * 2 + v % 2, t
            else:
                to = v, (t // NZ + step) % NY * NZ + t % NZ
            pairs.append((v * TOK + t, to[0] * TOK + to[1]))
    return lax.ppermute(a, ("vocab", "tok"), pairs)


def along_first(a, step):
    return along_rings(a, step, 0)


def along_second(a, step):
    return along_rings(a, step, 1)


def ring(a, along):
    return along(a, 2), a, along(a, 1), along(a, -1)


def to_ring(blocks, along):
    own, left, right, far = blocks
    return along(far, 2), along(left, -1), along(right, 1), own


def per_device(student_hidden, teacher_hidden, student_weight, teacher_weight, source_rows):
    v = lax.axis_index("vocab").astype(jnp.int32)
    y = lax.axis_index("tok").astype(jnp.int32) // NZ
    place = jnp.stack([v // 2, v % 2, y])
    packed = call(
        pack_kernel,
        [SM, HBM, HBM],
        [((NZ, ROWS, 2 * W + 128), BF)],
        source_rows, in_hbm(student_hidden), in_hbm(teacher_hidden),
        scratch=[pltpu.VMEM((ROWS, W), BF)] * 2 + [pltpu.SemaphoreType.DMA((2,))],
    )[0]
    sw2, tw2 = to_other_core(student_weight), to_other_core(teacher_weight)
    near = exchange(packed, "tok", Z_GROUPS).reshape(NEAR, 2 * W + 128)
    near, sw2, tw2 = lax.optimization_barrier((near, sw2, tw2))
    mine, digits = call(
        join_kernel,
        [SM] + [VM] * 4,
        [((N, 2 * W), BF), ((N, 128), BF)],
        place, *ring(near, along_second),
    )
    left, right = along_first(mine, 1), along_first(mine, -1)
    held = call(
        hold_kernel,
        [SM] + [HBM] * 4,
        [((D, C), BF)] + [((HALF, C), BF)] * 3,
        place, *(in_hbm(x) for x in (student_weight, teacher_weight, sw2, tw2)),
        scratch=[pltpu.SemaphoreType.DMA((4,))],
    )
    left, right, held = lax.optimization_barrier((left, right, held))
    sw, tw, sw2, tw2 = held
    far = along_first(left[: N // 2], 1), along_first(right[N // 2 :], -1)
    digits2 = to_other_core(digits)
    part = [((2, N, C), F32)]

    def near_part(own, *held):
        kernel = functools.partial(near_kernel, own)
        flops = 3 * N * HALF * C
        return call(kernel, [SM] + [VM] * 5, part, place, *held, mine, left, right, flops=flops)[0]

    logits = [((N, C), F32)]

    def far_part(own, *held_and_near):
        kernel = functools.partial(far_kernel, own)
        sw, tw, near = held_and_near
        return call(kernel, [SM] + [VM] * 5, logits * 2, place, sw, tw, *far, near)

    for_other, own = near_part(False, sw2, tw2), near_part(True, sw, tw)
    select = call(choose_kernel, [SM, VM, VM], [((N, N), BF)], place, digits, digits2)[0]
    far, for_other, own, select = lax.optimization_barrier((far, for_other, own, select))
    s_other, t_other = far_part(False, sw2, tw2, for_other)
    t_other, s_other = to_other_core(t_other), to_other_core(s_other)
    s_own, t_own = far_part(True, sw, tw, own)
    t_own, t_other = lax.optimization_barrier((t_own, t_other))
    t, table = call(
        teacher_logits_kernel,
        [VM] * 3,
        logits + [((N, 128), F32)],
        t_own, t_other, select,
    )
    s_other, t, table = lax.optimization_barrier((s_other, t, table))
    s, d, stats = call(
        student_logits_kernel,
        [VM] * 4,
        logits * 2 + [((VOC, 8, N // 2), F32)],
        s_own, s_other, t, table,
    )
    stats = exchange(stats, "vocab")
    stats = call(merge_kernel, [VM], [((TOK, 8, N // 2), F32)], stats)[0]
    stats = exchange(stats, "tok")
    half = ((NX // 2, N, W), BF)
    first, g, loss = call(
        first_for_other_kernel,
        [SM] + [VM] * 4,
        [half, ((N, C), BF), ((1, 1), F32)],
        place, stats, s, d, sw,
        scratch=[pltpu.VMEM((N, C), F32)],
    )
    second = call(second_for_other_kernel, [SM, VM, VM], [half], place, g, sw)[0]
    own = call(
        own_terms_kernel, [SM, VM, VM], [((NX, N, W), F32)], place, g, sw
    )[0]
    first, second, own = lax.optimization_barrier(
        (to_other_core(first), to_other_core(second), own)
    )
    blocks = call(
        add_kernel, [SM] + [VM] * 3, [((N, W), BF)] * 4, place, own, first, second
    )
    blocks = call(
        sum_first_kernel, [VM] * 4, [((NEAR, W), BF)] * 4, *to_ring(blocks, along_first)
    )
    partial = call(
        sum_second_kernel, [VM] * 4, [((NEAR, W), BF)], *to_ring(blocks, along_second)
    )[0]
    hidden_grad = summed(exchange(partial.reshape(NZ, ROWS, W), "tok", Z_GROUPS))
    return loss[0, 0], hidden_grad


def solution(mesh):
    in_specs = (
        P("tok", None),
        P("tok", None),
        P(None, ("vocab", "tok")),
        P(None, ("vocab", "tok")),
        P("tok"),
    )
    out_specs = (P(), P("tok", "vocab"))
    return jax.shard_map(
        per_device, mesh=mesh, in_specs=in_specs, out_specs=out_specs, check_vma=False
    )
```

```python
import functools

import jax
import jax.numpy as jnp
from jax import lax
from jax.experimental import pallas as pl
from jax.experimental.pallas import tpu as pltpu
from jax.sharding import PartitionSpec as P

BF = jnp.bfloat16
F32 = jnp.float32
TOK, VOC = 32, 8
NX, NY, NZ = 4, 4, 8
N = 512
D = 4096
C = 512
W = 512
ROWS = N // TOK
NEAR = N // NY
HALF = NX * W
MIB = 1 << 20
STEPS = (0, -1, 1, 2)
Z_GROUPS = [[y * NZ + z for z in range(NZ)] for y in range(NY)]


def dot(a, b, dims=((1,), (0,))):
    return lax.dot_general(a, b, (dims, ((), ())), preferred_element_type=F32)


PARAMS = pltpu.CompilerParams(vmem_limit_bytes=20 * MIB)
VM = pl.BlockSpec(memory_space=pltpu.VMEM)
SM = pl.BlockSpec(memory_space=pltpu.SMEM)
HBM = pl.BlockSpec(memory_space=pltpu.HBM)


def out(shape, dtype):
    return pltpu.VMEM(shape, dtype)


def in_hbm(x):
    return pltpu.with_memory_space_constraint(x, pltpu.HBM)


def cost(flops, mib=0):
    return pl.CostEstimate(flops=flops, bytes_accessed=mib * MIB, transcendentals=0)


def call(kernel, in_specs, outs, *args, scratch=(), flops=0):
    return pl.pallas_call(
        kernel,
        in_specs=in_specs,
        out_specs=[VM] * len(outs),
        out_shape=[out(*o) for o in outs],
        scratch_shapes=list(scratch),
        compiler_params=PARAMS,
        cost_estimate=cost(flops),
    )(*args)


def at_block(index, size):
    return pl.ds(pl.multiple_of(index * size, size), size)


def started(src, dst, sem):
    copy = pltpu.make_async_copy(src, dst, sem)
    copy.start()
    return copy


def pack_kernel(source_ref, s_ref, t_ref, out_ref, s_buf, t_buf, sem):
    v = lax.axis_index("vocab")
    columns = at_block(v, W)
    copies = [
        started(s_ref.at[:, columns], s_buf, sem.at[0]),
        started(t_ref.at[:, columns], t_buf, sem.at[1]),
    ]
    row = lax.broadcasted_iota(jnp.int32, (ROWS, 128), 0)
    lane = lax.broadcasted_iota(jnp.int32, (ROWS, 128), 1)
    digits = jnp.zeros((ROWS, 128), jnp.int32)
    for r in range(ROWS):
        source = source_ref[r]
        value = jnp.where(lane == 0, source >> 5, jnp.where(lane == 1, source & 31, 0))
        digits = jnp.where(row == r, value, digits)
    digits = digits.astype(F32).astype(BF)
    out_ref[:, :, 2 * W :] = jnp.broadcast_to(digits[None], (NZ, ROWS, 128))
    for k, (copy, buf) in enumerate(zip(copies, (s_buf, t_buf))):
        copy.wait()
        out_ref[:, :, k * W : (k + 1) * W] = jnp.broadcast_to(buf[...][None], (NZ, ROWS, W))


def join_kernel(place_ref, far_ref, own_ref, left_ref, right_ref, a_ref, b_ref, digits_ref):
    for k, (step, ref) in enumerate(zip(STEPS, (own_ref, left_ref, right_ref, far_ref))):
        (a_ref, b_ref)[k // 2][k % 2 * NEAR : (k % 2 + 1) * NEAR] = ref[:, : 2 * W]
        digits_ref[at_block((place_ref[2] + step) % NY, NEAR)] = ref[:, 2 * W :]


def hold_kernel(place_ref, *refs):
    sem = refs[-1]
    copies = []
    for n, (ref, out_ref) in enumerate(zip(refs[:4], refs[4:8])):
        for x in range(NX):
            rows = ref.at[at_block(2 * x + place_ref[1], W)]
            copies.append(started(rows, out_ref.at[x * W : (x + 1) * W], sem.at[n, x]))
    for copy in copies:
        copy.wait()


def weights(place_ref, refs, step):
    at = at_block((place_ref[0] + step) % NX, W)
    return [ref[at] for ref in refs]


def near_kernel(numbers, place_ref, sw_ref, tw_ref, *refs):
    pieces = [refs[2 * k : 2 * k + 2] for k in range(len(numbers))]
    steps = [STEPS[k] for k in numbers]
    before_refs, out_ref = refs[2 * len(numbers) : -1], refs[-1]
    y = place_ref[2]

    @pl.when(place_ref[1] == 0)
    def _():
        for n in range(2):
            columns = slice(n * W, (n + 1) * W)
            total = before_refs[0][n] if before_refs else None
            for step, halves in zip(steps, pieces):
                block = jnp.concatenate([ref[:, columns] for ref in halves], axis=0)
                part = dot(block, weights(place_ref, (sw_ref, tw_ref), step)[n])
                total = part if total is None else total + part
            out_ref[n] = total

    @pl.when(place_ref[1] == 1)
    def _():
        for n in range(2):
            columns = slice(n * W, (n + 1) * W)
            total = None
            for k, step in enumerate(STEPS):
                rows = slice(k % 2 * NEAR, (k % 2 + 1) * NEAR)
                block = jnp.concatenate([halves[k // 2][rows, columns] for halves in pieces], axis=0)
                part = dot(block, weights(place_ref, (sw_ref, tw_ref), step)[n])
                total = part if total is None else total + part
            for k, number in enumerate(numbers):
                out_ref[n, number * NEAR : (number + 1) * NEAR] = total[k * NEAR : (k + 1) * NEAR]
            for before_ref in before_refs:
                out_ref[n, :NEAR] = before_ref[n, :NEAR]


def far_kernel(place_ref, sw_ref, tw_ref, p3, p4, near_ref, *refs):
    y = place_ref[2]
    outs = refs[:2]

    @pl.when(place_ref[1] == 0)
    def _():
        for n, out_ref in enumerate(outs):
            columns = slice(n * W, (n + 1) * W)
            block = jnp.concatenate([p3[:, columns], p4[:, columns]], axis=0)
            part = dot(block, weights(place_ref, (sw_ref, tw_ref), STEPS[3])[n])
            for k, step in enumerate(STEPS):
                rows = at_block((y + step) % NY, NEAR)
                here = slice(k * NEAR, (k + 1) * NEAR)
                out_ref[rows] = near_ref[n, here] + part[here]

    @pl.when(place_ref[1] == 1)
    def _():
        for n, out_ref in enumerate(outs):
            columns = slice(n * W, (n + 1) * W)
            for k, step in enumerate(STEPS[:3]):
                here = slice(k * NEAR, (k + 1) * NEAR)
                out_ref[at_block((y + step) % NY, NEAR)] = near_ref[n, here]
            total = None
            for k, step in enumerate(STEPS):
                rows = slice(k % 2 * NEAR, (k % 2 + 1) * NEAR)
                block = (p3, p4)[k // 2][rows, columns]
                part = dot(block, weights(place_ref, (sw_ref, tw_ref), step)[n])
                total = part if total is None else total + part
            out_ref[at_block((y + STEPS[3]) % NY, NEAR)] = total


def choose_kernel(place_ref, own_ref, other_ref, out_ref):
    digits = jnp.where(
        place_ref[1] == 0, own_ref[...].astype(F32), other_ref[...].astype(F32)
    )
    index = (digits[:, 0:1] * 32.0 + digits[:, 1:2]).astype(jnp.int32)
    column = lax.broadcasted_iota(jnp.int32, (N, N), 1)
    out_ref[...] = (index == column).astype(F32).astype(BF)


def pack_stats(lse_s, mean, lse_t):
    half = N // 2
    row = lax.broadcasted_iota(jnp.int32, (8, half), 0)
    out = jnp.zeros((8, half), F32)
    for k, value in enumerate((lse_s, mean, lse_t)):
        out = jnp.where(row == k, value[:, :half], out)
        out = jnp.where(row == k + 4, value[:, half:], out)
    return out


def merge(stats):
    def rows(k):
        return jnp.concatenate([stats[:, k : k + 1], stats[:, k + 4 : k + 5]], axis=2)

    def lse(x):
        top = jnp.max(x, axis=0)
        return top + jnp.log(jnp.sum(jnp.exp(x - top[None]), axis=0))

    each_s, each_mean, each_t = rows(0), rows(1), rows(2)
    lse_s = lse(each_s)
    mean = jnp.sum(jnp.exp(each_s - lse_s[None]) * each_mean, axis=0)
    return lse_s, mean, lse(each_t)


def table_of(pairs, table):
    lane = lax.broadcasted_iota(jnp.int32, (N, 128), 1)
    for k, value in pairs:
        table = jnp.where(lane == k, value, table)
    return table


def teacher_logits_kernel(own_ref, other_ref, select_ref, t_ref, table_ref):
    t = own_ref[...] + other_ref[...]
    select = select_ref[...]
    high = t.astype(BF)
    rest = t - high.astype(F32)
    middle = rest.astype(BF)
    low = (rest - middle.astype(F32)).astype(BF)
    t = dot(select, high) + dot(select, middle) + dot(select, low)
    t_ref[...] = t
    top = jnp.max(t, axis=1, keepdims=True)
    total = jnp.sum(jnp.exp(t - top), axis=1, keepdims=True)
    table_ref[...] = table_of(((3, top), (4, total)), jnp.zeros((N, 128), F32))


def student_logits_kernel(own_ref, other_ref, t_ref, table_ref, s_ref, diff_ref, stat_ref):
    s = own_ref[...] + other_ref[...]
    s_ref[...] = s
    diff = s - t_ref[...]
    diff_ref[...] = diff
    top = jnp.max(s, axis=1, keepdims=True)
    e = jnp.exp(s - top)
    total = jnp.sum(e, axis=1, keepdims=True)
    mix = jnp.sum(e * diff, axis=1, keepdims=True)
    table = table_of(((0, top), (1, total), (2, mix)), table_ref[...])
    table = jnp.transpose(table)
    s_top, s_sum, mix, t_top, t_sum = (table[k : k + 1] for k in range(5))
    stat = pack_stats(s_top + jnp.log(s_sum), mix / s_sum, t_top + jnp.log(t_sum))
    stat_ref[...] = jnp.broadcast_to(stat[None], stat_ref.shape)


def merge_kernel(in_ref, out_ref):
    out_ref[...] = jnp.broadcast_to(pack_stats(*merge(in_ref[...]))[None], out_ref.shape)


def exchange(x, axis, groups=None):
    n = x.shape[0]
    flat = x.reshape((n * x.shape[1],) + x.shape[2:])
    out = lax.all_to_all(flat, axis, 0, 0, axis_index_groups=groups, tiled=True)
    return out.reshape(x.shape)


def terms(place_ref, g, sw_ref):
    for step in STEPS:
        yield dot(g, sw_ref[at_block((place_ref[0] + step) % NX, W)], ((1,), (1,)))


def logit_grad_kernel(place_ref, stat_ref, s_ref, d_ref, turned_ref, loss_ref, g_ref):
    lse_s, mean, lse_t = merge(stat_ref[...])
    loss_ref[...] = jnp.sum(mean - lse_s + lse_t, axis=1, keepdims=True) / N
    row = lax.broadcasted_iota(jnp.int32, (128, N), 0)
    table = jnp.where(row == 0, lse_s, jnp.where(row == 1, mean, 0.0))
    table = jnp.transpose(table)
    prob = jnp.exp(s_ref[...] - table[:, 0:1])
    g_ref[...] = prob * (d_ref[...] - table[:, 1:2])
    for k, step in enumerate(STEPS):
        rows = g_ref[at_block((place_ref[2] + step) % NY, NEAR)]
        turned_ref[k * NEAR : (k + 1) * NEAR] = rows.astype(BF)


def own_terms_kernel(place_ref, g_ref, sw_ref, out_ref):
    for k, part in enumerate(terms(place_ref, g_ref[...], sw_ref)):
        out_ref[k] = part


def add_kernel(place_ref, own_ref, g_ref, sw_ref, *out_refs):
    core = place_ref[1]
    for k, part in enumerate(terms(place_ref, g_ref[...], sw_ref)):
        total = (own_ref[k] + part).astype(BF)

        @pl.when(core == 0)
        def _():
            out_refs[k][...] = total

        @pl.when(core == 1)
        def _():
            for j, ref in enumerate(out_refs):
                ref[k * NEAR : (k + 1) * NEAR] = total[j * NEAR : (j + 1) * NEAR]


def total_of(refs):
    total = refs[0][...].astype(F32)
    for ref in refs[1:]:
        total = total + ref[...].astype(F32)
    return total.astype(BF)


def sum_first_kernel(*refs):
    total = total_of(refs[:4])
    for k, ref in enumerate(refs[4:]):
        ref[...] = total[k * NEAR : (k + 1) * NEAR]


def sum_second_kernel(*refs):
    refs[-1][...] = total_of(refs[:4])


def sum_kernel(in_ref, out_ref):
    out_ref[...] = jnp.sum(in_ref[...].astype(F32), axis=0).astype(BF)


def summed(x):
    return call(sum_kernel, [VM], [(x.shape[1:], BF)], x)[0]


def to_other_core(a):
    return lax.ppermute(a, "vocab", [(k, k ^ 1) for k in range(VOC)])


def along_rings(a, step, x_core):
    pairs = []
    for v in range(VOC):
        for t in range(TOK):
            if v % 2 == x_core:
                to = (v // 2 + step) % NX * 2 + v % 2, t
            else:
                to = v, (t // NZ + step) % NY * NZ + t % NZ
            pairs.append((v * TOK + t, to[0] * TOK + to[1]))
    return lax.ppermute(a, ("vocab", "tok"), pairs)


def along_first(a, step):
    return along_rings(a, step, 0)


def along_second(a, step):
    return along_rings(a, step, 1)


def ring(a, along):
    return along(a, 2), a, along(a, 1), along(a, -1)


def to_ring(blocks, along):
    own, left, right, far = blocks
    return along(far, 2), along(left, -1), along(right, 1), own


def per_device(student_hidden, teacher_hidden, student_weight, teacher_weight, source_rows):
    v = lax.axis_index("vocab").astype(jnp.int32)
    y = lax.axis_index("tok").astype(jnp.int32) // NZ
    place = jnp.stack([v // 2, v % 2, y])
    packed = call(
        pack_kernel,
        [SM, HBM, HBM],
        [((NZ, ROWS, 2 * W + 128), BF)],
        source_rows, in_hbm(student_hidden), in_hbm(teacher_hidden),
        scratch=[pltpu.VMEM((ROWS, W), BF)] * 2 + [pltpu.SemaphoreType.DMA((2,))],
    )[0]
    sw2, tw2 = to_other_core(student_weight), to_other_core(teacher_weight)
    near = exchange(packed, "tok", Z_GROUPS).reshape(NEAR, 2 * W + 128)
    near, sw2, tw2 = lax.optimization_barrier((near, sw2, tw2))
    half = ((N // 2, 2 * W), BF)
    mine_a, mine_b, digits = call(
        join_kernel,
        [SM] + [VM] * 4,
        [half, half, ((N, 128), BF)],
        place, *ring(near, along_second),
    )
    left_a, right_b = along_first(mine_a, 1), along_first(mine_b, -1)
    left_b, right_a = along_first(mine_b, 1), along_first(mine_a, -1)
    held = call(
        hold_kernel,
        [SM] + [HBM] * 4,
        [((HALF, C), BF)] * 4,
        place, *(in_hbm(x) for x in (student_weight, teacher_weight, sw2, tw2)),
        scratch=[pltpu.SemaphoreType.DMA((4, NX))],
    )
    left_a, right_b, held = lax.optimization_barrier((left_a, right_b, held))
    far = along_first(left_a, 1), along_first(right_b, -1)
    sw, tw, sw2, tw2 = held
    digits2 = to_other_core(digits)
    part = [((2, N, C), F32)]

    def near_part(numbers, held, *pieces):
        kernel = functools.partial(near_kernel, numbers)
        specs = [SM] + [VM] * (2 + len(pieces))
        flops = len(numbers) * N * HALF * C
        return call(kernel, specs, part, place, *held, *pieces, flops=flops)[0]

    weights_other, weights_own = (sw2, tw2), (sw, tw)
    for_other = near_part((0,), weights_other, mine_a, mine_b)
    own = near_part((0,), weights_own, mine_a, mine_b)
    left_b, right_a, for_other, own = lax.optimization_barrier((left_b, right_a, for_other, own))
    sides = left_a, left_b, right_a, right_b
    logits = [((N, C), F32)]

    def far_part(held, near):
        return call(far_kernel, [SM] + [VM] * 5, logits * 2, place, *held, *far, near)

    for_other = near_part((1, 2), weights_other, *sides, for_other)
    own = near_part((1, 2), weights_own, *sides, own)
    select = call(choose_kernel, [SM, VM, VM], [((N, N), BF)], place, digits, digits2)[0]
    far, for_other, own, select = lax.optimization_barrier((far, for_other, own, select))
    s_other, t_other = far_part(weights_other, for_other)
    t_other, s_other = to_other_core(t_other), to_other_core(s_other)
    s_own, t_own = far_part(weights_own, own)
    t_own, t_other = lax.optimization_barrier((t_own, t_other))
    t, table = call(
        teacher_logits_kernel,
        [VM] * 3,
        logits + [((N, 128), F32)],
        t_own, t_other, select,
    )
    s_other, t, table = lax.optimization_barrier((s_other, t, table))
    s, d, stats = call(
        student_logits_kernel,
        [VM] * 4,
        logits * 2 + [((VOC, 8, N // 2), F32)],
        s_own, s_other, t, table,
    )
    stats = exchange(stats, "vocab")
    stats = call(merge_kernel, [VM], [((TOK, 8, N // 2), F32)], stats)[0]
    stats = exchange(stats, "tok")
    g, loss = call(
        logit_grad_kernel,
        [SM] + [VM] * 3,
        [((N, C), BF), ((1, 1), F32)],
        place, stats, s, d,
        scratch=[pltpu.VMEM((N, C), F32)],
    )
    own = call(own_terms_kernel, [SM, VM, VM], [((NX, N, W), F32)], place, g, sw)[0]
    g_other, own = lax.optimization_barrier((to_other_core(g), own))
    blocks = call(
        add_kernel, [SM] + [VM] * 3, [((N, W), BF)] * 4, place, own, g_other, sw2
    )
    blocks = call(
        sum_first_kernel, [VM] * 4, [((NEAR, W), BF)] * 4, *to_ring(blocks, along_first)
    )
    partial = call(
        sum_second_kernel, [VM] * 4, [((NEAR, W), BF)], *to_ring(blocks, along_second)
    )[0]
    hidden_grad = summed(exchange(partial.reshape(NZ, ROWS, W), "tok", Z_GROUPS))
    return loss[0, 0], hidden_grad


def solution(mesh):
    in_specs = (
        P("tok", None),
        P("tok", None),
        P(None, ("vocab", "tok")),
        P(None, ("vocab", "tok")),
        P("tok"),
    )
    out_specs = (P(), P("tok", "vocab"))
    return jax.shard_map(
        per_device, mesh=mesh, in_specs=in_specs, out_specs=out_specs, check_vma=False
    )
```

```python
import functools

import jax
import jax.numpy as jnp
from jax import lax
from jax.experimental import pallas as pl
from jax.experimental.pallas import tpu as pltpu
from jax.sharding import PartitionSpec as P

BF = jnp.bfloat16
F32 = jnp.float32
TOK, VOC = 32, 8
NX, NY, NZ = 4, 4, 8
N = 512
D = 4096
C = 512
W = 512
ROWS = N // TOK
NEAR = N // NY
HALF = NX * W
MIB = 1 << 20
STEPS = (0, -1, 1, 2)
Z_GROUPS = [[y * NZ + z for z in range(NZ)] for y in range(NY)]


def dot(a, b, dims=((1,), (0,))):
    return lax.dot_general(a, b, (dims, ((), ())), preferred_element_type=F32)


PARAMS = pltpu.CompilerParams(vmem_limit_bytes=20 * MIB)
VM = pl.BlockSpec(memory_space=pltpu.VMEM)
SM = pl.BlockSpec(memory_space=pltpu.SMEM)
HBM = pl.BlockSpec(memory_space=pltpu.HBM)


def out(shape, dtype):
    return pltpu.VMEM(shape, dtype)


def in_hbm(x):
    return pltpu.with_memory_space_constraint(x, pltpu.HBM)


def cost(flops, mib=0):
    return pl.CostEstimate(flops=flops, bytes_accessed=mib * MIB, transcendentals=0)


def call(kernel, in_specs, outs, *args, scratch=(), flops=0):
    return pl.pallas_call(
        kernel,
        in_specs=in_specs,
        out_specs=[VM] * len(outs),
        out_shape=[out(*o) for o in outs],
        scratch_shapes=list(scratch),
        compiler_params=PARAMS,
        cost_estimate=cost(flops),
    )(*args)


def at_block(index, size):
    return pl.ds(pl.multiple_of(index * size, size), size)


def started(src, dst, sem):
    copy = pltpu.make_async_copy(src, dst, sem)
    copy.start()
    return copy


def pack_kernel(source_ref, s_ref, t_ref, out_ref, s_buf, t_buf, sem):
    v = lax.axis_index("vocab")
    columns = at_block(v, W)
    copies = [
        started(s_ref.at[:, columns], s_buf, sem.at[0]),
        started(t_ref.at[:, columns], t_buf, sem.at[1]),
    ]
    row = lax.broadcasted_iota(jnp.int32, (ROWS, 128), 0)
    lane = lax.broadcasted_iota(jnp.int32, (ROWS, 128), 1)
    digits = jnp.zeros((ROWS, 128), jnp.int32)
    for r in range(ROWS):
        source = source_ref[r]
        value = jnp.where(lane == 0, source >> 5, jnp.where(lane == 1, source & 31, 0))
        digits = jnp.where(row == r, value, digits)
    digits = digits.astype(F32).astype(BF)
    out_ref[:, :, 2 * W :] = jnp.broadcast_to(digits[None], (NZ, ROWS, 128))
    for k, (copy, buf) in enumerate(zip(copies, (s_buf, t_buf))):
        copy.wait()
        out_ref[:, :, k * W : (k + 1) * W] = jnp.broadcast_to(buf[...][None], (NZ, ROWS, W))


def join_kernel(place_ref, far_ref, own_ref, left_ref, right_ref, a_ref, b_ref, digits_ref):
    for k, (step, ref) in enumerate(zip(STEPS, (own_ref, left_ref, right_ref, far_ref))):
        (a_ref, b_ref)[k // 2][k % 2 * NEAR : (k % 2 + 1) * NEAR] = ref[:, : 2 * W]
        digits_ref[at_block((place_ref[2] + step) % NY, NEAR)] = ref[:, 2 * W :]


def hold_kernel(place_ref, *refs):
    sem = refs[-1]
    copies = []
    for n, (ref, out_ref) in enumerate(zip(refs[:4], refs[4:8])):
        for x in range(NX):
            rows = ref.at[at_block(2 * x + place_ref[1], W)]
            copies.append(started(rows, out_ref.at[x * W : (x + 1) * W], sem.at[n, x]))
    for copy in copies:
        copy.wait()


def weights(place_ref, refs, step):
    at = at_block((place_ref[0] + step) % NX, W)
    return [ref[at] for ref in refs]


def near_kernel(numbers, place_ref, sw_ref, tw_ref, *refs):
    pieces = [refs[2 * k : 2 * k + 2] for k in range(len(numbers))]
    steps = [STEPS[k] for k in numbers]
    before_refs, out_ref = refs[2 * len(numbers) : -1], refs[-1]
    y = place_ref[2]

    @pl.when(place_ref[1] == 0)
    def _():
        for n in range(2):
            columns = slice(n * W, (n + 1) * W)
            total = before_refs[0][n] if before_refs else None
            for step, halves in zip(steps, pieces):
                block = jnp.concatenate([ref[:, columns] for ref in halves], axis=0)
                part = dot(block, weights(place_ref, (sw_ref, tw_ref), step)[n])
                total = part if total is None else total + part
            out_ref[n] = total

    @pl.when(place_ref[1] == 1)
    def _():
        for n in range(2):
            columns = slice(n * W, (n + 1) * W)
            total = None
            for k, step in enumerate(STEPS):
                rows = slice(k % 2 * NEAR, (k % 2 + 1) * NEAR)
                block = jnp.concatenate([halves[k // 2][rows, columns] for halves in pieces], axis=0)
                part = dot(block, weights(place_ref, (sw_ref, tw_ref), step)[n])
                total = part if total is None else total + part
            for k, number in enumerate(numbers):
                out_ref[n, number * NEAR : (number + 1) * NEAR] = total[k * NEAR : (k + 1) * NEAR]
            for before_ref in before_refs:
                out_ref[n, :NEAR] = before_ref[n, :NEAR]


def far_kernel(place_ref, sw_ref, tw_ref, p3, p4, near_ref, *refs):
    y = place_ref[2]
    outs = refs[:2]

    @pl.when(place_ref[1] == 0)
    def _():
        for n, out_ref in enumerate(outs):
            columns = slice(n * W, (n + 1) * W)
            block = jnp.concatenate([p3[:, columns], p4[:, columns]], axis=0)
            part = dot(block, weights(place_ref, (sw_ref, tw_ref), STEPS[3])[n])
            for k, step in enumerate(STEPS):
                rows = at_block((y + step) % NY, NEAR)
                here = slice(k * NEAR, (k + 1) * NEAR)
                out_ref[rows] = near_ref[n, here] + part[here]

    @pl.when(place_ref[1] == 1)
    def _():
        for n, out_ref in enumerate(outs):
            columns = slice(n * W, (n + 1) * W)
            for k, step in enumerate(STEPS[:3]):
                here = slice(k * NEAR, (k + 1) * NEAR)
                out_ref[at_block((y + step) % NY, NEAR)] = near_ref[n, here]
            total = None
            for k, step in enumerate(STEPS):
                rows = slice(k % 2 * NEAR, (k % 2 + 1) * NEAR)
                block = (p3, p4)[k // 2][rows, columns]
                part = dot(block, weights(place_ref, (sw_ref, tw_ref), step)[n])
                total = part if total is None else total + part
            out_ref[at_block((y + STEPS[3]) % NY, NEAR)] = total


def choose_kernel(place_ref, own_ref, other_ref, out_ref):
    digits = jnp.where(
        place_ref[1] == 0, own_ref[...].astype(F32), other_ref[...].astype(F32)
    )
    index = (digits[:, 0:1] * 32.0 + digits[:, 1:2]).astype(jnp.int32)
    column = lax.broadcasted_iota(jnp.int32, (N, N), 1)
    out_ref[...] = (index == column).astype(F32).astype(BF)


def pack_stats(lse_s, mean, lse_t):
    half = N // 2
    row = lax.broadcasted_iota(jnp.int32, (8, half), 0)
    out = jnp.zeros((8, half), F32)
    for k, value in enumerate((lse_s, mean, lse_t)):
        out = jnp.where(row == k, value[:, :half], out)
        out = jnp.where(row == k + 4, value[:, half:], out)
    return out


def merge(stats):
    def rows(k):
        return jnp.concatenate([stats[:, k : k + 1], stats[:, k + 4 : k + 5]], axis=2)

    def lse(x):
        top = jnp.max(x, axis=0)
        return top + jnp.log(jnp.sum(jnp.exp(x - top[None]), axis=0))

    each_s, each_mean, each_t = rows(0), rows(1), rows(2)
    lse_s = lse(each_s)
    mean = jnp.sum(jnp.exp(each_s - lse_s[None]) * each_mean, axis=0)
    return lse_s, mean, lse(each_t)


def table_of(pairs, table):
    lane = lax.broadcasted_iota(jnp.int32, (N, 128), 1)
    for k, value in pairs:
        table = jnp.where(lane == k, value, table)
    return table


def teacher_logits_kernel(own_ref, other_ref, select_ref, t_ref, table_ref):
    t = own_ref[...] + other_ref[...]
    select = select_ref[...]
    high = t.astype(BF)
    rest = t - high.astype(F32)
    middle = rest.astype(BF)
    low = (rest - middle.astype(F32)).astype(BF)
    t = dot(select, high) + dot(select, middle) + dot(select, low)
    t_ref[...] = t
    top = jnp.max(t, axis=1, keepdims=True)
    total = jnp.sum(jnp.exp(t - top), axis=1, keepdims=True)
    table_ref[...] = table_of(((3, top), (4, total)), jnp.zeros((N, 128), F32))


def student_logits_kernel(own_ref, other_ref, t_ref, table_ref, s_ref, diff_ref, stat_ref):
    s = own_ref[...] + other_ref[...]
    s_ref[...] = s
    diff = s - t_ref[...]
    diff_ref[...] = diff
    top = jnp.max(s, axis=1, keepdims=True)
    e = jnp.exp(s - top)
    total = jnp.sum(e, axis=1, keepdims=True)
    mix = jnp.sum(e * diff, axis=1, keepdims=True)
    table = table_of(((0, top), (1, total), (2, mix)), table_ref[...])
    table = jnp.transpose(table)
    s_top, s_sum, mix, t_top, t_sum = (table[k : k + 1] for k in range(5))
    stat = pack_stats(s_top + jnp.log(s_sum), mix / s_sum, t_top + jnp.log(t_sum))
    stat_ref[...] = jnp.broadcast_to(stat[None], stat_ref.shape)


def merge_kernel(in_ref, out_ref):
    out_ref[...] = jnp.broadcast_to(pack_stats(*merge(in_ref[...]))[None], out_ref.shape)


def exchange(x, axis, groups=None):
    n = x.shape[0]
    flat = x.reshape((n * x.shape[1],) + x.shape[2:])
    out = lax.all_to_all(flat, axis, 0, 0, axis_index_groups=groups, tiled=True)
    return out.reshape(x.shape)


def terms(place_ref, g, sw_ref):
    for step in STEPS:
        yield dot(g, sw_ref[at_block((place_ref[0] + step) % NX, W)], ((1,), (1,)))


def logit_grad_kernel(place_ref, stat_ref, s_ref, d_ref, turned_ref, loss_ref, g_ref):
    lse_s, mean, lse_t = merge(stat_ref[...])
    loss_ref[...] = jnp.sum(mean - lse_s + lse_t, axis=1, keepdims=True) / N
    row = lax.broadcasted_iota(jnp.int32, (128, N), 0)
    table = jnp.where(row == 0, lse_s, jnp.where(row == 1, mean, 0.0))
    table = jnp.transpose(table)
    prob = jnp.exp(s_ref[...] - table[:, 0:1])
    g_ref[...] = prob * (d_ref[...] - table[:, 1:2])
    for k, step in enumerate(STEPS):
        rows = g_ref[at_block((place_ref[2] + step) % NY, NEAR)]
        turned_ref[k * NEAR : (k + 1) * NEAR] = rows.astype(BF)


def own_terms_kernel(place_ref, g_ref, sw_ref, out_ref):
    for k, part in enumerate(terms(place_ref, g_ref[...], sw_ref)):
        out_ref[k] = part


def far_block_kernel(place_ref, own_ref, g_ref, sw_ref, a_ref, b_ref):
    halves = a_ref, b_ref

    @pl.when(place_ref[1] == 0)
    def _():
        weight = sw_ref[at_block((place_ref[0] + STEPS[3]) % NX, W)]
        total = (own_ref[3] + dot(g_ref[...], weight, ((1,), (1,)))).astype(BF)
        for k, ref in enumerate(halves):
            ref[...] = total[k * N // 2 : (k + 1) * N // 2]

    @pl.when(place_ref[1] == 1)
    def _():
        rows = slice(3 * NEAR, N)
        for k, part in enumerate(terms(place_ref, g_ref[rows], sw_ref)):
            total = (own_ref[k, rows] + part).astype(BF)
            halves[k // 2][k % 2 * NEAR : (k % 2 + 1) * NEAR] = total


def other_blocks_kernel(place_ref, own_ref, g_ref, sw_ref, *out_refs):
    @pl.when(place_ref[1] == 0)
    def _():
        for k in range(3):
            weight = sw_ref[at_block((place_ref[0] + STEPS[k]) % NX, W)]
            total = (own_ref[k] + dot(g_ref[...], weight, ((1,), (1,)))).astype(BF)
            for j in range(2):
                out_refs[2 * k + j][...] = total[j * N // 2 : (j + 1) * N // 2]

    @pl.when(place_ref[1] == 1)
    def _():
        rows = slice(0, 3 * NEAR)
        for k, part in enumerate(terms(place_ref, g_ref[rows], sw_ref)):
            total = (own_ref[k, rows] + part).astype(BF)
            for j in range(3):
                ref = out_refs[2 * j + k // 2]
                ref[k % 2 * NEAR : (k % 2 + 1) * NEAR] = total[j * NEAR : (j + 1) * NEAR]


def total_of(refs):
    total = refs[0][...].astype(F32)
    for ref in refs[1:]:
        total = total + ref[...].astype(F32)
    return total.astype(BF)


def pass_on_kernel(a_ref, b_ref, c_ref, d_ref, first_ref, second_ref):
    first_ref[...] = total_of((a_ref, b_ref))
    second_ref[...] = total_of((c_ref, d_ref))


def sum_first_kernel(*refs):
    for j in range(2):
        total = total_of(refs[3 * j : 3 * j + 3])
        for k in range(2):
            refs[6 + 2 * j + k][...] = total[k * NEAR : (k + 1) * NEAR]


def sum_second_kernel(*refs):
    refs[-1][...] = total_of(refs[:4])


def sum_kernel(in_ref, out_ref):
    out_ref[...] = jnp.sum(in_ref[...].astype(F32), axis=0).astype(BF)


def summed(x):
    return call(sum_kernel, [VM], [(x.shape[1:], BF)], x)[0]


def to_other_core(a):
    return lax.ppermute(a, "vocab", [(k, k ^ 1) for k in range(VOC)])


def along_rings(a, step, x_core):
    pairs = []
    for v in range(VOC):
        for t in range(TOK):
            if v % 2 == x_core:
                to = (v // 2 + step) % NX * 2 + v % 2, t
            else:
                to = v, (t // NZ + step) % NY * NZ + t % NZ
            pairs.append((v * TOK + t, to[0] * TOK + to[1]))
    return lax.ppermute(a, ("vocab", "tok"), pairs)


def along_first(a, step):
    return along_rings(a, step, 0)


def along_second(a, step):
    return along_rings(a, step, 1)


def ring(a, along):
    return along(a, 2), a, along(a, 1), along(a, -1)


def to_ring(blocks, along):
    own, left, right, far = blocks
    return along(far, 2), along(left, -1), along(right, 1), own


def per_device(student_hidden, teacher_hidden, student_weight, teacher_weight, source_rows):
    v = lax.axis_index("vocab").astype(jnp.int32)
    y = lax.axis_index("tok").astype(jnp.int32) // NZ
    place = jnp.stack([v // 2, v % 2, y])
    packed = call(
        pack_kernel,
        [SM, HBM, HBM],
        [((NZ, ROWS, 2 * W + 128), BF)],
        source_rows, in_hbm(student_hidden), in_hbm(teacher_hidden),
        scratch=[pltpu.VMEM((ROWS, W), BF)] * 2 + [pltpu.SemaphoreType.DMA((2,))],
    )[0]
    sw2, tw2 = to_other_core(student_weight), to_other_core(teacher_weight)
    near = exchange(packed, "tok", Z_GROUPS).reshape(NEAR, 2 * W + 128)
    near, sw2, tw2 = lax.optimization_barrier((near, sw2, tw2))
    half = ((N // 2, 2 * W), BF)
    mine_a, mine_b, digits = call(
        join_kernel,
        [SM] + [VM] * 4,
        [half, half, ((N, 128), BF)],
        place, *ring(near, along_second),
    )
    left_a, right_b = along_first(mine_a, 1), along_first(mine_b, -1)
    left_b, right_a = along_first(mine_b, 1), along_first(mine_a, -1)
    held = call(
        hold_kernel,
        [SM] + [HBM] * 4,
        [((HALF, C), BF)] * 4,
        place, *(in_hbm(x) for x in (student_weight, teacher_weight, sw2, tw2)),
        scratch=[pltpu.SemaphoreType.DMA((4, NX))],
    )
    left_a, right_b, held = lax.optimization_barrier((left_a, right_b, held))
    far = along_first(left_a, 1), along_first(right_b, -1)
    sw, tw, sw2, tw2 = held
    digits2 = to_other_core(digits)
    part = [((2, N, C), F32)]

    def near_part(numbers, held, *pieces):
        kernel = functools.partial(near_kernel, numbers)
        specs = [SM] + [VM] * (2 + len(pieces))
        flops = len(numbers) * N * HALF * C
        return call(kernel, specs, part, place, *held, *pieces, flops=flops)[0]

    weights_other, weights_own = (sw2, tw2), (sw, tw)
    for_other = near_part((0,), weights_other, mine_a, mine_b)
    own = near_part((0,), weights_own, mine_a, mine_b)
    left_b, right_a, for_other, own = lax.optimization_barrier((left_b, right_a, for_other, own))
    sides = left_a, left_b, right_a, right_b
    logits = [((N, C), F32)]

    def far_part(held, near):
        return call(far_kernel, [SM] + [VM] * 5, logits * 2, place, *held, *far, near)

    for_other = near_part((1, 2), weights_other, *sides, for_other)
    own = near_part((1, 2), weights_own, *sides, own)
    select = call(choose_kernel, [SM, VM, VM], [((N, N), BF)], place, digits, digits2)[0]
    far, for_other, own, select = lax.optimization_barrier((far, for_other, own, select))
    s_other, t_other = far_part(weights_other, for_other)
    t_other, s_other = to_other_core(t_other), to_other_core(s_other)
    s_own, t_own = far_part(weights_own, own)
    t_own, t_other = lax.optimization_barrier((t_own, t_other))
    t, table = call(
        teacher_logits_kernel,
        [VM] * 3,
        logits + [((N, 128), F32)],
        t_own, t_other, select,
    )
    s_other, t, table = lax.optimization_barrier((s_other, t, table))
    s, d, stats = call(
        student_logits_kernel,
        [VM] * 4,
        logits * 2 + [((VOC, 8, N // 2), F32)],
        s_own, s_other, t, table,
    )
    stats = exchange(stats, "vocab")
    stats = call(merge_kernel, [VM], [((TOK, 8, N // 2), F32)], stats)[0]
    stats = exchange(stats, "tok")
    g, loss = call(
        logit_grad_kernel,
        [SM] + [VM] * 3,
        [((N, C), BF), ((1, 1), F32)],
        place, stats, s, d,
        scratch=[pltpu.VMEM((N, C), F32)],
    )
    own = call(own_terms_kernel, [SM, VM, VM], [((NX, N, W), F32)], place, g, sw)[0]
    g_other, own = lax.optimization_barrier((to_other_core(g), own))
    half = ((N // 2, W), BF)
    far_a, far_b = call(
        far_block_kernel, [SM] + [VM] * 3, [half] * 2, place, own, g_other, sw2
    )
    far_a, far_b = along_first(far_a, 1), along_first(far_b, -1)
    own_a, own_b, left_a, left_b, right_a, right_b = call(
        other_blocks_kernel, [SM] + [VM] * 3, [half] * 6, place, own, g_other, sw2
    )
    left_a, right_b = along_first(left_a, -1), along_first(right_b, 1)
    right_a, left_b = call(pass_on_kernel, [VM] * 4, [half] * 2, right_a, far_a, left_b, far_b)
    right_a, left_b = along_first(right_a, 1), along_first(left_b, -1)
    blocks = call(
        sum_first_kernel,
        [VM] * 6,
        [((NEAR, W), BF)] * 4,
        *(own_a, left_a, right_a, own_b, left_b, right_b),
    )
    blocks = to_ring(blocks, along_second)
    partial = call(
        sum_second_kernel, [VM] * 4, [((NEAR, W), BF)], *blocks
    )[0]
    hidden_grad = summed(exchange(partial.reshape(NZ, ROWS, W), "tok", Z_GROUPS))
    return loss[0, 0], hidden_grad


def solution(mesh):
    in_specs = (
        P("tok", None),
        P("tok", None),
        P(None, ("vocab", "tok")),
        P(None, ("vocab", "tok")),
        P("tok"),
    )
    out_specs = (P(), P("tok", "vocab"))
    return jax.shard_map(
        per_device, mesh=mesh, in_specs=in_specs, out_specs=out_specs, check_vma=False
    )
```

```python
import functools

import jax
import jax.numpy as jnp
from jax import lax
from jax.experimental import pallas as pl
from jax.experimental.pallas import tpu as pltpu
from jax.sharding import PartitionSpec as P

BF = jnp.bfloat16
F32 = jnp.float32
TOK, VOC = 32, 8
NX, NY, NZ = 4, 4, 8
N = 512
D = 4096
C = 512
W = 512
ROWS = N // TOK
NEAR = N // NY
HALF = NX * W
MIB = 1 << 20
STEPS = (0, -1, 1, 2)
STAT = 16


def device(x, core, y, z):
    return (2 * x + core) * TOK + y * NZ + z


CORE_Z_GROUPS = [
    [device(x, core, y, z) for core in range(2) for z in range(NZ)]
    for x in range(NX)
    for y in range(NY)
]
X_Y_GROUPS = [
    [device(x, core, y, z) for x in range(NX) for y in range(NY)]
    for core in range(2)
    for z in range(NZ)
]
Z_GROUPS = [[y * NZ + z for z in range(NZ)] for y in range(NY)]


def dot(a, b, dims=((1,), (0,))):
    return lax.dot_general(a, b, (dims, ((), ())), preferred_element_type=F32)


PARAMS = pltpu.CompilerParams(vmem_limit_bytes=20 * MIB)
VM = pl.BlockSpec(memory_space=pltpu.VMEM)
SM = pl.BlockSpec(memory_space=pltpu.SMEM)
HBM = pl.BlockSpec(memory_space=pltpu.HBM)


def out(shape, dtype):
    return pltpu.VMEM(shape, dtype)


def in_hbm(x):
    return pltpu.with_memory_space_constraint(x, pltpu.HBM)


def cost(flops, mib=0):
    return pl.CostEstimate(flops=flops, bytes_accessed=mib * MIB, transcendentals=0)


def call(kernel, in_specs, outs, *args, scratch=(), flops=0):
    return pl.pallas_call(
        kernel,
        in_specs=in_specs,
        out_specs=[VM] * len(outs),
        out_shape=[out(*o) for o in outs],
        scratch_shapes=list(scratch),
        compiler_params=PARAMS,
        cost_estimate=cost(flops),
    )(*args)


def at_block(index, size):
    return pl.ds(pl.multiple_of(index * size, size), size)


def started(src, dst, sem):
    copy = pltpu.make_async_copy(src, dst, sem)
    copy.start()
    return copy


def pack_kernel(source_hbm, s_ref, t_ref, out_ref, s_buf, t_buf, source_ref, sem):
    v = lax.axis_index("vocab")
    columns = at_block(v, W)
    copies = [
        started(s_ref.at[:, columns], s_buf, sem.at[0]),
        started(t_ref.at[:, columns], t_buf, sem.at[1]),
    ]
    started(source_hbm, source_ref, sem.at[2]).wait()
    row = lax.broadcasted_iota(jnp.int32, (ROWS, 128), 0)
    lane = lax.broadcasted_iota(jnp.int32, (ROWS, 128), 1)
    digits = jnp.zeros((ROWS, 128), jnp.int32)
    for r in range(ROWS):
        source = source_ref[r]
        value = jnp.where(lane == 0, source >> 5, jnp.where(lane == 1, source & 31, 0))
        digits = jnp.where(row == r, value, digits)
    digits = digits.astype(F32).astype(BF)
    out_ref[:, :, 2 * W :] = jnp.broadcast_to(digits[None], (NZ, ROWS, 128))
    for k, (copy, buf) in enumerate(zip(copies, (s_buf, t_buf))):
        copy.wait()
        out_ref[:, :, k * W : (k + 1) * W] = jnp.broadcast_to(buf[...][None], (NZ, ROWS, W))


def join_kernel(place_ref, far_ref, own_ref, left_ref, right_ref, a_ref, b_ref, digits_ref):
    for k, (step, ref) in enumerate(zip(STEPS, (own_ref, left_ref, right_ref, far_ref))):
        (a_ref, b_ref)[k // 2][k % 2 * NEAR : (k % 2 + 1) * NEAR] = ref[:, : 2 * W]
        digits_ref[at_block((place_ref[2] + step) % NY, NEAR)] = ref[:, 2 * W :]


def hold_kernel(place_ref, *refs):
    sem = refs[-1]
    copies = []
    for n, (ref, out_ref) in enumerate(zip(refs[:4], refs[4:8])):
        for x in range(NX):
            rows = ref.at[at_block(2 * x + place_ref[1], W)]
            copies.append(started(rows, out_ref.at[x * W : (x + 1) * W], sem.at[n, x]))
    for copy in copies:
        copy.wait()


def weights(place_ref, refs, step):
    at = at_block((place_ref[0] + step) % NX, W)
    return [ref[at] for ref in refs]


def near_kernel(numbers, place_ref, sw_ref, tw_ref, *refs):
    pieces = [refs[2 * k : 2 * k + 2] for k in range(len(numbers))]
    steps = [STEPS[k] for k in numbers]
    before_refs, out_ref = refs[2 * len(numbers) : -1], refs[-1]
    y = place_ref[2]

    @pl.when(place_ref[1] == 0)
    def _():
        for n in range(2):
            columns = slice(n * W, (n + 1) * W)
            total = before_refs[0][n] if before_refs else None
            for step, halves in zip(steps, pieces):
                block = jnp.concatenate([ref[:, columns] for ref in halves], axis=0)
                part = dot(block, weights(place_ref, (sw_ref, tw_ref), step)[n])
                total = part if total is None else total + part
            out_ref[n] = total

    @pl.when(place_ref[1] == 1)
    def _():
        for n in range(2):
            columns = slice(n * W, (n + 1) * W)
            total = None
            for k, step in enumerate(STEPS):
                rows = slice(k % 2 * NEAR, (k % 2 + 1) * NEAR)
                block = jnp.concatenate([halves[k // 2][rows, columns] for halves in pieces], axis=0)
                part = dot(block, weights(place_ref, (sw_ref, tw_ref), step)[n])
                total = part if total is None else total + part
            for k, number in enumerate(numbers):
                out_ref[n, number * NEAR : (number + 1) * NEAR] = total[k * NEAR : (k + 1) * NEAR]
            for before_ref in before_refs:
                out_ref[n, :NEAR] = before_ref[n, :NEAR]


def far_kernel(place_ref, sw_ref, tw_ref, p3, p4, near_ref, *refs):
    y = place_ref[2]
    outs = refs[:2]

    @pl.when(place_ref[1] == 0)
    def _():
        for n, out_ref in enumerate(outs):
            columns = slice(n * W, (n + 1) * W)
            block = jnp.concatenate([p3[:, columns], p4[:, columns]], axis=0)
            part = dot(block, weights(place_ref, (sw_ref, tw_ref), STEPS[3])[n])
            for k, step in enumerate(STEPS):
                rows = at_block((y + step) % NY, NEAR)
                here = slice(k * NEAR, (k + 1) * NEAR)
                out_ref[rows] = near_ref[n, here] + part[here]

    @pl.when(place_ref[1] == 1)
    def _():
        for n, out_ref in enumerate(outs):
            columns = slice(n * W, (n + 1) * W)
            for k, step in enumerate(STEPS[:3]):
                here = slice(k * NEAR, (k + 1) * NEAR)
                out_ref[at_block((y + step) % NY, NEAR)] = near_ref[n, here]
            total = None
            for k, step in enumerate(STEPS):
                rows = slice(k % 2 * NEAR, (k % 2 + 1) * NEAR)
                block = (p3, p4)[k // 2][rows, columns]
                part = dot(block, weights(place_ref, (sw_ref, tw_ref), step)[n])
                total = part if total is None else total + part
            out_ref[at_block((y + STEPS[3]) % NY, NEAR)] = total


def choose_kernel(place_ref, own_ref, other_ref, out_ref):
    digits = jnp.where(
        place_ref[1] == 0, own_ref[...].astype(F32), other_ref[...].astype(F32)
    )
    index = (digits[:, 0:1] * 32.0 + digits[:, 1:2]).astype(jnp.int32)
    column = lax.broadcasted_iota(jnp.int32, (N, N), 1)
    out_ref[...] = (index == column).astype(F32).astype(BF)


def pack_stats(lse_s, mean, lse_t):
    half = N // 2
    row = lax.broadcasted_iota(jnp.int32, (8, half), 0)
    out = jnp.zeros((8, half), F32)
    for k, value in enumerate((lse_s, mean, lse_t)):
        out = jnp.where(row == k, value[:, :half], out)
        out = jnp.where(row == k + 4, value[:, half:], out)
    return out


def merge(stats):
    def rows(k):
        return jnp.concatenate([stats[:, k : k + 1], stats[:, k + 4 : k + 5]], axis=2)

    def lse(x):
        top = jnp.max(x, axis=0)
        return top + jnp.log(jnp.sum(jnp.exp(x - top[None]), axis=0))

    each_s, each_mean, each_t = rows(0), rows(1), rows(2)
    lse_s = lse(each_s)
    mean = jnp.sum(jnp.exp(each_s - lse_s[None]) * each_mean, axis=0)
    return lse_s, mean, lse(each_t)


def table_of(pairs, table):
    lane = lax.broadcasted_iota(jnp.int32, (N, 128), 1)
    for k, value in pairs:
        table = jnp.where(lane == k, value, table)
    return table


def teacher_logits_kernel(own_ref, other_ref, select_ref, t_ref, table_ref):
    t = own_ref[...] + other_ref[...]
    select = select_ref[...]
    high = t.astype(BF)
    rest = t - high.astype(F32)
    middle = rest.astype(BF)
    low = (rest - middle.astype(F32)).astype(BF)
    t = dot(select, high) + dot(select, middle) + dot(select, low)
    t_ref[...] = t
    top = jnp.max(t, axis=1, keepdims=True)
    total = jnp.sum(jnp.exp(t - top), axis=1, keepdims=True)
    table_ref[...] = table_of(((3, top), (4, total)), jnp.zeros((N, 128), F32))


def student_logits_kernel(own_ref, other_ref, t_ref, table_ref, s_ref, diff_ref, stat_ref):
    s = own_ref[...] + other_ref[...]
    s_ref[...] = s
    diff = s - t_ref[...]
    diff_ref[...] = diff
    top = jnp.max(s, axis=1, keepdims=True)
    e = jnp.exp(s - top)
    total = jnp.sum(e, axis=1, keepdims=True)
    mix = jnp.sum(e * diff, axis=1, keepdims=True)
    table = table_of(((0, top), (1, total), (2, mix)), table_ref[...])
    table = jnp.transpose(table)
    s_top, s_sum, mix, t_top, t_sum = (table[k : k + 1] for k in range(5))
    stat = pack_stats(s_top + jnp.log(s_sum), mix / s_sum, t_top + jnp.log(t_sum))
    stat_ref[...] = jnp.broadcast_to(stat[None], stat_ref.shape)


def merge_kernel(in_ref, out_ref):
    out_ref[...] = jnp.broadcast_to(pack_stats(*merge(in_ref[...]))[None], out_ref.shape)


def exchange(x, axis, groups=None):
    n = x.shape[0]
    flat = x.reshape((n * x.shape[1],) + x.shape[2:])
    out = lax.all_to_all(flat, axis, 0, 0, axis_index_groups=groups, tiled=True)
    return out.reshape(x.shape)


def terms(place_ref, g, sw_ref):
    for step in STEPS:
        yield dot(g, sw_ref[at_block((place_ref[0] + step) % NX, W)], ((1,), (1,)))


def logit_grad_kernel(place_ref, stat_ref, s_ref, d_ref, turned_ref, loss_ref, g_ref):
    lse_s, mean, lse_t = merge(stat_ref[...])
    loss_ref[...] = jnp.sum(mean - lse_s + lse_t, axis=1, keepdims=True) / N
    row = lax.broadcasted_iota(jnp.int32, (128, N), 0)
    table = jnp.where(row == 0, lse_s, jnp.where(row == 1, mean, 0.0))
    table = jnp.transpose(table)
    prob = jnp.exp(s_ref[...] - table[:, 0:1])
    g_ref[...] = prob * (d_ref[...] - table[:, 1:2])
    for k, step in enumerate(STEPS):
        rows = g_ref[at_block((place_ref[2] + step) % NY, NEAR)]
        turned_ref[k * NEAR : (k + 1) * NEAR] = rows.astype(BF)


def own_terms_kernel(place_ref, g_ref, sw_ref, out_ref):
    for k, part in enumerate(terms(place_ref, g_ref[...], sw_ref)):
        out_ref[k] = part


def to_hbm_kernel(in_ref, out_ref, sem):
    started(in_ref, out_ref, sem).wait()


def far_block_kernel(place_ref, own_ref, g_ref, sw_ref, a_ref, b_ref):
    halves = a_ref, b_ref

    @pl.when(place_ref[1] == 0)
    def _():
        weight = sw_ref[at_block((place_ref[0] + STEPS[3]) % NX, W)]
        total = (own_ref[3] + dot(g_ref[...], weight, ((1,), (1,)))).astype(BF)
        for k, ref in enumerate(halves):
            ref[...] = total[k * N // 2 : (k + 1) * N // 2]

    @pl.when(place_ref[1] == 1)
    def _():
        rows = slice(3 * NEAR, N)
        for k, part in enumerate(terms(place_ref, g_ref[rows], sw_ref)):
            total = (own_ref[k, rows] + part).astype(BF)
            halves[k // 2][k % 2 * NEAR : (k % 2 + 1) * NEAR] = total


def other_blocks_kernel(place_ref, own_ref, g_ref, sw_ref, *out_refs):
    @pl.when(place_ref[1] == 0)
    def _():
        for k in range(3):
            weight = sw_ref[at_block((place_ref[0] + STEPS[k]) % NX, W)]
            total = (own_ref[k] + dot(g_ref[...], weight, ((1,), (1,)))).astype(BF)
            for j in range(2):
                out_refs[2 * k + j][...] = total[j * N // 2 : (j + 1) * N // 2]

    @pl.when(place_ref[1] == 1)
    def _():
        rows = slice(0, 3 * NEAR)
        for k, part in enumerate(terms(place_ref, g_ref[rows], sw_ref)):
            total = (own_ref[k, rows] + part).astype(BF)
            for j in range(3):
                ref = out_refs[2 * j + k // 2]
                ref[k % 2 * NEAR : (k % 2 + 1) * NEAR] = total[j * NEAR : (j + 1) * NEAR]


def total_of(refs):
    total = refs[0][...].astype(F32)
    for ref in refs[1:]:
        total = total + ref[...].astype(F32)
    return total.astype(BF)


def pass_on_kernel(a_ref, b_ref, c_ref, d_ref, first_ref, second_ref):
    first_ref[...] = total_of((a_ref, b_ref))
    second_ref[...] = total_of((c_ref, d_ref))


def sum_first_kernel(*refs):
    for j in range(2):
        total = total_of(refs[3 * j : 3 * j + 3])
        for k in range(2):
            refs[6 + 2 * j + k][...] = total[k * NEAR : (k + 1) * NEAR]


def sum_second_kernel(*refs):
    refs[-1][...] = total_of(refs[:4])


def sum_kernel(in_ref, out_ref):
    out_ref[...] = jnp.sum(in_ref[...].astype(F32), axis=0).astype(BF)


def summed(x):
    return call(sum_kernel, [VM], [(x.shape[1:], BF)], x)[0]


def to_other_core(a):
    return lax.ppermute(a, "vocab", [(k, k ^ 1) for k in range(VOC)])


def along_rings(a, step, x_core):
    pairs = []
    for v in range(VOC):
        for t in range(TOK):
            if v % 2 == x_core:
                to = (v // 2 + step) % NX * 2 + v % 2, t
            else:
                to = v, (t // NZ + step) % NY * NZ + t % NZ
            pairs.append((v * TOK + t, to[0] * TOK + to[1]))
    return lax.ppermute(a, ("vocab", "tok"), pairs)


def along_first(a, step):
    return along_rings(a, step, 0)


def along_second(a, step):
    return along_rings(a, step, 1)


def ring(a, along):
    return along(a, 2), a, along(a, 1), along(a, -1)


def to_ring(blocks, along):
    own, left, right, far = blocks
    return along(far, 2), along(left, -1), along(right, 1), own


def per_device(student_hidden, teacher_hidden, student_weight, teacher_weight, source_rows):
    v = lax.axis_index("vocab").astype(jnp.int32)
    y = lax.axis_index("tok").astype(jnp.int32) // NZ
    place = jnp.stack([v // 2, v % 2, y])
    packed = call(
        pack_kernel,
        [HBM, HBM, HBM],
        [((NZ, ROWS, 2 * W + 128), BF)],
        in_hbm(source_rows), in_hbm(student_hidden), in_hbm(teacher_hidden),
        scratch=[pltpu.VMEM((ROWS, W), BF)] * 2
        + [pltpu.SMEM((ROWS,), jnp.int32), pltpu.SemaphoreType.DMA((3,))],
    )[0]
    sw2, tw2 = to_other_core(student_weight), to_other_core(teacher_weight)
    near = exchange(packed, "tok", Z_GROUPS).reshape(NEAR, 2 * W + 128)
    near, sw2, tw2 = lax.optimization_barrier((near, sw2, tw2))
    half = ((N // 2, 2 * W), BF)
    mine_a, mine_b, digits = call(
        join_kernel,
        [SM] + [VM] * 4,
        [half, half, ((N, 128), BF)],
        place, *ring(near, along_second),
    )
    left_a, right_b = along_first(mine_a, 1), along_first(mine_b, -1)
    left_b, right_a = along_first(mine_b, 1), along_first(mine_a, -1)
    held = call(
        hold_kernel,
        [SM] + [HBM] * 4,
        [((HALF, C), BF)] * 4,
        place, *(in_hbm(x) for x in (student_weight, teacher_weight, sw2, tw2)),
        scratch=[pltpu.SemaphoreType.DMA((4, NX))],
    )
    left_a, right_b, held = lax.optimization_barrier((left_a, right_b, held))
    far = along_first(left_a, 1), along_first(right_b, -1)
    sw, tw, sw2, tw2 = held
    digits2 = to_other_core(digits)
    part = [((2, N, C), F32)]

    def near_part(numbers, held, *pieces):
        kernel = functools.partial(near_kernel, numbers)
        specs = [SM] + [VM] * (2 + len(pieces))
        flops = len(numbers) * N * HALF * C
        return call(kernel, specs, part, place, *held, *pieces, flops=flops)[0]

    weights_other, weights_own = (sw2, tw2), (sw, tw)
    for_other = near_part((0,), weights_other, mine_a, mine_b)
    own = near_part((0,), weights_own, mine_a, mine_b)
    left_b, right_a, for_other, own = lax.optimization_barrier((left_b, right_a, for_other, own))
    sides = left_a, left_b, right_a, right_b
    logits = [((N, C), F32)]

    def far_part(held, near):
        return call(far_kernel, [SM] + [VM] * 5, logits * 2, place, *held, *far, near)

    for_other = near_part((1, 2), weights_other, *sides, for_other)
    own = near_part((1, 2), weights_own, *sides, own)
    select = call(choose_kernel, [SM, VM, VM], [((N, N), BF)], place, digits, digits2)[0]
    far, for_other, own, select = lax.optimization_barrier((far, for_other, own, select))
    s_other, t_other = far_part(weights_other, for_other)
    t_other, s_other = to_other_core(t_other), to_other_core(s_other)
    s_own, t_own = far_part(weights_own, own)
    t_own, t_other = lax.optimization_barrier((t_own, t_other))
    t, table = call(
        teacher_logits_kernel,
        [VM] * 3,
        logits + [((N, 128), F32)],
        t_own, t_other, select,
    )
    s_other, t, table = lax.optimization_barrier((s_other, t, table))
    s, d, stats = call(
        student_logits_kernel,
        [VM] * 4,
        logits * 2 + [((STAT, 8, N // 2), F32)],
        s_own, s_other, t, table,
    )
    stats = exchange(stats, ("vocab", "tok"), X_Y_GROUPS)
    stats = call(merge_kernel, [VM], [((STAT, 8, N // 2), F32)], stats)[0]
    stats = exchange(stats, ("vocab", "tok"), CORE_Z_GROUPS)
    g, loss = call(
        logit_grad_kernel,
        [SM] + [VM] * 3,
        [((N, C), BF), ((1, 1), F32)],
        place, stats, s, d,
        scratch=[pltpu.VMEM((N, C), F32)],
    )
    own = call(own_terms_kernel, [SM, VM, VM], [((NX, N, W), F32)], place, g, sw)[0]
    g_other, own = lax.optimization_barrier((to_other_core(g), own))
    half = ((N // 2, W), BF)
    far_a, far_b = call(
        far_block_kernel, [SM] + [VM] * 3, [half] * 2, place, own, g_other, sw2
    )
    far_a, far_b = along_first(far_a, 1), along_first(far_b, -1)
    own_a, own_b, left_a, left_b, right_a, right_b = call(
        other_blocks_kernel, [SM] + [VM] * 3, [half] * 6, place, own, g_other, sw2
    )
    left_a, right_b = along_first(left_a, -1), along_first(right_b, 1)
    right_a, left_b = call(pass_on_kernel, [VM] * 4, [half] * 2, right_a, far_a, left_b, far_b)
    right_a, left_b = along_first(right_a, 1), along_first(left_b, -1)
    blocks = call(
        sum_first_kernel,
        [VM] * 6,
        [((NEAR, W), BF)] * 4,
        *(own_a, left_a, right_a, own_b, left_b, right_b),
    )
    blocks = to_ring(blocks, along_second)
    loss = pl.pallas_call(
        to_hbm_kernel,
        in_specs=[VM],
        out_specs=HBM,
        out_shape=pltpu.HBM((1, 1), F32),
        scratch_shapes=[pltpu.SemaphoreType.DMA(())],
        compiler_params=PARAMS,
        cost_estimate=cost(0),
    )(loss)
    blocks, loss = lax.optimization_barrier((blocks, loss))
    partial = call(
        sum_second_kernel, [VM] * 4, [((NEAR, W), BF)], *blocks
    )[0]
    hidden_grad = summed(exchange(partial.reshape(NZ, ROWS, W), "tok", Z_GROUPS))
    return loss[0, 0], hidden_grad


def solution(mesh):
    in_specs = (
        P("tok", None),
        P("tok", None),
        P(None, ("vocab", "tok")),
        P(None, ("vocab", "tok")),
        P("tok"),
    )
    out_specs = (P(), P("tok", "vocab"))
    return jax.shard_map(
        per_device, mesh=mesh, in_specs=in_specs, out_specs=out_specs, check_vma=False
    )
```

```python
import functools

import jax
import jax.numpy as jnp
from jax import lax
from jax.experimental import pallas as pl
from jax.experimental.pallas import tpu as pltpu
from jax.sharding import PartitionSpec as P

BF = jnp.bfloat16
F32 = jnp.float32
TOK, VOC = 32, 8
NX, NY, NZ = 4, 4, 8
N = 512
D = 4096
C = 512
W = 512
ROWS = N // TOK
NEAR = N // NY
HALF = NX * W
MIB = 1 << 20
STEPS = (0, -1, 1, 2)
STAT = 16


def device(x, core, y, z):
    return (2 * x + core) * TOK + y * NZ + z


CORE_Z_GROUPS = [
    [device(x, core, y, z) for core in range(2) for z in range(NZ)]
    for x in range(NX)
    for y in range(NY)
]
X_Y_GROUPS = [
    [device(x, core, y, z) for x in range(NX) for y in range(NY)]
    for core in range(2)
    for z in range(NZ)
]
Z_GROUPS = [[y * NZ + z for z in range(NZ)] for y in range(NY)]


def dot(a, b, dims=((1,), (0,))):
    return lax.dot_general(a, b, (dims, ((), ())), preferred_element_type=F32)


PARAMS = pltpu.CompilerParams(vmem_limit_bytes=20 * MIB)
VM = pl.BlockSpec(memory_space=pltpu.VMEM)
SM = pl.BlockSpec(memory_space=pltpu.SMEM)
HBM = pl.BlockSpec(memory_space=pltpu.HBM)


def out(shape, dtype):
    return pltpu.VMEM(shape, dtype)


def in_hbm(x):
    return pltpu.with_memory_space_constraint(x, pltpu.HBM)


def cost(flops, mib=0):
    return pl.CostEstimate(flops=flops, bytes_accessed=mib * MIB, transcendentals=0)


def call(kernel, in_specs, outs, *args, scratch=(), flops=0):
    return pl.pallas_call(
        kernel,
        in_specs=in_specs,
        out_specs=[VM] * len(outs),
        out_shape=[out(*o) for o in outs],
        scratch_shapes=list(scratch),
        compiler_params=PARAMS,
        cost_estimate=cost(flops),
    )(*args)


def at_block(index, size):
    return pl.ds(pl.multiple_of(index * size, size), size)


def started(src, dst, sem):
    copy = pltpu.make_async_copy(src, dst, sem)
    copy.start()
    return copy


def pack_kernel(source_hbm, s_ref, t_ref, out_ref, s_buf, t_buf, source_ref, sem):
    v = lax.axis_index("vocab")
    columns = at_block(v, W)
    copies = [
        started(s_ref.at[:, columns], s_buf, sem.at[0]),
        started(t_ref.at[:, columns], t_buf, sem.at[1]),
    ]
    started(source_hbm, source_ref, sem.at[2]).wait()
    row = lax.broadcasted_iota(jnp.int32, (ROWS, 128), 0)
    lane = lax.broadcasted_iota(jnp.int32, (ROWS, 128), 1)
    digits = jnp.zeros((ROWS, 128), jnp.int32)
    for r in range(ROWS):
        source = source_ref[r]
        value = jnp.where(lane == 0, source >> 5, jnp.where(lane == 1, source & 31, 0))
        digits = jnp.where(row == r, value, digits)
    digits = digits.astype(F32).astype(BF)
    out_ref[:, :, 2 * W :] = jnp.broadcast_to(digits[None], (NZ, ROWS, 128))
    for k, (copy, buf) in enumerate(zip(copies, (s_buf, t_buf))):
        copy.wait()
        out_ref[:, :, k * W : (k + 1) * W] = jnp.broadcast_to(buf[...][None], (NZ, ROWS, W))


def join_kernel(place_ref, far_ref, own_ref, left_ref, right_ref, a_ref, b_ref, digits_ref):
    for k, (step, ref) in enumerate(zip(STEPS, (own_ref, left_ref, right_ref, far_ref))):
        (a_ref, b_ref)[k // 2][k % 2 * NEAR : (k % 2 + 1) * NEAR] = ref[:, : 2 * W]
        digits_ref[at_block((place_ref[2] + step) % NY, NEAR)] = ref[:, 2 * W :]


def hold_kernel(place_ref, *refs):
    sem = refs[-1]
    copies = []
    for n, (ref, out_ref) in enumerate(zip(refs[:4], refs[4:8])):
        for x in range(NX):
            rows = ref.at[at_block(2 * x + place_ref[1], W)]
            copies.append(started(rows, out_ref.at[x * W : (x + 1) * W], sem.at[n, x]))
    for copy in copies:
        copy.wait()


def weights(place_ref, refs, step):
    at = at_block((place_ref[0] + step) % NX, W)
    return [ref[at] for ref in refs]


def near_kernel(numbers, place_ref, sw_ref, tw_ref, *refs):
    pieces = [refs[2 * k : 2 * k + 2] for k in range(len(numbers))]
    steps = [STEPS[k] for k in numbers]
    before_refs, out_ref = refs[2 * len(numbers) : -1], refs[-1]
    y = place_ref[2]

    @pl.when(place_ref[1] == 0)
    def _():
        for n in range(2):
            columns = slice(n * W, (n + 1) * W)
            total = before_refs[0][n] if before_refs else None
            for step, halves in zip(steps, pieces):
                block = jnp.concatenate([ref[:, columns] for ref in halves], axis=0)
                part = dot(block, weights(place_ref, (sw_ref, tw_ref), step)[n])
                total = part if total is None else total + part
            out_ref[n] = total

    @pl.when(place_ref[1] == 1)
    def _():
        for n in range(2):
            columns = slice(n * W, (n + 1) * W)
            total = None
            for k, step in enumerate(STEPS):
                rows = slice(k % 2 * NEAR, (k % 2 + 1) * NEAR)
                block = jnp.concatenate([halves[k // 2][rows, columns] for halves in pieces], axis=0)
                part = dot(block, weights(place_ref, (sw_ref, tw_ref), step)[n])
                total = part if total is None else total + part
            for k, number in enumerate(numbers):
                out_ref[n, number * NEAR : (number + 1) * NEAR] = total[k * NEAR : (k + 1) * NEAR]
            for before_ref in before_refs:
                out_ref[n, :NEAR] = before_ref[n, :NEAR]


def far_kernel(numbers, place_ref, sw_ref, tw_ref, p3, p4, near_ref, *outs):
    y = place_ref[2]

    @pl.when(place_ref[1] == 0)
    def _():
        for n, out_ref in zip(numbers, outs):
            columns = slice(n * W, (n + 1) * W)
            block = jnp.concatenate([p3[:, columns], p4[:, columns]], axis=0)
            part = dot(block, weights(place_ref, (sw_ref, tw_ref), STEPS[3])[n])
            for k, step in enumerate(STEPS):
                rows = at_block((y + step) % NY, NEAR)
                here = slice(k * NEAR, (k + 1) * NEAR)
                out_ref[rows] = near_ref[n, here] + part[here]

    @pl.when(place_ref[1] == 1)
    def _():
        for n, out_ref in zip(numbers, outs):
            columns = slice(n * W, (n + 1) * W)
            for k, step in enumerate(STEPS[:3]):
                here = slice(k * NEAR, (k + 1) * NEAR)
                out_ref[at_block((y + step) % NY, NEAR)] = near_ref[n, here]
            total = None
            for k, step in enumerate(STEPS):
                rows = slice(k % 2 * NEAR, (k % 2 + 1) * NEAR)
                block = (p3, p4)[k // 2][rows, columns]
                part = dot(block, weights(place_ref, (sw_ref, tw_ref), step)[n])
                total = part if total is None else total + part
            out_ref[at_block((y + STEPS[3]) % NY, NEAR)] = total


def choose_kernel(place_ref, own_ref, other_ref, out_ref):
    digits = jnp.where(
        place_ref[1] == 0, own_ref[...].astype(F32), other_ref[...].astype(F32)
    )
    index = (digits[:, 0:1] * 32.0 + digits[:, 1:2]).astype(jnp.int32)
    column = lax.broadcasted_iota(jnp.int32, (N, N), 1)
    out_ref[...] = (index == column).astype(F32).astype(BF)


def pack_stats(lse_s, mean, lse_t):
    half = N // 2
    row = lax.broadcasted_iota(jnp.int32, (8, half), 0)
    out = jnp.zeros((8, half), F32)
    for k, value in enumerate((lse_s, mean, lse_t)):
        out = jnp.where(row == k, value[:, :half], out)
        out = jnp.where(row == k + 4, value[:, half:], out)
    return out


def merge(stats):
    def rows(k):
        return jnp.concatenate([stats[:, k : k + 1], stats[:, k + 4 : k + 5]], axis=2)

    def lse(x):
        top = jnp.max(x, axis=0)
        return top + jnp.log(jnp.sum(jnp.exp(x - top[None]), axis=0))

    each_s, each_mean, each_t = rows(0), rows(1), rows(2)
    lse_s = lse(each_s)
    mean = jnp.sum(jnp.exp(each_s - lse_s[None]) * each_mean, axis=0)
    return lse_s, mean, lse(each_t)


def table_of(pairs, table):
    lane = lax.broadcasted_iota(jnp.int32, (N, 128), 1)
    for k, value in pairs:
        table = jnp.where(lane == k, value, table)
    return table


def teacher_logits_kernel(own_ref, other_ref, select_ref, t_ref, table_ref):
    t = own_ref[...] + other_ref[...]
    select = select_ref[...]
    high = t.astype(BF)
    rest = t - high.astype(F32)
    middle = rest.astype(BF)
    low = (rest - middle.astype(F32)).astype(BF)
    t = dot(select, high) + dot(select, middle) + dot(select, low)
    t_ref[...] = t
    top = jnp.max(t, axis=1, keepdims=True)
    total = jnp.sum(jnp.exp(t - top), axis=1, keepdims=True)
    table_ref[...] = table_of(((3, top), (4, total)), jnp.zeros((N, 128), F32))


def student_logits_kernel(own_ref, other_ref, t_ref, table_ref, s_ref, diff_ref, stat_ref):
    s = own_ref[...] + other_ref[...]
    s_ref[...] = s
    diff = s - t_ref[...]
    diff_ref[...] = diff
    top = jnp.max(s, axis=1, keepdims=True)
    e = jnp.exp(s - top)
    total = jnp.sum(e, axis=1, keepdims=True)
    mix = jnp.sum(e * diff, axis=1, keepdims=True)
    table = table_of(((0, top), (1, total), (2, mix)), table_ref[...])
    table = jnp.transpose(table)
    s_top, s_sum, mix, t_top, t_sum = (table[k : k + 1] for k in range(5))
    stat = pack_stats(s_top + jnp.log(s_sum), mix / s_sum, t_top + jnp.log(t_sum))
    stat_ref[...] = jnp.broadcast_to(stat[None], stat_ref.shape)


def merge_kernel(in_ref, out_ref):
    out_ref[...] = jnp.broadcast_to(pack_stats(*merge(in_ref[...]))[None], out_ref.shape)


def exchange(x, axis, groups=None):
    n = x.shape[0]
    flat = x.reshape((n * x.shape[1],) + x.shape[2:])
    out = lax.all_to_all(flat, axis, 0, 0, axis_index_groups=groups, tiled=True)
    return out.reshape(x.shape)


def terms(place_ref, g, sw_ref):
    for step in STEPS:
        yield dot(g, sw_ref[at_block((place_ref[0] + step) % NX, W)], ((1,), (1,)))


def logit_grad_kernel(place_ref, stat_ref, s_ref, d_ref, turned_ref, g_ref):
    lse_s, mean, _ = merge(stat_ref[...])
    row = lax.broadcasted_iota(jnp.int32, (128, N), 0)
    table = jnp.where(row == 0, lse_s, jnp.where(row == 1, mean, 0.0))
    table = jnp.transpose(table)
    prob = jnp.exp(s_ref[...] - table[:, 0:1])
    g_ref[...] = prob * (d_ref[...] - table[:, 1:2])
    for k, step in enumerate(STEPS):
        rows = g_ref[at_block((place_ref[2] + step) % NY, NEAR)]
        turned_ref[k * NEAR : (k + 1) * NEAR] = rows.astype(BF)


def own_terms_kernel(place_ref, g_ref, sw_ref, out_ref):
    for k, part in enumerate(terms(place_ref, g_ref[...], sw_ref)):
        out_ref[k] = part


def loss_kernel(stat_ref, out_ref, loss_ref, sem):
    lse_s, mean, lse_t = merge(stat_ref[...])
    loss_ref[...] = jnp.sum(mean - lse_s + lse_t, axis=1, keepdims=True) / N
    started(loss_ref, out_ref, sem).wait()


def far_block_kernel(place_ref, own_ref, g_ref, sw_ref, a_ref, b_ref):
    halves = a_ref, b_ref

    @pl.when(place_ref[1] == 0)
    def _():
        weight = sw_ref[at_block((place_ref[0] + STEPS[3]) % NX, W)]
        total = (own_ref[3] + dot(g_ref[...], weight, ((1,), (1,)))).astype(BF)
        for k, ref in enumerate(halves):
            ref[...] = total[k * N // 2 : (k + 1) * N // 2]

    @pl.when(place_ref[1] == 1)
    def _():
        rows = slice(3 * NEAR, N)
        for k, part in enumerate(terms(place_ref, g_ref[rows], sw_ref)):
            total = (own_ref[k, rows] + part).astype(BF)
            halves[k // 2][k % 2 * NEAR : (k % 2 + 1) * NEAR] = total


def other_blocks_kernel(place_ref, own_ref, g_ref, sw_ref, *out_refs):
    @pl.when(place_ref[1] == 0)
    def _():
        for k in range(3):
            weight = sw_ref[at_block((place_ref[0] + STEPS[k]) % NX, W)]
            total = (own_ref[k] + dot(g_ref[...], weight, ((1,), (1,)))).astype(BF)
            for j in range(2):
                out_refs[2 * k + j][...] = total[j * N // 2 : (j + 1) * N // 2]

    @pl.when(place_ref[1] == 1)
    def _():
        rows = slice(0, 3 * NEAR)
        for k, part in enumerate(terms(place_ref, g_ref[rows], sw_ref)):
            total = (own_ref[k, rows] + part).astype(BF)
            for j in range(3):
                ref = out_refs[2 * j + k // 2]
                ref[k % 2 * NEAR : (k % 2 + 1) * NEAR] = total[j * NEAR : (j + 1) * NEAR]


def total_of(refs):
    total = refs[0][...].astype(F32)
    for ref in refs[1:]:
        total = total + ref[...].astype(F32)
    return total.astype(BF)


def pass_on_kernel(a_ref, b_ref, c_ref, d_ref, first_ref, second_ref):
    first_ref[...] = total_of((a_ref, b_ref))
    second_ref[...] = total_of((c_ref, d_ref))


def sum_first_kernel(*refs):
    for j in range(2):
        total = total_of(refs[3 * j : 3 * j + 3])
        for k in range(2):
            refs[6 + 2 * j + k][...] = total[k * NEAR : (k + 1) * NEAR]


def sum_second_kernel(*refs):
    refs[-1][...] = total_of(refs[:4])


def sum_kernel(in_ref, out_ref):
    out_ref[...] = jnp.sum(in_ref[...].astype(F32), axis=0).astype(BF)


def summed(x):
    return call(sum_kernel, [VM], [(x.shape[1:], BF)], x)[0]


def to_other_core(a):
    return lax.ppermute(a, "vocab", [(k, k ^ 1) for k in range(VOC)])


def along_rings(a, step, x_core):
    pairs = []
    for v in range(VOC):
        for t in range(TOK):
            if v % 2 == x_core:
                to = (v // 2 + step) % NX * 2 + v % 2, t
            else:
                to = v, (t // NZ + step) % NY * NZ + t % NZ
            pairs.append((v * TOK + t, to[0] * TOK + to[1]))
    return lax.ppermute(a, ("vocab", "tok"), pairs)


def along_first(a, step):
    return along_rings(a, step, 0)


def along_second(a, step):
    return along_rings(a, step, 1)


def ring(a, along):
    return along(a, 2), a, along(a, 1), along(a, -1)


def to_ring(blocks, along):
    own, left, right, far = blocks
    return along(far, 2), along(left, -1), along(right, 1), own


def per_device(student_hidden, teacher_hidden, student_weight, teacher_weight, source_rows):
    v = lax.axis_index("vocab").astype(jnp.int32)
    y = lax.axis_index("tok").astype(jnp.int32) // NZ
    place = jnp.stack([v // 2, v % 2, y])
    packed = call(
        pack_kernel,
        [HBM, HBM, HBM],
        [((NZ, ROWS, 2 * W + 128), BF)],
        in_hbm(source_rows), in_hbm(student_hidden), in_hbm(teacher_hidden),
        scratch=[pltpu.VMEM((ROWS, W), BF)] * 2
        + [pltpu.SMEM((ROWS,), jnp.int32), pltpu.SemaphoreType.DMA((3,))],
    )[0]
    sw2, tw2 = to_other_core(student_weight), to_other_core(teacher_weight)
    near = exchange(packed, "tok", Z_GROUPS).reshape(NEAR, 2 * W + 128)
    near, sw2, tw2 = lax.optimization_barrier((near, sw2, tw2))
    half = ((N // 2, 2 * W), BF)
    mine_a, mine_b, digits = call(
        join_kernel,
        [SM] + [VM] * 4,
        [half, half, ((N, 128), BF)],
        place, *ring(near, along_second),
    )
    left_a, right_b = along_first(mine_a, 1), along_first(mine_b, -1)
    left_b, right_a = along_first(mine_b, 1), along_first(mine_a, -1)
    held = call(
        hold_kernel,
        [SM] + [HBM] * 4,
        [((HALF, C), BF)] * 4,
        place, *(in_hbm(x) for x in (student_weight, teacher_weight, sw2, tw2)),
        scratch=[pltpu.SemaphoreType.DMA((4, NX))],
    )
    left_a, right_b, held = lax.optimization_barrier((left_a, right_b, held))
    far = along_first(left_a, 1), along_first(right_b, -1)
    sw, tw, sw2, tw2 = held
    digits2 = to_other_core(digits)
    part = [((2, N, C), F32)]

    def near_part(numbers, held, *pieces):
        kernel = functools.partial(near_kernel, numbers)
        specs = [SM] + [VM] * (2 + len(pieces))
        flops = len(numbers) * N * HALF * C
        return call(kernel, specs, part, place, *held, *pieces, flops=flops)[0]

    weights_other, weights_own = (sw2, tw2), (sw, tw)
    for_other = near_part((0,), weights_other, mine_a, mine_b)
    own = near_part((0,), weights_own, mine_a, mine_b)
    left_b, right_a, for_other, own = lax.optimization_barrier((left_b, right_a, for_other, own))
    sides = left_a, left_b, right_a, right_b
    logits = [((N, C), F32)]

    def far_part(numbers, held, near):
        kernel = functools.partial(far_kernel, numbers)
        outs = logits * len(numbers)
        return call(kernel, [SM] + [VM] * 5, outs, place, *held, *far, near)

    for_other = near_part((1, 2), weights_other, *sides, for_other)
    own = near_part((1, 2), weights_own, *sides, own)
    select = call(choose_kernel, [SM, VM, VM], [((N, N), BF)], place, digits, digits2)[0]
    far, for_other, own, select = lax.optimization_barrier((far, for_other, own, select))
    t_other = to_other_core(far_part((1,), weights_other, for_other)[0])
    s_other = to_other_core(far_part((0,), weights_other, for_other)[0])
    s_own, t_own = far_part((0, 1), weights_own, own)
    t_own, t_other = lax.optimization_barrier((t_own, t_other))
    t, table = call(
        teacher_logits_kernel,
        [VM] * 3,
        logits + [((N, 128), F32)],
        t_own, t_other, select,
    )
    s_other, t, table = lax.optimization_barrier((s_other, t, table))
    s, d, stats = call(
        student_logits_kernel,
        [VM] * 4,
        logits * 2 + [((STAT, 8, N // 2), F32)],
        s_own, s_other, t, table,
    )
    stats = exchange(stats, ("vocab", "tok"), X_Y_GROUPS)
    stats = call(merge_kernel, [VM], [((STAT, 8, N // 2), F32)], stats)[0]
    stats = exchange(stats, ("vocab", "tok"), CORE_Z_GROUPS)
    g = call(
        logit_grad_kernel,
        [SM] + [VM] * 3,
        [((N, C), BF)],
        place, stats, s, d,
        scratch=[pltpu.VMEM((N, C), F32)],
    )[0]
    own = call(own_terms_kernel, [SM, VM, VM], [((NX, N, W), F32)], place, g, sw)[0]
    g_other, own = lax.optimization_barrier((to_other_core(g), own))
    half = ((N // 2, W), BF)
    far_a, far_b = call(
        far_block_kernel, [SM] + [VM] * 3, [half] * 2, place, own, g_other, sw2
    )
    far_a, far_b = along_first(far_a, 1), along_first(far_b, -1)
    own_a, own_b, left_a, left_b, right_a, right_b = call(
        other_blocks_kernel, [SM] + [VM] * 3, [half] * 6, place, own, g_other, sw2
    )
    left_a, right_b = along_first(left_a, -1), along_first(right_b, 1)
    right_a, left_b = call(pass_on_kernel, [VM] * 4, [half] * 2, right_a, far_a, left_b, far_b)
    right_a, left_b = along_first(right_a, 1), along_first(left_b, -1)
    blocks = call(
        sum_first_kernel,
        [VM] * 6,
        [((NEAR, W), BF)] * 4,
        *(own_a, left_a, right_a, own_b, left_b, right_b),
    )
    blocks = to_ring(blocks, along_second)
    loss = pl.pallas_call(
        loss_kernel,
        in_specs=[VM],
        out_specs=HBM,
        out_shape=pltpu.HBM((1, 1), F32),
        scratch_shapes=[pltpu.VMEM((1, 1), F32), pltpu.SemaphoreType.DMA(())],
        compiler_params=PARAMS,
        cost_estimate=cost(0),
    )(stats)
    blocks, loss = lax.optimization_barrier((blocks, loss))
    partial = call(
        sum_second_kernel, [VM] * 4, [((NEAR, W), BF)], *blocks
    )[0]
    hidden_grad = summed(exchange(partial.reshape(NZ, ROWS, W), "tok", Z_GROUPS))
    return loss[0, 0], hidden_grad


def solution(mesh):
    in_specs = (
        P("tok", None),
        P("tok", None),
        P(None, ("vocab", "tok")),
        P(None, ("vocab", "tok")),
        P("tok"),
    )
    out_specs = (P(), P("tok", "vocab"))
    return jax.shard_map(
        per_device, mesh=mesh, in_specs=in_specs, out_specs=out_specs, check_vma=False
    )
```

```python
import functools

import jax
import jax.numpy as jnp
from jax import lax
from jax.experimental import pallas as pl
from jax.experimental.pallas import tpu as pltpu
from jax.sharding import PartitionSpec as P

BF = jnp.bfloat16
F32 = jnp.float32
TOK, VOC = 32, 8
NX, NY, NZ = 4, 4, 8
N = 512
D = 4096
C = 512
W = 512
ROWS = N // TOK
NEAR = N // NY
HALF = NX * W
MIB = 1 << 20
STEPS = (0, -1, 1, 2)
STAT = 16


def device(x, core, y, z):
    return (2 * x + core) * TOK + y * NZ + z


CORE_Z_GROUPS = [
    [device(x, core, y, z) for core in range(2) for z in range(NZ)]
    for x in range(NX)
    for y in range(NY)
]
X_Y_GROUPS = [
    [device(x, core, y, z) for x in range(NX) for y in range(NY)]
    for core in range(2)
    for z in range(NZ)
]
Z_GROUPS = [[y * NZ + z for z in range(NZ)] for y in range(NY)]


def dot(a, b, dims=((1,), (0,))):
    return lax.dot_general(a, b, (dims, ((), ())), preferred_element_type=F32)


PARAMS = pltpu.CompilerParams(vmem_limit_bytes=20 * MIB)
VM = pl.BlockSpec(memory_space=pltpu.VMEM)
SM = pl.BlockSpec(memory_space=pltpu.SMEM)
HBM = pl.BlockSpec(memory_space=pltpu.HBM)


def out(shape, dtype):
    return pltpu.VMEM(shape, dtype)


def in_hbm(x):
    return pltpu.with_memory_space_constraint(x, pltpu.HBM)


def cost(flops, mib=0):
    return pl.CostEstimate(flops=flops, bytes_accessed=mib * MIB, transcendentals=0)


def call(kernel, in_specs, outs, *args, scratch=(), flops=0):
    return pl.pallas_call(
        kernel,
        in_specs=in_specs,
        out_specs=[VM] * len(outs),
        out_shape=[out(*o) for o in outs],
        scratch_shapes=list(scratch),
        compiler_params=PARAMS,
        cost_estimate=cost(flops),
    )(*args)


def at_block(index, size):
    return pl.ds(pl.multiple_of(index * size, size), size)


def started(src, dst, sem):
    copy = pltpu.make_async_copy(src, dst, sem)
    copy.start()
    return copy


def pack_kernel(source_hbm, s_ref, t_ref, out_ref, s_buf, t_buf, source_ref, sem):
    v = lax.axis_index("vocab")
    columns = at_block(v, W)
    copies = [
        started(s_ref.at[:, columns], s_buf, sem.at[0]),
        started(t_ref.at[:, columns], t_buf, sem.at[1]),
    ]
    started(source_hbm, source_ref, sem.at[2]).wait()
    row = lax.broadcasted_iota(jnp.int32, (ROWS, 128), 0)
    lane = lax.broadcasted_iota(jnp.int32, (ROWS, 128), 1)
    digits = jnp.zeros((ROWS, 128), jnp.int32)
    for r in range(ROWS):
        source = source_ref[r]
        value = jnp.where(lane == 0, source >> 5, jnp.where(lane == 1, source & 31, 0))
        digits = jnp.where(row == r, value, digits)
    digits = digits.astype(F32).astype(BF)
    out_ref[:, :, 2 * W :] = jnp.broadcast_to(digits[None], (NZ, ROWS, 128))
    for k, (copy, buf) in enumerate(zip(copies, (s_buf, t_buf))):
        copy.wait()
        out_ref[:, :, k * W : (k + 1) * W] = jnp.broadcast_to(buf[...][None], (NZ, ROWS, W))


def join_kernel(place_ref, far_ref, own_ref, left_ref, right_ref, a_ref, b_ref, digits_ref):
    for k, (step, ref) in enumerate(zip(STEPS, (own_ref, left_ref, right_ref, far_ref))):
        (a_ref, b_ref)[k // 2][k % 2 * NEAR : (k % 2 + 1) * NEAR] = ref[:, : 2 * W]
        digits_ref[at_block((place_ref[2] + step) % NY, NEAR)] = ref[:, 2 * W :]


def hold_kernel(place_ref, *refs):
    sem = refs[-1]
    copies = []
    for n, (ref, out_ref) in enumerate(zip(refs[:4], refs[4:8])):
        for x in range(NX):
            rows = ref.at[at_block(2 * x + place_ref[1], W)]
            copies.append(started(rows, out_ref.at[x * W : (x + 1) * W], sem.at[n, x]))
    for copy in copies:
        copy.wait()


def weights(place_ref, refs, step):
    at = at_block((place_ref[0] + step) % NX, W)
    return [ref[at] for ref in refs]


def near_kernel(numbers, place_ref, sw_ref, tw_ref, *refs):
    pieces = [refs[2 * k : 2 * k + 2] for k in range(len(numbers))]
    steps = [STEPS[k] for k in numbers]
    before_refs, out_ref = refs[2 * len(numbers) : -1], refs[-1]
    y = place_ref[2]

    @pl.when(place_ref[1] == 0)
    def _():
        for n in range(2):
            columns = slice(n * W, (n + 1) * W)
            total = before_refs[0][n] if before_refs else None
            for step, halves in zip(steps, pieces):
                block = jnp.concatenate([ref[:, columns] for ref in halves], axis=0)
                part = dot(block, weights(place_ref, (sw_ref, tw_ref), step)[n])
                total = part if total is None else total + part
            out_ref[n] = total

    @pl.when(place_ref[1] == 1)
    def _():
        for n in range(2):
            columns = slice(n * W, (n + 1) * W)
            total = None
            for k, step in enumerate(STEPS):
                rows = slice(k % 2 * NEAR, (k % 2 + 1) * NEAR)
                block = jnp.concatenate([halves[k // 2][rows, columns] for halves in pieces], axis=0)
                part = dot(block, weights(place_ref, (sw_ref, tw_ref), step)[n])
                total = part if total is None else total + part
            for k, number in enumerate(numbers):
                out_ref[n, number * NEAR : (number + 1) * NEAR] = total[k * NEAR : (k + 1) * NEAR]
            for before_ref in before_refs:
                out_ref[n, :NEAR] = before_ref[n, :NEAR]


def far_kernel(numbers, place_ref, sw_ref, tw_ref, p3, p4, near_ref, *outs):
    y = place_ref[2]

    @pl.when(place_ref[1] == 0)
    def _():
        for n, out_ref in zip(numbers, outs):
            columns = slice(n * W, (n + 1) * W)
            block = jnp.concatenate([p3[:, columns], p4[:, columns]], axis=0)
            part = dot(block, weights(place_ref, (sw_ref, tw_ref), STEPS[3])[n])
            for k, step in enumerate(STEPS):
                rows = at_block((y + step) % NY, NEAR)
                here = slice(k * NEAR, (k + 1) * NEAR)
                out_ref[rows] = near_ref[n, here] + part[here]

    @pl.when(place_ref[1] == 1)
    def _():
        for n, out_ref in zip(numbers, outs):
            columns = slice(n * W, (n + 1) * W)
            for k, step in enumerate(STEPS[:3]):
                here = slice(k * NEAR, (k + 1) * NEAR)
                out_ref[at_block((y + step) % NY, NEAR)] = near_ref[n, here]
            total = None
            for k, step in enumerate(STEPS):
                rows = slice(k % 2 * NEAR, (k % 2 + 1) * NEAR)
                block = (p3, p4)[k // 2][rows, columns]
                part = dot(block, weights(place_ref, (sw_ref, tw_ref), step)[n])
                total = part if total is None else total + part
            out_ref[at_block((y + STEPS[3]) % NY, NEAR)] = total


def choose_kernel(place_ref, own_ref, other_ref, out_ref):
    digits = jnp.where(
        place_ref[1] == 0, own_ref[...].astype(F32), other_ref[...].astype(F32)
    )
    index = (digits[:, 0:1] * 32.0 + digits[:, 1:2]).astype(jnp.int32)
    column = lax.broadcasted_iota(jnp.int32, (N, N), 1)
    out_ref[...] = (index == column).astype(F32).astype(BF)


def pack_stats(lse_s, mean, lse_t):
    half = N // 2
    row = lax.broadcasted_iota(jnp.int32, (8, half), 0)
    out = jnp.zeros((8, half), F32)
    for k, value in enumerate((lse_s, mean, lse_t)):
        out = jnp.where(row == k, value[:, :half], out)
        out = jnp.where(row == k + 4, value[:, half:], out)
    return out


def merge(stats):
    def rows(k):
        return jnp.concatenate([stats[:, k : k + 1], stats[:, k + 4 : k + 5]], axis=2)

    def lse(x):
        top = jnp.max(x, axis=0)
        return top + jnp.log(jnp.sum(jnp.exp(x - top[None]), axis=0))

    each_s, each_mean, each_t = rows(0), rows(1), rows(2)
    lse_s = lse(each_s)
    mean = jnp.sum(jnp.exp(each_s - lse_s[None]) * each_mean, axis=0)
    return lse_s, mean, lse(each_t)


def table_of(pairs, table):
    lane = lax.broadcasted_iota(jnp.int32, (N, 128), 1)
    for k, value in pairs:
        table = jnp.where(lane == k, value, table)
    return table


def teacher_logits_kernel(own_ref, other_ref, select_ref, t_ref, table_ref):
    t = own_ref[...] + other_ref[...]
    select = select_ref[...]
    high = t.astype(BF)
    rest = t - high.astype(F32)
    middle = rest.astype(BF)
    low = (rest - middle.astype(F32)).astype(BF)
    t = dot(select, high) + dot(select, middle) + dot(select, low)
    t_ref[...] = t
    top = jnp.max(t, axis=1, keepdims=True)
    total = jnp.sum(jnp.exp(t - top), axis=1, keepdims=True)
    table_ref[...] = table_of(((3, top), (4, total)), jnp.zeros((N, 128), F32))


def student_logits_kernel(own_ref, other_ref, t_ref, table_ref, s_ref, diff_ref, stat_ref):
    s = own_ref[...] + other_ref[...]
    s_ref[...] = s
    diff = s - t_ref[...]
    diff_ref[...] = diff
    top = jnp.max(s, axis=1, keepdims=True)
    e = jnp.exp(s - top)
    total = jnp.sum(e, axis=1, keepdims=True)
    mix = jnp.sum(e * diff, axis=1, keepdims=True)
    table = table_of(((0, top), (1, total), (2, mix)), table_ref[...])
    table = jnp.transpose(table)
    s_top, s_sum, mix, t_top, t_sum = (table[k : k + 1] for k in range(5))
    stat = pack_stats(s_top + jnp.log(s_sum), mix / s_sum, t_top + jnp.log(t_sum))
    stat_ref[...] = jnp.broadcast_to(stat[None], stat_ref.shape)


def merge_kernel(in_ref, out_ref):
    out_ref[...] = jnp.broadcast_to(pack_stats(*merge(in_ref[...]))[None], out_ref.shape)


def exchange(x, axis, groups=None):
    n = x.shape[0]
    flat = x.reshape((n * x.shape[1],) + x.shape[2:])
    out = lax.all_to_all(flat, axis, 0, 0, axis_index_groups=groups, tiled=True)
    return out.reshape(x.shape)


def terms(place_ref, g, sw_ref):
    for step in STEPS:
        yield dot(g, sw_ref[at_block((place_ref[0] + step) % NX, W)], ((1,), (1,)))


def logit_grad_kernel(place_ref, stat_ref, s_ref, d_ref, turned_ref, g_ref):
    lse_s, mean, _ = merge(stat_ref[...])
    row = lax.broadcasted_iota(jnp.int32, (128, N), 0)
    table = jnp.where(row == 0, lse_s, jnp.where(row == 1, mean, 0.0))
    table = jnp.transpose(table)
    prob = jnp.exp(s_ref[...] - table[:, 0:1])
    g_ref[...] = prob * (d_ref[...] - table[:, 1:2])
    for k, step in enumerate(STEPS):
        rows = g_ref[at_block((place_ref[2] + step) % NY, NEAR)]
        turned_ref[k * NEAR : (k + 1) * NEAR] = rows.astype(BF)


def own_terms_kernel(place_ref, g_ref, sw_ref, out_ref):
    for k, part in enumerate(terms(place_ref, g_ref[...], sw_ref)):
        out_ref[k] = part


def loss_kernel(stat_ref, out_ref, loss_ref, sem):
    lse_s, mean, lse_t = merge(stat_ref[...])
    loss_ref[...] = jnp.sum(mean - lse_s + lse_t, axis=1, keepdims=True) / N
    started(loss_ref, out_ref, sem).wait()


def far_block_kernel(place_ref, own_ref, g_ref, sw_ref, a_ref, b_ref):
    halves = a_ref, b_ref

    @pl.when(place_ref[1] == 0)
    def _():
        weight = sw_ref[at_block((place_ref[0] + STEPS[3]) % NX, W)]
        total = (own_ref[3] + dot(g_ref[...], weight, ((1,), (1,)))).astype(BF)
        for k, ref in enumerate(halves):
            ref[...] = total[k * N // 2 : (k + 1) * N // 2]

    @pl.when(place_ref[1] == 1)
    def _():
        rows = slice(3 * NEAR, N)
        for k, part in enumerate(terms(place_ref, g_ref[rows], sw_ref)):
            total = (own_ref[k, rows] + part).astype(BF)
            halves[k // 2][k % 2 * NEAR : (k % 2 + 1) * NEAR] = total


def other_blocks_kernel(place_ref, own_ref, g_ref, sw_ref, *out_refs):
    @pl.when(place_ref[1] == 0)
    def _():
        for k in range(3):
            weight = sw_ref[at_block((place_ref[0] + STEPS[k]) % NX, W)]
            total = (own_ref[k] + dot(g_ref[...], weight, ((1,), (1,)))).astype(BF)
            for j in range(2):
                out_refs[2 * k + j][...] = total[j * N // 2 : (j + 1) * N // 2]

    @pl.when(place_ref[1] == 1)
    def _():
        rows = slice(0, 3 * NEAR)
        for k, part in enumerate(terms(place_ref, g_ref[rows], sw_ref)):
            total = (own_ref[k, rows] + part).astype(BF)
            for j in range(3):
                ref = out_refs[2 * j + k // 2]
                ref[k % 2 * NEAR : (k % 2 + 1) * NEAR] = total[j * NEAR : (j + 1) * NEAR]


def total_of(refs):
    total = refs[0][...].astype(F32)
    for ref in refs[1:]:
        total = total + ref[...].astype(F32)
    return total.astype(BF)


def pass_on_kernel(a_ref, b_ref, c_ref, d_ref, first_ref, second_ref):
    first_ref[...] = total_of((a_ref, b_ref))
    second_ref[...] = total_of((c_ref, d_ref))


def sum_first_kernel(*refs):
    for j in range(2):
        total = total_of(refs[3 * j : 3 * j + 3])
        for k in range(2):
            refs[6 + 2 * j + k][...] = total[k * NEAR : (k + 1) * NEAR]


def sum_second_kernel(*refs):
    refs[-1][...] = total_of(refs[:4])


def sum_kernel(in_ref, out_ref):
    out_ref[...] = jnp.sum(in_ref[...].astype(F32), axis=0).astype(BF)


def summed(x):
    return call(sum_kernel, [VM], [(x.shape[1:], BF)], x)[0]


def to_other_core(a):
    return lax.ppermute(a, "vocab", [(k, k ^ 1) for k in range(VOC)])


def along_rings(a, step, x_core):
    pairs = []
    for v in range(VOC):
        for t in range(TOK):
            if v % 2 == x_core:
                to = (v // 2 + step) % NX * 2 + v % 2, t
            else:
                to = v, (t // NZ + step) % NY * NZ + t % NZ
            pairs.append((v * TOK + t, to[0] * TOK + to[1]))
    return lax.ppermute(a, ("vocab", "tok"), pairs)


def along_first(a, step):
    return along_rings(a, step, 0)


def along_second(a, step):
    return along_rings(a, step, 1)


def ring(a, along):
    return along(a, 2), a, along(a, 1), along(a, -1)


def to_ring(blocks, along):
    own, left, right, far = blocks
    return along(far, 2), along(left, -1), along(right, 1), own


def per_device(student_hidden, teacher_hidden, student_weight, teacher_weight, source_rows):
    v = lax.axis_index("vocab").astype(jnp.int32)
    y = lax.axis_index("tok").astype(jnp.int32) // NZ
    place = jnp.stack([v // 2, v % 2, y])
    packed = call(
        pack_kernel,
        [HBM, HBM, HBM],
        [((NZ, ROWS, 2 * W + 128), BF)],
        in_hbm(source_rows), in_hbm(student_hidden), in_hbm(teacher_hidden),
        scratch=[pltpu.VMEM((ROWS, W), BF)] * 2
        + [pltpu.SMEM((ROWS,), jnp.int32), pltpu.SemaphoreType.DMA((3,))],
    )[0]
    sw2, tw2 = to_other_core(student_weight), to_other_core(teacher_weight)
    near = exchange(packed, "tok", Z_GROUPS).reshape(NEAR, 2 * W + 128)
    near, sw2, tw2 = lax.optimization_barrier((near, sw2, tw2))
    half = ((N // 2, 2 * W), BF)
    mine_a, mine_b, digits = call(
        join_kernel,
        [SM] + [VM] * 4,
        [half, half, ((N, 128), BF)],
        place, *ring(near, along_second),
    )
    left_a, right_b = along_first(mine_a, 1), along_first(mine_b, -1)
    left_b, right_a = along_first(mine_b, 1), along_first(mine_a, -1)
    held = call(
        hold_kernel,
        [SM] + [HBM] * 4,
        [((HALF, C), BF)] * 4,
        place, *(in_hbm(x) for x in (student_weight, teacher_weight, sw2, tw2)),
        scratch=[pltpu.SemaphoreType.DMA((4, NX))],
    )
    left_a, right_b, held = lax.optimization_barrier((left_a, right_b, held))
    far = along_first(left_a, 1), along_first(right_b, -1)
    sw, tw, sw2, tw2 = held
    digits2 = to_other_core(digits)
    part = [((2, N, C), F32)]

    def near_part(numbers, held, *pieces):
        kernel = functools.partial(near_kernel, numbers)
        specs = [SM] + [VM] * (2 + len(pieces))
        flops = len(numbers) * N * HALF * C
        return call(kernel, specs, part, place, *held, *pieces, flops=flops)[0]

    weights_other, weights_own = (sw2, tw2), (sw, tw)
    for_other = near_part((0,), weights_other, mine_a, mine_b)
    own = near_part((0,), weights_own, mine_a, mine_b)
    left_b, right_a, for_other, own = lax.optimization_barrier((left_b, right_a, for_other, own))
    sides = left_a, left_b, right_a, right_b
    logits = [((N, C), F32)]

    def far_part(numbers, held, near):
        kernel = functools.partial(far_kernel, numbers)
        outs = logits * len(numbers)
        return call(kernel, [SM] + [VM] * 5, outs, place, *held, *far, near)

    for_other = near_part((1, 2), weights_other, *sides, for_other)
    own = near_part((1, 2), weights_own, *sides, own)
    select = call(choose_kernel, [SM, VM, VM], [((N, N), BF)], place, digits, digits2)[0]
    far, for_other, own, select = lax.optimization_barrier((far, for_other, own, select))
    t_other = to_other_core(far_part((1,), weights_other, for_other)[0])
    s_other = to_other_core(far_part((0,), weights_other, for_other)[0])
    s_own, t_own = far_part((0, 1), weights_own, own)
    t_own, t_other = lax.optimization_barrier((t_own, t_other))
    t, table = call(
        teacher_logits_kernel,
        [VM] * 3,
        logits + [((N, 128), F32)],
        t_own, t_other, select,
    )
    s_other, t, table = lax.optimization_barrier((s_other, t, table))
    s, d, stats = call(
        student_logits_kernel,
        [VM] * 4,
        logits * 2 + [((STAT, 8, N // 2), F32)],
        s_own, s_other, t, table,
    )
    stats = exchange(stats, ("vocab", "tok"), CORE_Z_GROUPS)
    stats = call(merge_kernel, [VM], [((STAT, 8, N // 2), F32)], stats)[0]
    stats = exchange(stats, ("vocab", "tok"), X_Y_GROUPS)
    g = call(
        logit_grad_kernel,
        [SM] + [VM] * 3,
        [((N, C), BF)],
        place, stats, s, d,
        scratch=[pltpu.VMEM((N, C), F32)],
    )[0]
    own = call(own_terms_kernel, [SM, VM, VM], [((NX, N, W), F32)], place, g, sw)[0]
    g_other, own = lax.optimization_barrier((to_other_core(g), own))
    half = ((N // 2, W), BF)
    far_a, far_b = call(
        far_block_kernel, [SM] + [VM] * 3, [half] * 2, place, own, g_other, sw2
    )
    far_a, far_b = along_first(far_a, 1), along_first(far_b, -1)
    own_a, own_b, left_a, left_b, right_a, right_b = call(
        other_blocks_kernel, [SM] + [VM] * 3, [half] * 6, place, own, g_other, sw2
    )
    left_a, right_b = along_first(left_a, -1), along_first(right_b, 1)
    right_a, left_b = call(pass_on_kernel, [VM] * 4, [half] * 2, right_a, far_a, left_b, far_b)
    right_a, left_b = along_first(right_a, 1), along_first(left_b, -1)
    blocks = call(
        sum_first_kernel,
        [VM] * 6,
        [((NEAR, W), BF)] * 4,
        *(own_a, left_a, right_a, own_b, left_b, right_b),
    )
    blocks = to_ring(blocks, along_second)
    loss = pl.pallas_call(
        loss_kernel,
        in_specs=[VM],
        out_specs=HBM,
        out_shape=pltpu.HBM((1, 1), F32),
        scratch_shapes=[pltpu.VMEM((1, 1), F32), pltpu.SemaphoreType.DMA(())],
        compiler_params=PARAMS,
        cost_estimate=cost(0),
    )(stats)
    blocks, loss = lax.optimization_barrier((blocks, loss))
    partial = call(
        sum_second_kernel, [VM] * 4, [((NEAR, W), BF)], *blocks
    )[0]
    hidden_grad = summed(exchange(partial.reshape(NZ, ROWS, W), "tok", Z_GROUPS))
    return loss[0, 0], hidden_grad


def solution(mesh):
    in_specs = (
        P("tok", None),
        P("tok", None),
        P(None, ("vocab", "tok")),
        P(None, ("vocab", "tok")),
        P("tok"),
    )
    out_specs = (P(), P("tok", "vocab"))
    return jax.shard_map(
        per_device, mesh=mesh, in_specs=in_specs, out_specs=out_specs, check_vma=False
    )
```
